32 devices in a mesh: dp: 16 (over z, x, core), side: 2 (over y).
Axes of the slice: x: 2, y: 2, z: 4, core: 2. Of those that a mesh axis runs over, the one named last changes fastest.
Arguments:
- backbone_in: bfloat16 [65536, 768], P(('dp', 'side')), may hold values from -6 to 6
- segment_ids: int32 [65536], P('dp'), may hold values from 0 to 511, never falling along the last dimension, each value on 1 to 1024 neighbouring positions
- gate_index: int32 [1], replicated, may hold values from 0 to 11
- norm_before: float32 [768], replicated, may hold values from 0.5 to 1.5
- norm_middle: float32 [768], replicated, may hold values from 0.5 to 1.5
- frozen_query: bfloat16 [768, 768], replicated, may hold values from -0.21875 to 0.21875
- frozen_key: bfloat16 [768, 768], replicated, may hold values from -0.21875 to 0.21875
- frozen_value: bfloat16 [768, 768], replicated, may hold values from -0.21875 to 0.21875
- frozen_output: bfloat16 [768, 768], replicated, may hold values from -0.875 to 0.875
- frozen_expand: bfloat16 [768, 3072], replicated, may hold values from -0.21875 to 0.21875
- frozen_reduce: bfloat16 [3072, 768], replicated, may hold values from -0.109375 to 0.109375
- tap_weight: bfloat16 [768, 96], replicated, may hold values from -0.21875 to 0.21875
- gate_table: float32 [12, 96], replicated, may hold values from -6 to 6
- side_stream: bfloat16 [65536, 96], P(('dp', 'side')), may hold values from -6 to 6
- ladder_before: float32 [96], replicated, may hold values from 0.5 to 1.5
- ladder_middle: float32 [96], replicated, may hold values from 0.5 to 1.5
- ladder_query: bfloat16 [96, 96], P(None, 'side'), may hold values from -0.625 to 0.625
- ladder_key: bfloat16 [96, 96], P(None, 'side'), may hold values from -0.625 to 0.625
- ladder_value: bfloat16 [96, 96], P(None, 'side'), may hold values from -0.625 to 0.625
- ladder_output: bfloat16 [96, 96], P('side'), may hold values from -2.5 to 2.5
- ladder_expand: bfloat16 [96, 384], P(None, 'side'), may hold values from -0.625 to 0.625
- ladder_reduce: bfloat16 [384, 96], P('side'), may hold values from -0.4375 to 0.4375
- cotangent: bfloat16 [65536, 96], P(('dp', 'side')), may hold values from -6 to 6
Outputs:
- ladder_out: bfloat16 [65536, 96], P(('dp', 'side'))
- stream_grad: bfloat16 [65536, 96], P(('dp', 'side'))
- tap_grad: float32 [768, 96], replicated
- gate_grad: float32 [12, 96], replicated
- before_grad: float32 [96], replicated
- middle_grad: float32 [96], replicated
- query_grad: float32 [96, 96], P(None, 'side')
- key_grad: float32 [96, 96], P(None, 'side')
- value_grad: float32 [96, 96], P(None, 'side')
- output_grad: float32 [96, 96], P('side')
- expand_grad: float32 [96, 384], P(None, 'side')
- reduce_grad: float32 [384, 96], P('side')
The draws below stay inside these ranges and needn't reach their ends.
Inputs may be any that keep to these rules, and one draw needn't show every extreme that they name: `segment_ids`: segment numbers never fall along the tokens; attention stays within one segment and one block of 1024 tokens.
All inputs are finite; a program needn't handle non-finite values.
Results may differ from the reference program's by a relative error of at most 0.033.
Values may be sent and summed in bfloat16 or wider, within the bound.
No kernel may reach another device: no remote copies, remote signals or barrier semaphores. Data moves between devices by JAX's collectives and lax.ppermute only.
A program may use at most 192 MiB of HBM per device.

```python
import math
import jax
import jax.numpy as jnp
import numpy as np
from jax import lax

D_MODEL = 768
HEAD = 64
FF = 3072
LAYERS = 12
D_SIDE = 96
SIDE_HEAD = 8
SIDE_FF = 384
SEQ = 1024
TOKENS = 65536


def shard_levels(key, shape, cuts, low, high):
    level = 1.0
    for position, shards_of in cuts:
        heights = jax.random.uniform(jax.random.fold_in(jax.random.fold_in(key, 6), position), (shards_of,), jnp.float32, low / len(cuts), high / len(cuts))
        level = level * jnp.repeat(jnp.exp(heights), shape[position] // shards_of).reshape((-1,) + (1,) * (len(shape) - 1 - position))
    return level


def profile(count, total, reach, skew):
    portions = [(1 << 20) // math.isqrt(rank ** skew) + 1 for rank in range(2, count + 1)]
    rest, counts = total - reach - (count - 1), [1] * (count - 1)
    while rest > 0:
        free = [i for i in range(count - 1) if counts[i] < reach]
        whole, budget = sum([portions[i] for i in free]), rest
        for i in free:
            more = min(reach - counts[i], max(1, budget * portions[i] // whole), rest)
            counts[i] = counts[i] + more
            rest = rest - more
    return np.array([reach] + counts)


def ragged_sizes(stream_key, amount, total, bound, skew):
    if amount == 2:
        one = jax.random.randint(stream_key, (), max(1, total - bound), min(bound, total - 1) + 1)
        return jnp.stack([one, total - one])
    lengths = jnp.asarray(profile(amount, total, bound, skew), jnp.int32)
    twos = (amount - 1) // 2
    giver, sink = lengths[1:1 + 2 * twos:2], lengths[2:2 + 2 * twos:2]
    margin = jnp.minimum(giver - 1, bound - sink)
    moved = jax.random.randint(jax.random.fold_in(stream_key, 1), (twos,), 0, 1 << 20) % (margin + 1)
    lengths = lengths.at[1:1 + 2 * twos:2].set(giver - moved).at[2:2 + 2 * twos:2].set(sink + moved)
    return lengths[jax.random.permutation(jax.random.fold_in(stream_key, 2), amount)]


def gaussian(rng, dims, deviation, reach, cuts=(), held_as=jnp.bfloat16):
    loudness = shard_levels(rng, dims, cuts, -0.22, 0.18) if cuts else 1.0
    values = jax.random.normal(rng, dims, jnp.float32) * deviation * loudness
    return jnp.minimum(jnp.maximum(values, -reach), reach).astype(held_as)


def setup_inputs(seed: int = 0) -> dict:
    key_of = jax.random.split(jax.random.key(seed), 24)
    backbone_in = gaussian(key_of[0], (TOKENS, D_MODEL), 1.0, 6.0, ((0, 32),))
    segment_ids = jnp.searchsorted(jnp.cumsum(ragged_sizes(key_of[1], TOKENS // min(128, SEQ // 2), TOKENS, SEQ, 2)), jnp.arange(TOKENS), side="right").astype(jnp.int32)
    gate_index = jax.random.randint(key_of[2], (1,), 0, LAYERS).astype(jnp.int32)
    norm_before = jnp.clip(jax.random.uniform(key_of[3], (D_MODEL,), jnp.float32, 0.5, 1.5), 0.5, 1.5)
    norm_middle = jnp.clip(jax.random.uniform(key_of[4], (D_MODEL,), jnp.float32, 0.5, 1.5), 0.5, 1.5)
    frozen_query = gaussian(key_of[5], (D_MODEL, D_MODEL), D_MODEL ** -0.5, 0.21875)
    frozen_key = gaussian(key_of[6], (D_MODEL, D_MODEL), D_MODEL ** -0.5, 0.21875)
    frozen_value = gaussian(key_of[7], (D_MODEL, D_MODEL), D_MODEL ** -0.5, 0.21875)
    frozen_output = gaussian(key_of[8], (D_MODEL, D_MODEL), (D_MODEL // 16) ** -0.5, 0.875)
    frozen_expand = gaussian(key_of[9], (D_MODEL, FF), D_MODEL ** -0.5, 0.21875)
    frozen_reduce = gaussian(key_of[10], (FF, D_MODEL), FF ** -0.5, 0.109375)
    tap_weight = gaussian(key_of[11], (D_MODEL, D_SIDE), D_MODEL ** -0.5, 0.21875)
    gate_table = gaussian(key_of[12], (LAYERS, D_SIDE), 1.5, 6.0, (), jnp.float32)
    side_stream = gaussian(key_of[13], (TOKENS, D_SIDE), 1.0, 6.0, ((0, 32),))
    ladder_before = jnp.clip(jax.random.uniform(key_of[14], (D_SIDE,), jnp.float32, 0.5, 1.5), 0.5, 1.5)
    ladder_middle = jnp.clip(jax.random.uniform(key_of[15], (D_SIDE,), jnp.float32, 0.5, 1.5), 0.5, 1.5)
    ladder_query = gaussian(key_of[16], (D_SIDE, D_SIDE), D_SIDE ** -0.5, 0.625, ((1, 2),))
    ladder_key = gaussian(key_of[17], (D_SIDE, D_SIDE), D_SIDE ** -0.5, 0.625, ((1, 2),))
    ladder_value = gaussian(key_of[18], (D_SIDE, D_SIDE), D_SIDE ** -0.5, 0.625, ((1, 2),))
    ladder_output = gaussian(key_of[19], (D_SIDE, D_SIDE), (D_SIDE // 16) ** -0.5, 2.5, ((0, 2),))
    ladder_expand = gaussian(key_of[20], (D_SIDE, SIDE_FF), D_SIDE ** -0.5, 0.625, ((1, 2),))
    ladder_reduce = gaussian(key_of[21], (SIDE_FF, D_SIDE), (SIDE_FF // 2) ** -0.5, 0.4375, ((0, 2),))
    cotangent = gaussian(key_of[22], (TOKENS, D_SIDE), 1.0, 6.0, ((0, 32),))
    return {"backbone_in": backbone_in, "segment_ids": segment_ids, "gate_index": gate_index, "norm_before": norm_before, "norm_middle": norm_middle, "frozen_query": frozen_query, "frozen_key": frozen_key, "frozen_value": frozen_value, "frozen_output": frozen_output, "frozen_expand": frozen_expand, "frozen_reduce": frozen_reduce, "tap_weight": tap_weight, "gate_table": gate_table, "side_stream": side_stream, "ladder_before": ladder_before, "ladder_middle": ladder_middle, "ladder_query": ladder_query, "ladder_key": ladder_key, "ladder_value": ladder_value, "ladder_output": ladder_output, "ladder_expand": ladder_expand, "ladder_reduce": ladder_reduce, "cotangent": cotangent}


EPS = 1e-06
HIGH = lax.Precision.HIGHEST

@jax.custom_vjp
def low(v):
    return lax.optimization_barrier(v.astype(jnp.bfloat16)).astype(jnp.float32)

@jax.custom_vjp
def low_back(v):
    return v

def low_keep(v):
    return (low(v), None)

def low_pass(kept, grad):
    return (grad,)

def back_keep(v):
    return (v, None)

def back_low(kept, grad):
    return (low(grad),)
low.defvjp(low_keep, low_pass)
low_back.defvjp(back_keep, back_low)

def matmul(left, right):
    return jnp.dot(left, right, precision=HIGH)

def rms(values, gain):
    return values * lax.rsqrt(lax.optimization_barrier(jnp.mean(values * values, axis=-1, keepdims=True)) + EPS) * gain

def attend(query, key, value, segment, width):

    def block(inputs):
        block_query, block_key, block_value, block_segment = inputs
        heads = block_query.shape[1] // width
        shaped_query = block_query.reshape(SEQ, heads, width)
        shaped_key = block_key.reshape(SEQ, heads, width)
        shaped_value = block_value.reshape(SEQ, heads, width)
        raw = low_back(jnp.einsum('qhe,khe->hqk', shaped_query, shaped_key, precision=HIGH) * width ** (-0.5))
        same = block_segment[:, None] == block_segment[None, :]
        probs = low(jax.nn.softmax(jnp.where(same[None], raw, -1e+30), axis=-1))
        context = jnp.einsum('hqk,khe->qhe', probs, shaped_value, precision=HIGH)
        return context.reshape(SEQ, heads * width)
    pieces = lax.map(jax.checkpoint(block), (query.reshape(-1, SEQ, query.shape[1]), key.reshape(-1, SEQ, key.shape[1]), value.reshape(-1, SEQ, value.shape[1]), segment.reshape(-1, SEQ)))
    return pieces.reshape(query.shape)

def backbone(rows, segment, frozen):
    before, middle_gain, w_query, w_key, w_value, w_output, w_expand, w_reduce = frozen
    normed = low(rms(rows, before))
    query = low(matmul(normed, w_query))
    key = low(matmul(normed, w_key))
    value = low(matmul(normed, w_value))
    context = low(attend(query, key, value, segment, HEAD))
    middle = rows + matmul(context, w_output)
    expanded = low(jax.nn.gelu(matmul(low(rms(middle, middle_gain)), w_expand)))
    return low(middle + matmul(expanded, w_reduce))

def side_forward(top, segment, gate_index, params, stream):
    down, table, before, middle_gain, w_query, w_key, w_value, w_output, w_expand, w_reduce = params
    tap = low(low_back(matmul(top, down)))
    gate = jax.nn.sigmoid(lax.dynamic_index_in_dim(table, gate_index[0], 0, keepdims=False))
    mixed = gate * tap + (1.0 - gate) * stream
    first = low(rms(mixed, before))
    query = low(low_back(matmul(first, w_query)))
    key = low(low_back(matmul(first, w_key)))
    value = low(low_back(matmul(first, w_value)))
    context = low(low_back(attend(query, key, value, segment, SIDE_HEAD)))
    residual = mixed + low_back(matmul(context, w_output))
    second = low(rms(residual, middle_gain))
    pre_act = low_back(matmul(second, w_expand))
    act = low(jax.nn.gelu(pre_act))
    return residual + low_back(matmul(act, w_reduce))

def reference(backbone_in, segment_ids, gate_index, norm_before, norm_middle, frozen_query, frozen_key, frozen_value, frozen_output, frozen_expand, frozen_reduce, tap_weight, gate_table, side_stream, ladder_before, ladder_middle, ladder_query, ladder_key, ladder_value, ladder_output, ladder_expand, ladder_reduce, cotangent):
    frozen = (norm_before, norm_middle, frozen_query.astype(jnp.float32), frozen_key.astype(jnp.float32), frozen_value.astype(jnp.float32), frozen_output.astype(jnp.float32), frozen_expand.astype(jnp.float32), frozen_reduce.astype(jnp.float32))
    params = (tap_weight.astype(jnp.float32), gate_table, ladder_before, ladder_middle, ladder_query.astype(jnp.float32), ladder_key.astype(jnp.float32), ladder_value.astype(jnp.float32), ladder_output.astype(jnp.float32), ladder_expand.astype(jnp.float32), ladder_reduce.astype(jnp.float32))
    group_rows = 4 * SEQ

    def step(totals, inputs):
        rows, segment, stream, upstream = inputs
        top = backbone(rows.astype(jnp.float32), segment, frozen)

        def forward(weights, stream_values):
            return side_forward(top, segment, gate_index, weights, stream_values)
        result, pull = jax.vjp(forward, params, stream.astype(jnp.float32))
        weight_grads, stream_grad = pull(upstream.astype(jnp.float32))
        totals = jax.tree.map(lambda left, right: left + right, totals, weight_grads)
        return (totals, (result.astype(jnp.bfloat16), stream_grad.astype(jnp.bfloat16)))

    def grouped(values):
        return values.reshape((-1, group_rows) + values.shape[1:])
    start = jax.tree.map(jnp.zeros_like, params)
    totals, outputs = lax.scan(step, start, (grouped(backbone_in), grouped(segment_ids), grouped(side_stream), grouped(cotangent)))
    result, stream_grad = outputs
    return (result.reshape(-1, D_SIDE), stream_grad.reshape(-1, D_SIDE), totals[0], totals[1], totals[2], totals[3], totals[4], totals[5], totals[6], totals[7], totals[8], totals[9])
```

```python
import functools

import jax
import jax.numpy as jnp
from jax import lax
from jax.experimental import pallas as pl
from jax.experimental.pallas import tpu as pltpu
from jax.sharding import PartitionSpec as P

HEAD = 64
SIDE_HEAD = 8
SEQ = 1024
EPS = 1e-06
MASKED = -1e30
LOG2E = 1.4426950408889634
SAFE = 64.0
TILE = 512
ROWS = 96

F32 = jnp.float32
BF16 = jnp.bfloat16
NN = (((1,), (0,)), ((), ()))
NT = (((1,), (1,)), ((), ()))
TN = (((0,), (0,)), ((), ()))


def dot(left, right, dims=NN):
    return lax.dot_general(left, right, dims, preferred_element_type=F32)


def gelu_inner(values):
    return 0.7978845608028654 * values * (1.0 + 0.044715 * values * values)


def gelu(values):
    return 0.5 * values * (1.0 + jnp.tanh(gelu_inner(values)))


def gelu_both(values):
    square = values * values
    bend = jnp.tanh(0.7978845608028654 * values * (1.0 + 0.044715 * square))
    half = 0.5 * (1.0 + bend)
    slope = 0.7978845608028654 * (1.0 + 3.0 * 0.044715 * square)
    return values * half, half + 0.5 * values * (1.0 - bend * bend) * slope


def fill_mask(segment_ref, mask_ref):
    row = segment_ref[0].astype(F32)
    column = jnp.transpose(jnp.broadcast_to(row, (8, SEQ)))[:, 0:1]

    def part(step, carry):
        lanes = pl.ds(pl.multiple_of(step * 128, 128), 128)
        tile = segment_ref[0, :, lanes].astype(F32)
        mask_ref[:, lanes] = jnp.where(column == tile, 1.0, 0.0).astype(BF16)
        return carry

    lax.fori_loop(0, SEQ // 128, part, 0)


def weights_of(scores, mask, careful):
    if not careful:
        return jnp.exp2(scores).astype(BF16) * mask
    allowed = mask.astype(F32) > 0.5
    scores = jnp.where(allowed, scores, MASKED)
    highest = jnp.max(scores, axis=0, keepdims=True)
    return jnp.exp2(scores - highest).astype(BF16)


def frozen_kernel(
    segment_ref,
    x_ref,
    before_ref,
    middle_ref,
    wq_ref,
    wk_ref,
    wv_ref,
    wo_ref,
    we_ref,
    wr_ref,
    tap_w_ref,
    top_ref,
    tap_ref,
    mask_ref,
    normed_ref,
    q_ref,
    k_ref,
    v_ref,
    ctx_ref,
    wv_t_ref,
    tap_t_ref,
):
    width = x_ref.shape[1]
    heads = width // HEAD
    padded = v_ref.shape[1]

    @pl.when(pl.program_id(0) == 0)
    def _():
        wv_t_ref[...] = jnp.transpose(wv_ref[...])
        tap_t_ref[...] = jnp.transpose(tap_w_ref[...])

    fill_mask(segment_ref, mask_ref)
    base = x_ref[...].astype(F32)
    factor = lax.rsqrt(jnp.mean(base * base, axis=-1, keepdims=True) + EPS)
    normed_ref[...] = (base * factor * before_ref[...]).astype(BF16)
    member = lax.broadcasted_iota(jnp.int32, (width, 128), 0) // HEAD
    member = jnp.where(member == lax.broadcasted_iota(jnp.int32, (width, 128), 1), 1.0, 0.0).astype(BF16)

    def largest(values):
        wide = values.astype(F32)
        return jnp.max(dot((wide * wide).astype(BF16), member), axis=0, keepdims=True)

    q = (dot(normed_ref[...], wq_ref[...]) * (HEAD**-0.5 * LOG2E)).astype(BF16)
    q_ref[...] = q
    q_top = largest(q)
    k = dot(normed_ref[...], wk_ref[...]).astype(BF16)
    k_ref[...] = k
    bound = jnp.max(q_top * largest(k)) * 1.1
    safe = bound <= SAFE * SAFE
    v = dot(wv_t_ref[...], normed_ref[...], NT).astype(BF16)
    for head in range(heads):
        v_ref[head, 0:HEAD] = v[head * HEAD : (head + 1) * HEAD]
        v_ref[head, HEAD:padded] = jnp.ones((padded - HEAD, SEQ), BF16)

    def attend(careful, tile):
        def one(head, start):
            lanes = pl.ds(start, tile)
            cols = slice(head * HEAD, (head + 1) * HEAD)
            scores = dot(k_ref[:, cols], q_ref[lanes, cols], NT)
            probs = weights_of(scores, mask_ref[:, lanes], careful)
            mixed = dot(v_ref[head], probs)
            ctx_ref[cols, lanes] = (mixed[0:HEAD] / mixed[HEAD : HEAD + 1]).astype(BF16)

        for head in range(heads):
            if careful:

                def step(i, carry):
                    one(head, pl.multiple_of(i * tile, tile))
                    return carry

                lax.fori_loop(0, SEQ // tile, step, 0)
            else:
                for i in range(SEQ // tile):
                    one(head, i * tile)

    pl.when(safe)(lambda: attend(False, TILE))
    pl.when(jnp.logical_not(safe))(lambda: attend(True, 256))

    chunk = 256
    hidden = we_ref.shape[1]
    piece = 768

    for part in range(SEQ // chunk):
        rows = slice(part * chunk, (part + 1) * chunk)
        middle = x_ref[rows].astype(F32) + dot(ctx_ref[:, rows], wo_ref[...], TN)
        scale = lax.rsqrt(jnp.mean(middle * middle, axis=-1, keepdims=True) + EPS)
        normed = (middle * scale * middle_ref[...]).astype(BF16)
        total = middle
        for j in range(hidden // piece):
            cols = slice(j * piece, (j + 1) * piece)
            expanded = gelu(dot(normed, we_ref[:, cols])).astype(BF16)
            total = total + dot(expanded, wr_ref[cols])
        top = total.astype(BF16)
        top_ref[rows] = top
        tap_ref[0, :, rows] = dot(tap_t_ref[...], top, NT).astype(BF16)


def frozen_block(segment, x, before, middle, wq, wk, wv, wo, we, wr, tap_w):
    tokens, width = x.shape
    hidden = we.shape[1]
    heads = width // HEAD
    side = tap_w.shape[1]
    count = tokens // SEQ

    def whole(shape):
        return pl.BlockSpec(shape, lambda i: (0,) * len(shape), pipeline_mode=pl.Buffered(1))

    return pl.pallas_call(
        frozen_kernel,
        grid=(count,),
        in_specs=[
            pl.BlockSpec((1, 1, SEQ), lambda i: (i, 0, 0)),
            pl.BlockSpec((SEQ, width), lambda i: (i, 0)),
            whole((1, width)),
            whole((1, width)),
            whole((width, width)),
            whole((width, width)),
            whole((width, width)),
            whole((width, width)),
            whole((width, hidden)),
            whole((hidden, width)),
            whole((width, side)),
        ],
        out_specs=[
            pl.BlockSpec((SEQ, width), lambda i: (i, 0)),
            pl.BlockSpec((1, side, SEQ), lambda i: (i, 0, 0)),
        ],
        out_shape=[
            jax.ShapeDtypeStruct((tokens, width), BF16),
            jax.ShapeDtypeStruct((count, side, SEQ), BF16),
        ],
        scratch_shapes=[
            pltpu.VMEM((SEQ, SEQ), BF16),
            pltpu.VMEM((SEQ, width), BF16),
            pltpu.VMEM((SEQ, width), BF16),
            pltpu.VMEM((SEQ, width), BF16),
            pltpu.VMEM((heads, HEAD + 16, SEQ), BF16),
            pltpu.VMEM((width, SEQ), BF16),
            pltpu.VMEM((width, width), BF16),
            pltpu.VMEM((side, width), BF16),
        ],
        compiler_params=pltpu.CompilerParams(vmem_limit_bytes=60 << 20),
        name="frozen_block",
    )(segment, x, before, middle, wq, wk, wv, wo, we, wr, tap_w)


def outer_rows(left, right):
    return [left[e : e + 1] * right for e in range(SIDE_HEAD)]


def side_kernel(
    index_ref,
    segment_ref,
    tap_ref,
    stream_ref,
    up_ref,
    top_ref,
    table_ref,
    before_ref,
    middle_ref,
    wide_own_ref,
    wide_other_ref,
    tall_own_ref,
    tall_other_ref,
    out_ref,
    stream_grad_ref,
    tap_grad_ref,
    wide_grad_ref,
    out_grad_ref,
    expand_grad_ref,
    reduce_grad_ref,
    small_ref,
    mask_ref,
    w_ref,
    we_ref,
    wo_ref,
    wr_ref,
    e_ref,
    qkv_ref,
    q16_ref,
    k16_ref,
    rows_ref,
    moment_ref,
    ctx_ref,
    dctx_ref,
    dqkv_ref,
):
    side = tap_ref.shape[1]
    heads = side // SIDE_HEAD
    local = side // 2
    hidden = we_ref.shape[1]
    half = hidden // 2
    first = pl.program_id(0) == 0

    @pl.when(first)
    def _():
        for t in range(3):
            own = slice(half + t * local, half + (t + 1) * local)
            w_ref[:, t * side : t * side + local] = wide_own_ref[:, own]
            w_ref[:, t * side + local : (t + 1) * side] = wide_other_ref[:, own]
        we_ref[:, 0:half] = wide_own_ref[:, 0:half]
        we_ref[:, half:hidden] = wide_other_ref[:, 0:half]
        wo_ref[0:local] = tall_own_ref[0:local]
        wo_ref[local:side] = tall_other_ref[0:local]
        wr_ref[0:half] = tall_own_ref[local : local + half]
        wr_ref[half:hidden] = tall_other_ref[local : local + half]
        tap_grad_ref[...] = jnp.zeros_like(tap_grad_ref)
        wide_grad_ref[...] = jnp.zeros_like(wide_grad_ref)
        out_grad_ref[...] = jnp.zeros_like(out_grad_ref)
        expand_grad_ref[...] = jnp.zeros_like(expand_grad_ref)
        reduce_grad_ref[...] = jnp.zeros_like(reduce_grad_ref)
        small_ref[...] = jnp.zeros_like(small_ref)

    fill_mask(segment_ref, mask_ref)
    logits = table_ref[pl.ds(index_ref[0], 1), :]
    stacked = jnp.concatenate(
        [
            jnp.broadcast_to(jax.nn.sigmoid(logits), (8, side)),
            jnp.broadcast_to(before_ref[...], (8, side)),
            jnp.broadcast_to(middle_ref[...], (8, side)),
        ],
        axis=0,
    )
    columns = jnp.transpose(stacked)
    gate, before, middle = columns[:, 0:1], columns[:, 8:9], columns[:, 16:17]
    eye = jnp.where(
        lax.broadcasted_iota(jnp.int32, (side, side), 0) == lax.broadcasted_iota(jnp.int32, (side, side), 1),
        1.0,
        0.0,
    ).astype(BF16)

    tap = tap_ref[0].astype(F32)
    stream = dot(eye, stream_ref[...], NT)
    mixed = gate * tap + (1.0 - gate) * stream
    factor1 = lax.rsqrt(jnp.mean(mixed * mixed, axis=0, keepdims=True) + EPS)
    n1 = (mixed * factor1 * before).astype(BF16)
    qkv_ref[...] = dot(w_ref[...], n1, TN)

    zeros8 = jnp.zeros((SIDE_HEAD, SEQ), F32)
    ones8 = jnp.ones((SIDE_HEAD, SEQ), F32)

    def prepare(head, bound):
        at = pl.multiple_of(head * SIDE_HEAD, SIDE_HEAD)
        q = qkv_ref[pl.ds(at, SIDE_HEAD)] * (SIDE_HEAD**-0.5 * LOG2E)
        q = q.astype(BF16).astype(F32)
        k = qkv_ref[pl.ds(side + at, SIDE_HEAD)].astype(BF16).astype(F32)
        v = qkv_ref[pl.ds(2 * side + at, SIDE_HEAD)].astype(BF16).astype(F32)
        qkv_ref[pl.ds(at, SIDE_HEAD)] = q
        qkv_ref[pl.ds(side + at, SIDE_HEAD)] = k
        qkv_ref[pl.ds(2 * side + at, SIDE_HEAD)] = v
        q16_ref[head] = jnp.concatenate([q, zeros8], axis=0).astype(BF16)
        k16_ref[head] = jnp.concatenate([k, zeros8], axis=0).astype(BF16)
        rows = [v, ones8, k, zeros8] + outer_rows(v, k)
        rows_ref[head] = jnp.concatenate(rows, axis=0).astype(BF16)
        return jnp.maximum(
            bound,
            jnp.max(jnp.sum(q * q, axis=0, keepdims=True), axis=1, keepdims=True)
            * jnp.max(jnp.sum(k * k, axis=0, keepdims=True), axis=1, keepdims=True),
        )

    bound = lax.fori_loop(0, heads, prepare, jnp.zeros((1, 1), F32))
    safe = jnp.max(bound) * 1.1 <= SAFE * SAFE

    def attend(careful, tile):
        def one(head, start):
            at = pl.multiple_of(head * SIDE_HEAD, SIDE_HEAD)
            lanes = pl.ds(start, tile)
            scores = dot(k16_ref[head], q16_ref[head, :, lanes], TN)
            probs = weights_of(scores, mask_ref[:, lanes], careful)
            e_ref[head, :, lanes] = probs
            found = dot(rows_ref[head], probs)
            inverse = 1.0 / found[8:16]
            ctx_ref[pl.ds(at, SIDE_HEAD), lanes] = found[0:8] * inverse
            moment_ref[head, 8:16, lanes] = inverse
            moment_ref[head, 16:24, lanes] = found[16:24] * inverse
            for e in range(SIDE_HEAD):
                low = 32 + e * SIDE_HEAD
                moment_ref[head, low : low + 8, lanes] = found[low : low + 8] * inverse

        def step(head, carry):
            for i in range(SEQ // tile):
                one(head, i * tile)
            return carry

        lax.fori_loop(0, heads, step, 0)

    pl.when(safe)(lambda: attend(False, TILE))
    pl.when(jnp.logical_not(safe))(lambda: attend(True, TILE))

    ctx = ctx_ref[...].astype(BF16)
    res1 = mixed + dot(wo_ref[...], ctx, TN)
    factor2 = lax.rsqrt(jnp.mean(res1 * res1, axis=0, keepdims=True) + EPS)
    z = res1 * factor2
    n2 = (z * middle).astype(BF16)
    pre = dot(we_ref[...], n2, TN)
    act, slope = gelu_both(pre)
    act = act.astype(BF16)
    result = res1 + dot(wr_ref[...], act, TN)
    out_ref[...] = jnp.transpose(result).astype(BF16)

    up = dot(eye, up_ref[...], NT)
    low_up = up.astype(BF16)
    reduce_grad_ref[...] += dot(act, low_up, NT)
    dpre = (dot(wr_ref[...], low_up) * slope).astype(BF16)
    expand_grad_ref[...] += dot(n2, dpre, NT)
    dn2 = dot(we_ref[...], dpre)
    middle_grad = jnp.sum(dn2 * z, axis=1, keepdims=True)
    u = dn2 * middle
    spread = jnp.mean(u * res1, axis=0, keepdims=True)
    dres1 = up + factor2 * u - z * (factor2 * factor2 * spread)
    low_dres = dres1.astype(BF16)
    out_grad_ref[...] += dot(ctx, low_dres, NT)
    dctx_ref[...] = dot(wo_ref[...], low_dres).astype(BF16).astype(F32)

    def prepare_back(head, carry):
        at = pl.multiple_of(head * SIDE_HEAD, SIDE_HEAD)
        q = qkv_ref[pl.ds(at, SIDE_HEAD)]
        dctx = dctx_ref[pl.ds(at, SIDE_HEAD)]
        inverse = moment_ref[head, 8:16]
        inner = jnp.sum(dctx * ctx_ref[pl.ds(at, SIDE_HEAD)], axis=0, keepdims=True)
        dq = -inner * moment_ref[head, 16:24]
        for e in range(SIDE_HEAD):
            low = 32 + e * SIDE_HEAD
            dq = dq + dctx[e : e + 1] * moment_ref[head, low : low + 8]
        dqkv_ref[pl.ds(at, SIDE_HEAD)] = dq * SIDE_HEAD**-0.5
        scaled = dctx * inverse
        rows = [scaled, zeros8, (inner * inverse) * q, zeros8] + outer_rows(scaled, q)
        rows_ref[head] = jnp.concatenate(rows, axis=0).astype(BF16)
        return carry

    lax.fori_loop(0, heads, prepare_back, 0)

    def back(head, carry):
        at = pl.multiple_of(head * SIDE_HEAD, SIDE_HEAD)
        found = dot(rows_ref[head], e_ref[head], NT)
        v = qkv_ref[pl.ds(2 * side + at, SIDE_HEAD)]
        dk = -found[16:24]
        for e in range(SIDE_HEAD):
            low = 32 + e * SIDE_HEAD
            dk = dk + v[e : e + 1] * found[low : low + 8]
        dqkv_ref[pl.ds(side + at, SIDE_HEAD)] = dk * (1.0 / LOG2E)
        dqkv_ref[pl.ds(2 * side + at, SIDE_HEAD)] = found[0:8]
        return carry

    lax.fori_loop(0, heads, back, 0)

    dqkv = dqkv_ref[...].astype(BF16)
    wide_grad_ref[...] += dot(n1, dqkv, NT)
    dn1 = dot(w_ref[...], dqkv)
    unit = mixed * factor1
    before_grad = jnp.sum(dn1 * unit, axis=1, keepdims=True)
    u = dn1 * before
    spread = jnp.mean(u * mixed, axis=0, keepdims=True)
    dmixed = dres1 + factor1 * u - unit * (factor1 * factor1 * spread)
    logit = jnp.sum(dmixed * (tap - stream), axis=1, keepdims=True) * gate * (1.0 - gate)
    small_ref[...] += jnp.concatenate(
        [logit, before_grad, middle_grad, jnp.zeros((side, 5), F32)], axis=1
    )
    tap_grad_ref[...] += dot((gate * dmixed).astype(BF16), top_ref[...])
    stream_grad_ref[...] = jnp.transpose((1.0 - gate) * dmixed).astype(BF16)


def side_block(index, segment, tap, stream, up, top, table, before, middle, wide_own, wide_other, tall_own, tall_other):
    tokens, side = stream.shape
    width = top.shape[1]
    heads = side // SIDE_HEAD
    half = wide_own.shape[1] - 3 * (side // 2)
    hidden = 2 * half
    count = tokens // SEQ

    def whole(shape, **kw):
        return pl.BlockSpec(shape, lambda i: (0,) * len(shape), **kw)

    one = pl.Buffered(1)
    return pl.pallas_call(
        side_kernel,
        grid=(count,),
        in_specs=[
            pl.BlockSpec(memory_space=pltpu.SMEM),
            pl.BlockSpec((1, 1, SEQ), lambda i: (i, 0, 0)),
            pl.BlockSpec((1, side, SEQ), lambda i: (i, 0, 0)),
            pl.BlockSpec((SEQ, side), lambda i: (i, 0)),
            pl.BlockSpec((SEQ, side), lambda i: (i, 0)),
            pl.BlockSpec((SEQ, width), lambda i: (i, 0)),
            whole(table.shape),
            whole((1, side)),
            whole((1, side)),
            whole(wide_own.shape),
            whole(wide_other.shape),
            whole(tall_own.shape),
            whole(tall_other.shape),
        ],
        out_specs=[
            pl.BlockSpec((SEQ, side), lambda i: (i, 0)),
            pl.BlockSpec((SEQ, side), lambda i: (i, 0)),
            whole((side, width)),
            whole((side, 3 * side)),
            whole((side, side)),
            whole((side, hidden)),
            whole((hidden, side)),
            whole((side, 8)),
        ],
        out_shape=[
            jax.ShapeDtypeStruct((tokens, side), BF16),
            jax.ShapeDtypeStruct((tokens, side), BF16),
            jax.ShapeDtypeStruct((side, width), F32),
            jax.ShapeDtypeStruct((side, 3 * side), F32),
            jax.ShapeDtypeStruct((side, side), F32),
            jax.ShapeDtypeStruct((side, hidden), F32),
            jax.ShapeDtypeStruct((hidden, side), F32),
            jax.ShapeDtypeStruct((side, 8), F32),
        ],
        scratch_shapes=[
            pltpu.VMEM((SEQ, SEQ), BF16),
            pltpu.VMEM((side, 3 * side), BF16),
            pltpu.VMEM((side, hidden), BF16),
            pltpu.VMEM((side, side), BF16),
            pltpu.VMEM((hidden, side), BF16),
            pltpu.VMEM((heads, SEQ, SEQ), BF16),
            pltpu.VMEM((3 * side, SEQ), F32),
            pltpu.VMEM((heads, 16, SEQ), BF16),
            pltpu.VMEM((heads, 16, SEQ), BF16),
            pltpu.VMEM((heads, ROWS, SEQ), BF16),
            pltpu.VMEM((heads, ROWS, SEQ), F32),
            pltpu.VMEM((side, SEQ), F32),
            pltpu.VMEM((side, SEQ), F32),
            pltpu.VMEM((3 * side, SEQ), F32),
        ],
        compiler_params=pltpu.CompilerParams(vmem_limit_bytes=60 << 20),
        name="side_block",
    )(index, segment, tap, stream, up, top, table, before, middle, wide_own, wide_other, tall_own, tall_other)


def shards(
    backbone_in,
    segment_ids,
    gate_index,
    norm_before,
    norm_middle,
    frozen_query,
    frozen_key,
    frozen_value,
    frozen_output,
    frozen_expand,
    frozen_reduce,
    tap_weight,
    gate_table,
    side_stream,
    ladder_before,
    ladder_middle,
    ladder_query,
    ladder_key,
    ladder_value,
    ladder_output,
    ladder_expand,
    ladder_reduce,
    cotangent,
):
    own_rows = backbone_in.shape[0]
    side = side_stream.shape[1]
    local = ladder_query.shape[1]
    half = ladder_expand.shape[1]
    position = lax.axis_index("side")
    swap = [(0, 1), (1, 0)]
    wide = jnp.concatenate([ladder_expand, ladder_query, ladder_key, ladder_value], axis=1)
    tall = jnp.concatenate([ladder_output, ladder_reduce], axis=0)
    wide_other = lax.ppermute(wide, "side", swap)
    tall_other = lax.ppermute(tall, "side", swap)
    segment = lax.dynamic_slice_in_dim(segment_ids, position * own_rows, own_rows).reshape(-1, 1, SEQ)
    top, tap = frozen_block(
        segment,
        backbone_in,
        norm_before[None],
        norm_middle[None],
        frozen_query,
        frozen_key,
        frozen_value,
        frozen_output,
        frozen_expand,
        frozen_reduce,
        tap_weight,
    )
    result, stream_grad, tap_grad, wide_grad, out_grad, expand_grad, reduce_grad, small = side_block(
        gate_index,
        segment,
        tap,
        side_stream,
        cotangent,
        top,
        gate_table,
        ladder_before[None],
        ladder_middle[None],
        wide,
        wide_other,
        tall,
        tall_other,
    )
    q_grad, k_grad, v_grad = (wide_grad[:, t * side : (t + 1) * side] for t in range(3))

    def halves(values, axis):
        size = values.shape[axis] // 2
        return (
            lax.slice_in_dim(values, 0, size, axis=axis),
            lax.slice_in_dim(values, size, 2 * size, axis=axis),
        )

    pairs = [
        halves(q_grad, 1),
        halves(k_grad, 1),
        halves(v_grad, 1),
        halves(out_grad, 0),
        halves(expand_grad, 1),
        halves(reduce_grad, 0),
    ]
    mine = jnp.concatenate([a.reshape(-1) for a, _ in pairs])
    theirs = jnp.concatenate([b.reshape(-1) for _, b in pairs])
    mine = mine + lax.ppermute(theirs, "side", swap)
    mine = lax.psum(mine, "dp")
    shared = lax.psum(jnp.concatenate([tap_grad.reshape(-1), small.reshape(-1)]), ("dp", "side"))
    outs = []
    at = 0
    for a, _ in pairs:
        outs.append(mine[at : at + a.size].reshape(a.shape))
        at += a.size
    tap_sum = shared[: tap_grad.size].reshape(tap_grad.shape).T
    small_sum = shared[tap_grad.size :].reshape(small.shape)
    pick = (jnp.arange(gate_table.shape[0]) == gate_index[0]).astype(F32)
    gate_sum = pick[:, None] * small_sum[:, 0][None, :]
    return (
        result,
        stream_grad,
        tap_sum,
        gate_sum,
        small_sum[:, 1],
        small_sum[:, 2],
        *outs,
    )


def solution(mesh):
    rows = P(("dp", "side"), None)
    placed = (
        rows,
        P("dp"),
        *([P()] * 11),
        rows,
        P(),
        P(),
        P(None, "side"),
        P(None, "side"),
        P(None, "side"),
        P("side", None),
        P(None, "side"),
        P("side", None),
        rows,
    )
    return jax.shard_map(
        shards,
        mesh=mesh,
        in_specs=placed,
        out_specs=(
            rows,
            rows,
            P(),
            P(),
            P(),
            P(),
            P(None, "side"),
            P(None, "side"),
            P(None, "side"),
            P("side", None),
            P(None, "side"),
            P("side", None),
        ),
        check_vma=False,
    )
```

```python
import functools

import jax
import jax.numpy as jnp
from jax import lax
from jax.experimental import pallas as pl
from jax.experimental.pallas import tpu as pltpu
from jax.sharding import PartitionSpec as P

HEAD = 64
SIDE_HEAD = 8
SEQ = 1024
EPS = 1e-06
MASKED = -1e30
LOG2E = 1.4426950408889634
SAFE = 64.0
TILE = 512
ROWS = 96

F32 = jnp.float32
BF16 = jnp.bfloat16
NN = (((1,), (0,)), ((), ()))
NT = (((1,), (1,)), ((), ()))
TN = (((0,), (0,)), ((), ()))


def dot(left, right, dims=NN):
    return lax.dot_general(left, right, dims, preferred_element_type=F32)


def gelu_inner(values):
    return 0.7978845608028654 * values * (1.0 + 0.044715 * values * values)


def gelu(values):
    return 0.5 * values * (1.0 + jnp.tanh(gelu_inner(values)))


def gelu_both(values):
    square = values * values
    bend = jnp.tanh(0.7978845608028654 * values * (1.0 + 0.044715 * square))
    half = 0.5 * (1.0 + bend)
    slope = 0.7978845608028654 * (1.0 + 3.0 * 0.044715 * square)
    return values * half, half + 0.5 * values * (1.0 - bend * bend) * slope


def fill_mask(row, mask_ref):
    row = row.astype(F32)
    column = jnp.transpose(jnp.broadcast_to(row, (8, SEQ)))[:, 0:1]
    for step in range(SEQ // 128):
        lanes = slice(step * 128, (step + 1) * 128)
        mask_ref[:, lanes] = jnp.where(column == row[:, lanes], 1.0, 0.0).astype(BF16)


def weights_of(scores, mask, careful):
    if not careful:
        return jnp.exp2(scores).astype(BF16) * mask
    allowed = mask.astype(F32) > 0.5
    scores = jnp.where(allowed, scores, MASKED)
    highest = jnp.max(scores, axis=0, keepdims=True)
    return jnp.exp2(scores - highest).astype(BF16)


def frozen_kernel(
    segment_ref,
    x_ref,
    before_ref,
    middle_ref,
    wq_ref,
    wk_ref,
    wv_ref,
    wo_ref,
    we_ref,
    wr_ref,
    tap_t_ref,
    top_ref,
    tap_ref,
    mask_ref,
    normed_ref,
    q_ref,
    k_ref,
    v_ref,
    ctx_ref,
    wv_t_ref,
):
    width = x_ref.shape[1]
    heads = width // HEAD
    padded = v_ref.shape[1]

    @pl.when(pl.program_id(0) == 0)
    def _():
        wv_t_ref[...] = jnp.transpose(wv_ref[...])

    here = lax.axis_index("side") * pl.num_programs(0) + pl.program_id(0)
    fill_mask(segment_ref[here], mask_ref)
    base = x_ref[...].astype(F32)
    factor = lax.rsqrt(jnp.mean(base * base, axis=-1, keepdims=True) + EPS)
    normed_ref[...] = (base * factor * before_ref[...][None]).astype(BF16)
    member = lax.broadcasted_iota(jnp.int32, (width, 128), 0) // HEAD
    member = jnp.where(member == lax.broadcasted_iota(jnp.int32, (width, 128), 1), 1.0, 0.0).astype(BF16)

    def largest(values):
        wide = values.astype(F32)
        return jnp.max(dot((wide * wide).astype(BF16), member), axis=0, keepdims=True)

    q = (dot(normed_ref[...], wq_ref[...]) * (HEAD**-0.5 * LOG2E)).astype(BF16)
    q_ref[...] = q
    q_top = largest(q)
    k = dot(normed_ref[...], wk_ref[...]).astype(BF16)
    k_ref[...] = k
    bound = jnp.max(q_top * largest(k)) * 1.1
    safe = bound <= SAFE * SAFE
    v = dot(wv_t_ref[...], normed_ref[...], NT).astype(BF16)
    for head in range(heads):
        v_ref[head, 0:HEAD] = v[head * HEAD : (head + 1) * HEAD]
        v_ref[head, HEAD:padded] = jnp.ones((padded - HEAD, SEQ), BF16)

    def attend(careful, tile):
        def one(head, start):
            lanes = pl.ds(start, tile)
            cols = slice(head * HEAD, (head + 1) * HEAD)
            scores = dot(k_ref[:, cols], q_ref[lanes, cols], NT)
            probs = weights_of(scores, mask_ref[:, lanes], careful)
            mixed = dot(v_ref[head], probs)
            ctx_ref[cols, lanes] = (mixed[0:HEAD] / mixed[HEAD : HEAD + 1]).astype(BF16)

        for head in range(heads):
            if careful:

                def step(i, carry):
                    one(head, pl.multiple_of(i * tile, tile))
                    return carry

                lax.fori_loop(0, SEQ // tile, step, 0)
            else:
                for i in range(SEQ // tile):
                    one(head, i * tile)

    pl.when(safe)(lambda: attend(False, TILE))
    pl.when(jnp.logical_not(safe))(lambda: attend(True, 256))

    chunk = 256
    hidden = we_ref.shape[1]
    piece = 768

    for part in range(SEQ // chunk):
        rows = slice(part * chunk, (part + 1) * chunk)
        middle = x_ref[rows].astype(F32) + dot(ctx_ref[:, rows], wo_ref[...], TN)
        scale = lax.rsqrt(jnp.mean(middle * middle, axis=-1, keepdims=True) + EPS)
        normed = (middle * scale * middle_ref[...][None]).astype(BF16)
        total = middle
        for j in range(hidden // piece):
            cols = slice(j * piece, (j + 1) * piece)
            expanded = gelu(dot(normed, we_ref[:, cols])).astype(BF16)
            total = total + dot(expanded, wr_ref[cols])
        top = total.astype(BF16)
        top_ref[rows] = top
        tap_ref[:, rows] = dot(tap_t_ref[...], top, NT).astype(BF16)


def whole(array):
    shape = array.shape
    return pl.BlockSpec(shape, lambda i: (0,) * len(shape), pipeline_mode=pl.Buffered(1))


def frozen_block(segment, x, before, middle, wq, wk, wv, wo, we, wr, tap_t):
    tokens, width = x.shape
    heads = width // HEAD
    side = tap_t.shape[0]
    return pl.pallas_call(
        frozen_kernel,
        grid=(tokens // SEQ,),
        in_specs=[
            whole(segment),
            pl.BlockSpec((SEQ, width), lambda i: (i, 0)),
            *map(whole, (before, middle, wq, wk, wv, wo, we, wr, tap_t)),
        ],
        out_specs=[
            pl.BlockSpec((SEQ, width), lambda i: (i, 0)),
            pl.BlockSpec((side, SEQ), lambda i: (0, i)),
        ],
        out_shape=[
            jax.ShapeDtypeStruct((tokens, width), BF16),
            jax.ShapeDtypeStruct((side, tokens), BF16),
        ],
        scratch_shapes=[
            pltpu.VMEM((SEQ, SEQ), BF16),
            pltpu.VMEM((SEQ, width), BF16),
            pltpu.VMEM((SEQ, width), BF16),
            pltpu.VMEM((SEQ, width), BF16),
            pltpu.VMEM((heads, HEAD + 16, SEQ), BF16),
            pltpu.VMEM((width, SEQ), BF16),
            pltpu.VMEM((width, width), BF16),
        ],
        compiler_params=pltpu.CompilerParams(vmem_limit_bytes=60 << 20),
        name="frozen_block",
    )(segment, x, before, middle, wq, wk, wv, wo, we, wr, tap_t)


def outer_rows(left, right):
    return [left[e : e + 1] * right for e in range(SIDE_HEAD)]


def pack_kernel(expand_ref, q_ref, k_ref, v_ref, output_ref, reduce_ref, packed_ref):
    side, half = expand_ref.shape
    packed_ref[0:side] = expand_ref[:, 0:side]
    packed_ref[side : 2 * side] = expand_ref[:, side:half]
    at = half
    for ref in (q_ref, k_ref, v_ref, output_ref, reduce_ref):
        packed_ref[at : at + ref.shape[0]] = ref[...]
        at += ref.shape[0]


def side_kernel(
    index_ref,
    segment_ref,
    tap_ref,
    stream_ref,
    up_ref,
    top_ref,
    table_ref,
    before_ref,
    middle_ref,
    own_ref,
    other_ref,
    out_ref,
    stream_grad_ref,
    keep_ref,
    send_ref,
    tap_grad_ref,
    qkv_grad_ref,
    out_grad_ref,
    expand_grad_ref,
    reduce_grad_ref,
    small_ref,
    bundle_ref,
    mask_ref,
    w_ref,
    we_ref,
    wo_ref,
    wr_ref,
    e_ref,
    qkv_ref,
    q16_ref,
    k16_ref,
    rows_ref,
    moment_ref,
    ctx_ref,
    dctx_ref,
    dqkv_ref,
):
    side = tap_ref.shape[0]
    heads = side // SIDE_HEAD
    local = side // 2
    hidden = we_ref.shape[1]
    half = hidden // 2

    @pl.when(pl.program_id(0) == 0)
    def _():
        for turn, ref in ((0, own_ref), (1, other_ref)):
            we_ref[:, turn * half : turn * half + side] = ref[0:side]
            we_ref[:, turn * half + side : (turn + 1) * half] = ref[side:half]
            at = half
            w_ref[turn * 3 * local : (turn + 1) * 3 * local] = ref[at : at + 3 * local]
            at += 3 * local
            wo_ref[turn * local : (turn + 1) * local] = ref[at : at + local]
            at += local
            wr_ref[turn * half : (turn + 1) * half] = ref[at : at + half]
        tap_grad_ref[...] = jnp.zeros_like(tap_grad_ref)
        qkv_grad_ref[...] = jnp.zeros_like(qkv_grad_ref)
        out_grad_ref[...] = jnp.zeros_like(out_grad_ref)
        expand_grad_ref[...] = jnp.zeros_like(expand_grad_ref)
        reduce_grad_ref[...] = jnp.zeros_like(reduce_grad_ref)
        small_ref[...] = jnp.zeros_like(small_ref)

    here = lax.axis_index("side") * pl.num_programs(0) + pl.program_id(0)
    fill_mask(segment_ref[here], mask_ref)
    logits = table_ref[pl.ds(index_ref[0], 1), :]
    stacked = jnp.concatenate(
        [
            jnp.broadcast_to(jax.nn.sigmoid(logits), (8, side)),
            jnp.broadcast_to(before_ref[...], (8, side)),
            jnp.broadcast_to(middle_ref[...], (8, side)),
        ],
        axis=0,
    )
    columns = jnp.transpose(stacked)
    gate, before, middle = columns[:, 0:1], columns[:, 8:9], columns[:, 16:17]

    def head_rows(kind, head):
        start = (head // (heads // 2)) * 3 * local + kind * local + (head % (heads // 2)) * SIDE_HEAD
        return pl.ds(pl.multiple_of(start, SIDE_HEAD), SIDE_HEAD)

    tap = tap_ref[...].astype(F32)
    stream = stream_ref[...].astype(F32)
    mixed = gate * tap + (1.0 - gate) * stream
    factor1 = lax.rsqrt(jnp.mean(mixed * mixed, axis=0, keepdims=True) + EPS)
    n1 = (mixed * factor1 * before).astype(BF16)
    qkv_ref[...] = dot(w_ref[...], n1)

    zeros8 = jnp.zeros((SIDE_HEAD, SEQ), F32)
    ones8 = jnp.ones((SIDE_HEAD, SEQ), F32)

    def prepare(head, bound):
        q = qkv_ref[head_rows(0, head)] * (SIDE_HEAD**-0.5 * LOG2E)
        q = q.astype(BF16).astype(F32)
        k = qkv_ref[head_rows(1, head)].astype(BF16).astype(F32)
        v = qkv_ref[head_rows(2, head)].astype(BF16).astype(F32)
        qkv_ref[head_rows(0, head)] = q
        qkv_ref[head_rows(1, head)] = k
        qkv_ref[head_rows(2, head)] = v
        q16_ref[head] = jnp.concatenate([q, zeros8], axis=0).astype(BF16)
        k16_ref[head] = jnp.concatenate([k, zeros8], axis=0).astype(BF16)
        rows = [v, ones8, k, zeros8] + outer_rows(v, k)
        rows_ref[head] = jnp.concatenate(rows, axis=0).astype(BF16)
        return jnp.maximum(
            bound,
            jnp.max(jnp.sum(q * q, axis=0, keepdims=True), axis=1, keepdims=True)
            * jnp.max(jnp.sum(k * k, axis=0, keepdims=True), axis=1, keepdims=True),
        )

    bound = lax.fori_loop(0, heads, prepare, jnp.zeros((1, 1), F32))
    safe = jnp.max(bound) * 1.1 <= SAFE * SAFE

    def attend(careful, tile):
        def one(head, start):
            at = pl.multiple_of(head * SIDE_HEAD, SIDE_HEAD)
            lanes = pl.ds(start, tile)
            scores = dot(k16_ref[head], q16_ref[head, :, lanes], TN)
            probs = weights_of(scores, mask_ref[:, lanes], careful)
            e_ref[head, :, lanes] = probs
            found = dot(rows_ref[head], probs)
            inverse = 1.0 / found[8:16]
            ctx_ref[pl.ds(at, SIDE_HEAD), lanes] = found[0:8] * inverse
            moment_ref[head, 8:16, lanes] = inverse
            moment_ref[head, 16:24, lanes] = found[16:24] * inverse
            for e in range(SIDE_HEAD):
                low = 32 + e * SIDE_HEAD
                moment_ref[head, low : low + 8, lanes] = found[low : low + 8] * inverse

        def step(head, carry):
            for i in range(SEQ // tile):
                one(head, i * tile)
            return carry

        lax.fori_loop(0, heads, step, 0)

    pl.when(safe)(lambda: attend(False, TILE))
    pl.when(jnp.logical_not(safe))(lambda: attend(True, TILE))

    ctx = ctx_ref[...].astype(BF16)
    res1 = mixed + dot(wo_ref[...], ctx, TN)
    factor2 = lax.rsqrt(jnp.mean(res1 * res1, axis=0, keepdims=True) + EPS)
    z = res1 * factor2
    n2 = (z * middle).astype(BF16)
    pre = dot(we_ref[...], n2, TN)
    act, slope = gelu_both(pre)
    act = act.astype(BF16)
    result = res1 + dot(wr_ref[...], act, TN)
    out_ref[...] = result.astype(BF16)

    low_up = up_ref[...]
    up = low_up.astype(F32)
    reduce_grad_ref[...] += dot(low_up, act, NT)
    dpre = (dot(wr_ref[...], low_up) * slope).astype(BF16)
    expand_grad_ref[...] += dot(n2, dpre, NT)
    dn2 = dot(we_ref[...], dpre)
    middle_grad = jnp.sum(dn2 * z, axis=1, keepdims=True)
    u = dn2 * middle
    spread = jnp.mean(u * res1, axis=0, keepdims=True)
    dres1 = up + factor2 * u - z * (factor2 * factor2 * spread)
    low_dres = dres1.astype(BF16)
    out_grad_ref[...] += dot(low_dres, ctx, NT)
    dctx_ref[...] = dot(wo_ref[...], low_dres).astype(BF16).astype(F32)

    def prepare_back(head, carry):
        at = pl.multiple_of(head * SIDE_HEAD, SIDE_HEAD)
        q = qkv_ref[head_rows(0, head)]
        dctx = dctx_ref[pl.ds(at, SIDE_HEAD)]
        inverse = moment_ref[head, 8:16]
        inner = jnp.sum(dctx * ctx_ref[pl.ds(at, SIDE_HEAD)], axis=0, keepdims=True)
        dq = -inner * moment_ref[head, 16:24]
        for e in range(SIDE_HEAD):
            low = 32 + e * SIDE_HEAD
            dq = dq + dctx[e : e + 1] * moment_ref[head, low : low + 8]
        dqkv_ref[head_rows(0, head)] = dq * SIDE_HEAD**-0.5
        scaled = dctx * inverse
        rows = [scaled, zeros8, (inner * inverse) * q, zeros8] + outer_rows(scaled, q)
        rows_ref[head] = jnp.concatenate(rows, axis=0).astype(BF16)
        return carry

    lax.fori_loop(0, heads, prepare_back, 0)

    def back(head, carry):
        found = dot(rows_ref[head], e_ref[head], NT)
        v = qkv_ref[head_rows(2, head)]
        dk = -found[16:24]
        for e in range(SIDE_HEAD):
            low = 32 + e * SIDE_HEAD
            dk = dk + v[e : e + 1] * found[low : low + 8]
        dqkv_ref[head_rows(1, head)] = dk * (1.0 / LOG2E)
        dqkv_ref[head_rows(2, head)] = found[0:8]
        return carry

    lax.fori_loop(0, heads, back, 0)

    dqkv = dqkv_ref[...].astype(BF16)
    qkv_grad_ref[...] += dot(n1, dqkv, NT)
    dn1 = dot(w_ref[...], dqkv, TN)
    unit = mixed * factor1
    before_grad = jnp.sum(dn1 * unit, axis=1, keepdims=True)
    u = dn1 * before
    spread = jnp.mean(u * mixed, axis=0, keepdims=True)
    dmixed = dres1 + factor1 * u - unit * (factor1 * factor1 * spread)
    logit = jnp.sum(dmixed * (tap - stream), axis=1, keepdims=True) * gate * (1.0 - gate)
    small_ref[...] += jnp.concatenate(
        [logit, before_grad, middle_grad, jnp.zeros((side, 5), F32)], axis=1
    )
    tap_grad_ref[...] += dot((gate * dmixed).astype(BF16), top_ref[...])
    stream_grad_ref[...] = ((1.0 - gate) * dmixed).astype(BF16)

    @pl.when(pl.program_id(0) == pl.num_programs(0) - 1)
    def _():
        for turn in range(2):
            bundle_ref[turn] = jnp.concatenate(
                [
                    expand_grad_ref[:, turn * half : (turn + 1) * half],
                    reduce_grad_ref[:, turn * half : (turn + 1) * half],
                    qkv_grad_ref[:, turn * 3 * local : (turn + 1) * 3 * local],
                    out_grad_ref[:, turn * local : (turn + 1) * local],
                    small_ref[...],
                    jnp.zeros((side, bundle_ref.shape[2] - 2 * half - 4 * local - 8), F32),
                ],
                axis=1,
            )
        place = lax.axis_index("dp")
        me = (place % 2, (place // 2) % 2, lax.axis_index("side"))
        fourth = side // 4
        width = tap_grad_ref.shape[1]
        for core in range(2):
            for x in range(2):
                part = 2 * (me[0] ^ core) + (me[1] ^ x)
                lines = pl.ds(pl.multiple_of(part * fourth, 8), fourth)
                for turn in range(2):
                    first = (me[2] ^ turn) * (width // 2)
                    pieces = [
                        tap_grad_ref[lines, pl.ds(pl.multiple_of(first + j * 128, 128), 128)]
                        for j in range(width // 256)
                    ] + [
                        bundle_ref[turn, lines, j * 128 : (j + 1) * 128]
                        for j in range(bundle_ref.shape[2] // 128)
                    ]
                    block = jnp.concatenate(pieces, axis=0).astype(BF16)
                    (send_ref if core else keep_ref)[2 * x + turn] = block


def side_block(index, segment, tap, stream, up, top, table, before, middle, own, other):
    side, tokens = stream.shape
    width = top.shape[1]
    heads = side // SIDE_HEAD
    hidden = own.shape[0] - 2 * side
    bundle = -(-(hidden + 2 * side + 8) // 128) * 128
    block = (side // 4) * (width // 256 + bundle // 128)

    def lanes(height):
        return pl.BlockSpec((height, SEQ), lambda i: (0, i))

    packed = pl.BlockSpec((4, block, 128), lambda i: (0, 0, 0))
    return pl.pallas_call(
        side_kernel,
        grid=(tokens // SEQ,),
        in_specs=[
            pl.BlockSpec(memory_space=pltpu.SMEM),
            whole(segment),
            lanes(side),
            lanes(side),
            lanes(side),
            pl.BlockSpec((SEQ, width), lambda i: (i, 0)),
            *map(whole, (table, before, middle, own, other)),
        ],
        out_specs=[lanes(side), lanes(side), packed, packed],
        out_shape=[
            jax.ShapeDtypeStruct((side, tokens), BF16),
            jax.ShapeDtypeStruct((side, tokens), BF16),
            jax.ShapeDtypeStruct((4, block, 128), BF16),
            jax.ShapeDtypeStruct((4, block, 128), BF16),
        ],
        scratch_shapes=[
            pltpu.VMEM((side, width), F32),
            pltpu.VMEM((side, 3 * side), F32),
            pltpu.VMEM((side, side), F32),
            pltpu.VMEM((side, hidden), F32),
            pltpu.VMEM((side, hidden), F32),
            pltpu.VMEM((side, 8), F32),
            pltpu.VMEM((2, side, bundle), F32),
            pltpu.VMEM((SEQ, SEQ), BF16),
            pltpu.VMEM((3 * side, side), BF16),
            pltpu.VMEM((side, hidden), BF16),
            pltpu.VMEM((side, side), BF16),
            pltpu.VMEM((hidden, side), BF16),
            pltpu.VMEM((heads, SEQ, SEQ), BF16),
            pltpu.VMEM((3 * side, SEQ), F32),
            pltpu.VMEM((heads, 16, SEQ), BF16),
            pltpu.VMEM((heads, 16, SEQ), BF16),
            pltpu.VMEM((heads, ROWS, SEQ), BF16),
            pltpu.VMEM((heads, ROWS, SEQ), F32),
            pltpu.VMEM((side, SEQ), F32),
            pltpu.VMEM((side, SEQ), F32),
            pltpu.VMEM((3 * side, SEQ), F32),
        ],
        compiler_params=pltpu.CompilerParams(vmem_limit_bytes=60 << 20),
        name="side_block",
    )(index, segment, tap, stream, up, top, table, before, middle, own, other)


def unpack_kernel(
    index_ref,
    near_ref,
    far_ref,
    tap_ref,
    gate_ref,
    before_ref,
    middle_ref,
    q_ref,
    k_ref,
    v_ref,
    output_ref,
    expand_ref,
    reduce_ref,
    bundle_ref,
):
    side, width = tap_ref.shape
    half = expand_ref.shape[1]
    local = side // 2
    fourth = side // 4
    taps = width // 256
    tiles = bundle_ref.shape[1] // 128
    block = fourth * (taps + tiles)
    place = lax.axis_index("dp")
    me = (place % 2, (place // 2) % 2, lax.axis_index("side"))
    for core in range(2):
        held = (far_ref if core else near_ref)[...].astype(F32)
        for x in range(2):
            part = 2 * (me[0] ^ core) + (me[1] ^ x)
            lines = pl.ds(pl.multiple_of(part * fourth, 8), fourth)
            for turn in range(2):
                at = 2 * block + x * taps * fourth if turn else x * block
                first = (me[2] ^ turn) * (width // 2)
                for j in range(taps):
                    cols = pl.ds(pl.multiple_of(first + j * 128, 128), 128)
                    tap_ref[lines, cols] = held[at + j * fourth : at + (j + 1) * fourth]
            for j in range(tiles):
                at = x * block + (taps + j) * fourth
                bundle_ref[lines, j * 128 : (j + 1) * 128] = held[at : at + fourth]
    expand_ref[...] = bundle_ref[:, 0:half]
    reduce_ref[...] = jnp.transpose(bundle_ref[:, half : 2 * half])
    rest = jnp.transpose(bundle_ref[:, 2 * half : 2 * half + 4 * local + 8])
    q_ref[...] = rest[0:local]
    k_ref[...] = rest[local : 2 * local]
    v_ref[...] = rest[2 * local : 3 * local]
    output_ref[...] = rest[3 * local : 4 * local]
    small = rest[4 * local : 4 * local + 8]
    picked = lax.broadcasted_iota(jnp.int32, gate_ref.shape, 0) == index_ref[0]
    gate_ref[...] = jnp.where(picked, small[0:1], 0.0)
    before_ref[...] = small[1:2]
    middle_ref[...] = small[2:3]


def exchange(values, dp, side, dp_size):
    pairs = [
        (2 * i + s, 2 * (i ^ dp) + (s ^ side)) for i in range(dp_size) for s in range(2)
    ]
    return lax.ppermute(values, ("dp", "side"), pairs)


def add(*values):
    return functools.reduce(lambda a, b: a + b, [v.astype(F32) for v in values]).astype(BF16)


def shards(
    dp_size,
    backbone_in,
    segment_ids,
    gate_index,
    norm_before,
    norm_middle,
    frozen_query,
    frozen_key,
    frozen_value,
    frozen_output,
    frozen_expand,
    frozen_reduce,
    tap_weight,
    gate_table,
    side_stream,
    ladder_before,
    ladder_middle,
    ladder_query,
    ladder_key,
    ladder_value,
    ladder_output,
    ladder_expand,
    ladder_reduce,
    cotangent,
):
    side = side_stream.shape[1]
    width = tap_weight.shape[0]
    local = side // 2
    half = ladder_expand.shape[1]
    swap = functools.partial(exchange, dp_size=dp_size)
    own = pl.pallas_call(
        pack_kernel,
        out_shape=jax.ShapeDtypeStruct((2 * half + 4 * local, side), BF16),
        name="pack_weights",
    )(ladder_expand, ladder_query.T, ladder_key.T, ladder_value.T, ladder_output, ladder_reduce)
    other = swap(own, 0, 1)
    segment = segment_ids.reshape(-1, 1, SEQ)
    top, tap = frozen_block(
        segment,
        backbone_in,
        norm_before,
        norm_middle,
        frozen_query,
        frozen_key,
        frozen_value,
        frozen_output,
        frozen_expand,
        frozen_reduce,
        tap_weight.T,
    )
    result, stream_grad, keep, send = side_block(
        gate_index,
        segment,
        tap,
        side_stream.T,
        cotangent.T,
        top,
        gate_table,
        ladder_before[None],
        ladder_middle[None],
        own,
        other,
    )
    block = keep.shape[1]
    taps = (side // 4) * (width // 256)
    quad = add(keep, swap(send, 1, 0))
    mine = add(quad[0], swap(quad[1], 0, 1), swap(quad[2], 2, 0), swap(quad[3], 2, 1))
    bit = 4
    while bit < dp_size:
        steps = [bit] if 2 * bit >= dp_size else [bit, 2 * bit, 3 * bit]
        mine = add(mine, *[swap(mine, step, 0) for step in steps])
        bit *= 2 * len(steps) if len(steps) == 1 else 4
    near = jnp.concatenate(
        [mine, swap(mine, 2, 0), swap(mine[:taps], 0, 1), swap(mine[:taps], 2, 1)], axis=0
    )
    far = swap(near, 1, 0)
    shape = functools.partial(jax.ShapeDtypeStruct, dtype=F32)
    tap_sum, gate_sum, before_sum, middle_sum, q_sum, k_sum, v_sum, out_sum, expand_sum, reduce_sum = pl.pallas_call(
        unpack_kernel,
        in_specs=[
            pl.BlockSpec(memory_space=pltpu.SMEM),
            pl.BlockSpec(memory_space=pltpu.VMEM),
            pl.BlockSpec(memory_space=pltpu.VMEM),
        ],
        out_shape=[
            shape((side, width)),
            shape(gate_table.shape),
            shape((1, side)),
            shape((1, side)),
            shape((local, side)),
            shape((local, side)),
            shape((local, side)),
            shape((local, side)),
            shape((side, half)),
            shape((half, side)),
        ],
        scratch_shapes=[pltpu.VMEM((side, (block - taps) // (side // 4) * 128), F32)],
        name="unpack_gradients",
    )(gate_index, near, far)
    return (
        result.T,
        stream_grad.T,
        tap_sum.T,
        gate_sum,
        before_sum[0],
        middle_sum[0],
        q_sum.T,
        k_sum.T,
        v_sum.T,
        out_sum,
        expand_sum,
        reduce_sum,
    )


def solution(mesh):
    rows = P(("dp", "side"), None)
    placed = (
        rows,
        P("dp"),
        *([P()] * 11),
        rows,
        P(),
        P(),
        P(None, "side"),
        P(None, "side"),
        P(None, "side"),
        P("side", None),
        P(None, "side"),
        P("side", None),
        rows,
    )
    return jax.shard_map(
        functools.partial(shards, mesh.shape["dp"]),
        mesh=mesh,
        in_specs=placed,
        out_specs=(
            rows,
            rows,
            P(),
            P(),
            P(),
            P(),
            P(None, "side"),
            P(None, "side"),
            P(None, "side"),
            P("side", None),
            P(None, "side"),
            P("side", None),
        ),
        check_vma=False,
    )
```

```python
import functools

import jax
import jax.numpy as jnp
from jax import lax
from jax.experimental import pallas as pl
from jax.experimental.pallas import tpu as pltpu
from jax.sharding import PartitionSpec as P

HEAD = 64
SIDE_HEAD = 8
SEQ = 1024
EPS = 1e-06
MASKED = -1e30
LOG2E = 1.4426950408889634
SAFE = 64.0
TILE = 512
ROWS = 96
GROUP = 4
PAIRS = 2

F32 = jnp.float32
BF16 = jnp.bfloat16
NN = (((1,), (0,)), ((), ()))
NT = (((1,), (1,)), ((), ()))
TN = (((0,), (0,)), ((), ()))


def dot(left, right, dims=NN):
    return lax.dot_general(left, right, dims, preferred_element_type=F32)


def gelu_inner(values):
    return 0.7978845608028654 * values * (1.0 + 0.044715 * values * values)


def gelu(values):
    return 0.5 * values * (1.0 + jnp.tanh(gelu_inner(values)))


def gelu_both(values):
    square = values * values
    bend = jnp.tanh(0.7978845608028654 * values * (1.0 + 0.044715 * square))
    half = 0.5 * (1.0 + bend)
    slope = 0.7978845608028654 * (1.0 + 3.0 * 0.044715 * square)
    return values * half, half + 0.5 * values * (1.0 - bend * bend) * slope


def fill_mask(row, mask_ref):
    row = row.astype(F32)
    column = jnp.transpose(jnp.broadcast_to(row, (8, SEQ)))[:, 0:1]
    for step in range(SEQ // 128):
        lanes = slice(step * 128, (step + 1) * 128)
        mask_ref[:, lanes] = jnp.where(column == row[:, lanes], 1.0, 0.0).astype(BF16)


def weights_of(scores, mask, careful):
    if not careful:
        return jnp.exp2(scores).astype(BF16) * mask
    allowed = mask.astype(F32) > 0.5
    scores = jnp.where(allowed, scores, MASKED)
    highest = jnp.max(scores, axis=0, keepdims=True)
    return jnp.exp2(scores - highest).astype(BF16)


def frozen_kernel(
    segment_ref,
    x_ref,
    before_ref,
    middle_ref,
    tap_t_ref,
    wq_hbm,
    wk_hbm,
    wv_hbm,
    wo_hbm,
    we_hbm,
    wr_hbm,
    top_ref,
    tap_ref,
    wq_ref,
    wk_ref,
    wv_ref,
    wo_ref,
    we_ref,
    wr_ref,
    copied,
    mask_ref,
    normed_ref,
    q_ref,
    k_ref,
    v_ref,
    ctx_ref,
    wv_t_ref,
):
    width = x_ref.shape[1]
    heads = width // HEAD
    padded = v_ref.shape[1]

    starting = pl.program_id(0) == 0
    copies = [
        pltpu.make_async_copy(source, target, copied.at[i])
        for i, (source, target) in enumerate(
            (
                (wq_hbm, wq_ref),
                (wk_hbm, wk_ref),
                (wv_hbm, wv_ref),
                (wo_hbm, wo_ref),
                (we_hbm, we_ref),
                (wr_hbm, wr_ref),
            )
        )
    ]

    @pl.when(starting)
    def _():
        for copy in copies:
            copy.start()
        v_ref[:, HEAD:padded] = jnp.ones((heads, padded - HEAD, SEQ), BF16)

    here = lax.axis_index("side") * pl.num_programs(0) + pl.program_id(0)
    fill_mask(segment_ref[here], mask_ref)
    base = x_ref[...].astype(F32)
    factor = lax.rsqrt(jnp.mean(base * base, axis=-1, keepdims=True) + EPS)
    normed_ref[...] = (base * factor * before_ref[...][None]).astype(BF16)
    member = lax.broadcasted_iota(jnp.int32, (width, 128), 0) // HEAD
    member = jnp.where(member == lax.broadcasted_iota(jnp.int32, (width, 128), 1), 1.0, 0.0).astype(BF16)

    def largest(values):
        wide = values.astype(F32)
        return jnp.max(dot((wide * wide).astype(BF16), member), axis=0, keepdims=True)

    @pl.when(starting)
    def _():
        for copy in copies[0:3]:
            copy.wait()
        wv_t_ref[...] = jnp.transpose(wv_ref[...])

    q = (dot(normed_ref[...], wq_ref[...]) * (HEAD**-0.5 * LOG2E)).astype(BF16)
    q_ref[...] = q
    q_top = largest(q)
    k = dot(normed_ref[...], wk_ref[...]).astype(BF16)
    k_ref[...] = k
    bound = jnp.max(q_top * largest(k)) * 1.1
    safe = bound <= SAFE * SAFE
    v = dot(wv_t_ref[...], normed_ref[...], NT).astype(BF16)
    for head in range(heads):
        v_ref[head, 0:HEAD] = v[head * HEAD : (head + 1) * HEAD]

    def attend(careful, tile, together):
        def one(pair, turn, start):
            lanes = pl.ds(start, tile)
            both = pl.ds(pl.multiple_of(pair * 2 * HEAD, 2 * HEAD), 2 * HEAD)
            cols = slice(turn * HEAD, (turn + 1) * HEAD)
            scores = dot(k_ref[:, both][:, cols], q_ref[lanes, both][:, cols], NT)
            probs = weights_of(scores, mask_ref[:, lanes], careful)
            mixed = dot(v_ref[2 * pair + turn], probs)
            rows = pl.ds(pl.multiple_of((2 * pair + turn) * HEAD, HEAD), HEAD)
            ctx_ref[rows, lanes] = (mixed[0:HEAD] / mixed[HEAD : HEAD + 1]).astype(BF16)

        def step(group, carry):
            for pair in range(together):
                for turn in range(2):
                    for i in range(SEQ // tile):
                        one(group * together + pair, turn, i * tile)
            return carry

        lax.fori_loop(0, heads // 2 // together, step, 0)

    pl.when(safe)(lambda: attend(False, TILE, PAIRS))
    pl.when(jnp.logical_not(safe))(lambda: attend(True, TILE, 1))

    @pl.when(starting)
    def _():
        for copy in copies[3:6]:
            copy.wait()

    chunk = 1024
    hidden = we_ref.shape[1]
    piece = 768

    def feed_forward(part, carry):
        rows = pl.ds(pl.multiple_of(part * chunk, chunk), chunk)
        middle = x_ref[rows].astype(F32) + dot(ctx_ref[:, rows], wo_ref[...], TN)
        scale = lax.rsqrt(jnp.mean(middle * middle, axis=-1, keepdims=True) + EPS)
        normed = (middle * scale * middle_ref[...][None]).astype(BF16)
        total = middle
        for j in range(hidden // piece):
            cols = slice(j * piece, (j + 1) * piece)
            expanded = gelu(dot(normed, we_ref[:, cols])).astype(BF16)
            total = total + dot(expanded, wr_ref[cols])
        top = total.astype(BF16)
        top_ref[rows] = top
        tap_ref[:, rows] = dot(tap_t_ref[...], top, NT).astype(BF16)
        return carry

    lax.fori_loop(0, SEQ // chunk, feed_forward, 0)


def whole(array):
    shape = array.shape
    return pl.BlockSpec(shape, lambda i: (0,) * len(shape), pipeline_mode=pl.Buffered(1))


def frozen_block(segment, x, before, middle, wq, wk, wv, wo, we, wr, tap_t):
    tokens, width = x.shape
    heads = width // HEAD
    side = tap_t.shape[0]
    return pl.pallas_call(
        frozen_kernel,
        grid=(tokens // SEQ,),
        in_specs=[
            whole(segment),
            pl.BlockSpec((SEQ, width), lambda i: (i, 0)),
            *map(whole, (before, middle, tap_t)),
            *[pl.BlockSpec(memory_space=pl.ANY)] * 6,
        ],
        out_specs=[
            pl.BlockSpec((SEQ, width), lambda i: (i, 0)),
            pl.BlockSpec((side, SEQ), lambda i: (0, i)),
        ],
        out_shape=[
            jax.ShapeDtypeStruct((tokens, width), BF16),
            jax.ShapeDtypeStruct((side, tokens), BF16),
        ],
        scratch_shapes=[
            *[pltpu.VMEM(w.shape, BF16) for w in (wq, wk, wv, wo, we, wr)],
            pltpu.SemaphoreType.DMA((6,)),
            pltpu.VMEM((SEQ, SEQ), BF16),
            pltpu.VMEM((SEQ, width), BF16),
            pltpu.VMEM((SEQ, width), BF16),
            pltpu.VMEM((SEQ, width), BF16),
            pltpu.VMEM((heads, HEAD + 16, SEQ), BF16),
            pltpu.VMEM((width, SEQ), BF16),
            pltpu.VMEM((width, width), BF16),
        ],
        compiler_params=pltpu.CompilerParams(vmem_limit_bytes=60 << 20),
        name="frozen_block",
    )(segment, x, before, middle, tap_t, wq, wk, wv, wo, we, wr)


def outer_rows(left, right):
    return [left[e : e + 1] * right for e in range(SIDE_HEAD)]


def pack_kernel(expand_ref, q_ref, k_ref, v_ref, output_ref, reduce_ref, packed_ref):
    side, half = expand_ref.shape
    packed_ref[0:side] = expand_ref[:, 0:side]
    packed_ref[side : 2 * side] = expand_ref[:, side:half]
    at = half
    for ref in (q_ref, k_ref, v_ref, output_ref, reduce_ref):
        packed_ref[at : at + ref.shape[0]] = ref[...]
        at += ref.shape[0]


def side_kernel(
    index_ref,
    segment_ref,
    tap_ref,
    stream_ref,
    up_ref,
    top_ref,
    table_ref,
    before_ref,
    middle_ref,
    own_ref,
    other_ref,
    out_ref,
    stream_grad_ref,
    keep_ref,
    send_ref,
    tap_grad_ref,
    qkv_grad_ref,
    out_grad_ref,
    expand_grad_ref,
    reduce_grad_ref,
    small_ref,
    bundle_ref,
    mask_ref,
    w_ref,
    we_ref,
    wo_ref,
    wr_ref,
    e_ref,
    qkv_ref,
    q16_ref,
    k16_ref,
    rows_ref,
    moment_ref,
    ctx_ref,
    dctx_ref,
    dqkv_ref,
):
    side = tap_ref.shape[0]
    heads = side // SIDE_HEAD
    local = side // 2
    hidden = we_ref.shape[1]
    half = hidden // 2

    @pl.when(pl.program_id(0) == 0)
    def _():
        for turn, ref in ((0, own_ref), (1, other_ref)):
            we_ref[:, turn * half : turn * half + side] = ref[0:side]
            we_ref[:, turn * half + side : (turn + 1) * half] = ref[side:half]
            at = half
            w_ref[turn * 3 * local : (turn + 1) * 3 * local] = ref[at : at + 3 * local]
            at += 3 * local
            wo_ref[turn * local : (turn + 1) * local] = ref[at : at + local]
            at += local
            wr_ref[turn * half : (turn + 1) * half] = ref[at : at + half]
        tap_grad_ref[...] = jnp.zeros_like(tap_grad_ref)
        qkv_grad_ref[...] = jnp.zeros_like(qkv_grad_ref)
        out_grad_ref[...] = jnp.zeros_like(out_grad_ref)
        expand_grad_ref[...] = jnp.zeros_like(expand_grad_ref)
        reduce_grad_ref[...] = jnp.zeros_like(reduce_grad_ref)
        small_ref[...] = jnp.zeros_like(small_ref)

    here = lax.axis_index("side") * pl.num_programs(0) + pl.program_id(0)
    fill_mask(segment_ref[here], mask_ref)
    logits = table_ref[pl.ds(index_ref[0], 1), :]
    stacked = jnp.concatenate(
        [
            jnp.broadcast_to(jax.nn.sigmoid(logits), (8, side)),
            jnp.broadcast_to(before_ref[...], (8, side)),
            jnp.broadcast_to(middle_ref[...], (8, side)),
        ],
        axis=0,
    )
    columns = jnp.transpose(stacked)
    gate, before, middle = columns[:, 0:1], columns[:, 8:9], columns[:, 16:17]

    def head_rows(kind, head):
        start = (head // (heads // 2)) * 3 * local + kind * local + (head % (heads // 2)) * SIDE_HEAD
        return pl.ds(pl.multiple_of(start, SIDE_HEAD), SIDE_HEAD)

    tap = tap_ref[...].astype(F32)
    stream = stream_ref[...].astype(F32)
    mixed = gate * tap + (1.0 - gate) * stream
    factor1 = lax.rsqrt(jnp.mean(mixed * mixed, axis=0, keepdims=True) + EPS)
    n1 = (mixed * factor1 * before).astype(BF16)
    qkv_ref[...] = dot(w_ref[...], n1)

    zeros8 = jnp.zeros((SIDE_HEAD, SEQ), F32)
    ones8 = jnp.ones((SIDE_HEAD, SEQ), F32)

    def prepare(head, bound):
        q = qkv_ref[head_rows(0, head)] * (SIDE_HEAD**-0.5 * LOG2E)
        q = q.astype(BF16).astype(F32)
        k = qkv_ref[head_rows(1, head)].astype(BF16).astype(F32)
        v = qkv_ref[head_rows(2, head)].astype(BF16).astype(F32)
        qkv_ref[head_rows(0, head)] = q
        qkv_ref[head_rows(1, head)] = k
        qkv_ref[head_rows(2, head)] = v
        q16_ref[head] = jnp.concatenate([q, zeros8], axis=0).astype(BF16)
        k16_ref[head] = jnp.concatenate([k, zeros8], axis=0).astype(BF16)
        rows = [v, ones8, k, zeros8] + outer_rows(v, k)
        rows_ref[head] = jnp.concatenate(rows, axis=0).astype(BF16)
        return jnp.maximum(
            bound,
            jnp.max(jnp.sum(q * q, axis=0, keepdims=True), axis=1, keepdims=True)
            * jnp.max(jnp.sum(k * k, axis=0, keepdims=True), axis=1, keepdims=True),
        )

    bound = lax.fori_loop(0, heads, prepare, jnp.zeros((1, 1), F32))
    safe = jnp.max(bound) * 1.1 <= SAFE * SAFE

    def attend(careful, tile):
        def one(head, start):
            at = pl.multiple_of(head * SIDE_HEAD, SIDE_HEAD)
            lanes = pl.ds(start, tile)
            scores = dot(k16_ref[head], q16_ref[head, :, lanes], TN)
            probs = weights_of(scores, mask_ref[:, lanes], careful)
            e_ref[head, :, lanes] = probs
            found = dot(rows_ref[head], probs)
            inverse = 1.0 / found[8:16]
            ctx_ref[pl.ds(at, SIDE_HEAD), lanes] = found[0:8] * inverse
            moment_ref[head, 8:16, lanes] = inverse
            moment_ref[head, 16:24, lanes] = found[16:24] * inverse
            for e in range(SIDE_HEAD):
                low = 32 + e * SIDE_HEAD
                moment_ref[head, low : low + 8, lanes] = found[low : low + 8] * inverse

        together = 1 if careful else GROUP

        def step(group, carry):
            for turn in range(together):
                for i in range(SEQ // tile):
                    one(group * together + turn, i * tile)
            return carry

        lax.fori_loop(0, heads // together, step, 0)

    pl.when(safe)(lambda: attend(False, TILE))
    pl.when(jnp.logical_not(safe))(lambda: attend(True, TILE))

    ctx = ctx_ref[...].astype(BF16)
    res1 = mixed + dot(wo_ref[...], ctx, TN)
    factor2 = lax.rsqrt(jnp.mean(res1 * res1, axis=0, keepdims=True) + EPS)
    z = res1 * factor2
    n2 = (z * middle).astype(BF16)
    pre = dot(we_ref[...], n2, TN)
    act, slope = gelu_both(pre)
    act = act.astype(BF16)
    result = res1 + dot(wr_ref[...], act, TN)
    out_ref[...] = result.astype(BF16)

    low_up = up_ref[...]
    up = low_up.astype(F32)
    reduce_grad_ref[...] += dot(low_up, act, NT)
    dpre = (dot(wr_ref[...], low_up) * slope).astype(BF16)
    expand_grad_ref[...] += dot(n2, dpre, NT)
    dn2 = dot(we_ref[...], dpre)
    middle_grad = jnp.sum(dn2 * z, axis=1, keepdims=True)
    u = dn2 * middle
    spread = jnp.mean(u * res1, axis=0, keepdims=True)
    dres1 = up + factor2 * u - z * (factor2 * factor2 * spread)
    low_dres = dres1.astype(BF16)
    out_grad_ref[...] += dot(low_dres, ctx, NT)
    dctx_ref[...] = dot(wo_ref[...], low_dres).astype(BF16).astype(F32)

    def prepare_back(head, carry):
        at = pl.multiple_of(head * SIDE_HEAD, SIDE_HEAD)
        q = qkv_ref[head_rows(0, head)]
        dctx = dctx_ref[pl.ds(at, SIDE_HEAD)]
        inverse = moment_ref[head, 8:16]
        inner = jnp.sum(dctx * ctx_ref[pl.ds(at, SIDE_HEAD)], axis=0, keepdims=True)
        dq = -inner * moment_ref[head, 16:24]
        for e in range(SIDE_HEAD):
            low = 32 + e * SIDE_HEAD
            dq = dq + dctx[e : e + 1] * moment_ref[head, low : low + 8]
        dqkv_ref[head_rows(0, head)] = dq * SIDE_HEAD**-0.5
        scaled = dctx * inverse
        rows = [scaled, zeros8, (inner * inverse) * q, zeros8] + outer_rows(scaled, q)
        rows_ref[head] = jnp.concatenate(rows, axis=0).astype(BF16)
        return carry

    lax.fori_loop(0, heads, prepare_back, 0)

    def back(head):
        found = dot(rows_ref[head], e_ref[head], NT)
        v = qkv_ref[head_rows(2, head)]
        dk = -found[16:24]
        for e in range(SIDE_HEAD):
            low = 32 + e * SIDE_HEAD
            dk = dk + v[e : e + 1] * found[low : low + 8]
        dqkv_ref[head_rows(1, head)] = dk * (1.0 / LOG2E)
        dqkv_ref[head_rows(2, head)] = found[0:8]

    def back_group(group, carry):
        for turn in range(GROUP):
            back(group * GROUP + turn)
        return carry

    lax.fori_loop(0, heads // GROUP, back_group, 0)

    dqkv = dqkv_ref[...].astype(BF16)
    qkv_grad_ref[...] += dot(n1, dqkv, NT)
    dn1 = dot(w_ref[...], dqkv, TN)
    unit = mixed * factor1
    before_grad = jnp.sum(dn1 * unit, axis=1, keepdims=True)
    u = dn1 * before
    spread = jnp.mean(u * mixed, axis=0, keepdims=True)
    dmixed = dres1 + factor1 * u - unit * (factor1 * factor1 * spread)
    logit = jnp.sum(dmixed * (tap - stream), axis=1, keepdims=True) * gate * (1.0 - gate)
    small_ref[...] += jnp.concatenate(
        [logit, before_grad, middle_grad, jnp.zeros((side, 5), F32)], axis=1
    )
    tap_grad_ref[...] += dot((gate * dmixed).astype(BF16), top_ref[...])
    stream_grad_ref[...] = ((1.0 - gate) * dmixed).astype(BF16)

    @pl.when(pl.program_id(0) == pl.num_programs(0) - 1)
    def _():
        for turn in range(2):
            bundle_ref[turn] = jnp.concatenate(
                [
                    expand_grad_ref[:, turn * half : (turn + 1) * half],
                    reduce_grad_ref[:, turn * half : (turn + 1) * half],
                    qkv_grad_ref[:, turn * 3 * local : (turn + 1) * 3 * local],
                    out_grad_ref[:, turn * local : (turn + 1) * local],
                    small_ref[...],
                    jnp.zeros((side, bundle_ref.shape[2] - 2 * half - 4 * local - 8), F32),
                ],
                axis=1,
            )
        place = lax.axis_index("dp")
        me = (place % 2, (place // 2) % 2, lax.axis_index("side"))
        fourth = side // 4
        width = tap_grad_ref.shape[1]
        for core in range(2):
            for x in range(2):
                part = 2 * (me[0] ^ core) + (me[1] ^ x)
                lines = pl.ds(pl.multiple_of(part * fourth, 8), fourth)
                for turn in range(2):
                    first = (me[2] ^ turn) * (width // 2)
                    pieces = [
                        tap_grad_ref[lines, pl.ds(pl.multiple_of(first + j * 128, 128), 128)]
                        for j in range(width // 256)
                    ] + [
                        bundle_ref[turn, lines, j * 128 : (j + 1) * 128]
                        for j in range(bundle_ref.shape[2] // 128)
                    ]
                    block = jnp.concatenate(pieces, axis=0).astype(BF16)
                    (send_ref if core else keep_ref)[2 * x + turn] = block


def side_block(index, segment, tap, stream, up, top, table, before, middle, own, other):
    side, tokens = stream.shape
    width = top.shape[1]
    heads = side // SIDE_HEAD
    hidden = own.shape[0] - 2 * side
    bundle = -(-(hidden + 2 * side + 8) // 128) * 128
    block = (side // 4) * (width // 256 + bundle // 128)

    def lanes(height):
        return pl.BlockSpec((height, SEQ), lambda i: (0, i))

    packed = pl.BlockSpec((4, block, 128), lambda i: (0, 0, 0))
    return pl.pallas_call(
        side_kernel,
        grid=(tokens // SEQ,),
        in_specs=[
            pl.BlockSpec(memory_space=pltpu.SMEM),
            whole(segment),
            lanes(side),
            lanes(side),
            lanes(side),
            pl.BlockSpec((SEQ, width), lambda i: (i, 0)),
            *map(whole, (table, before, middle, own, other)),
        ],
        out_specs=[lanes(side), lanes(side), packed, packed],
        out_shape=[
            jax.ShapeDtypeStruct((side, tokens), BF16),
            jax.ShapeDtypeStruct((side, tokens), BF16),
            jax.ShapeDtypeStruct((4, block, 128), BF16),
            jax.ShapeDtypeStruct((4, block, 128), BF16),
        ],
        scratch_shapes=[
            pltpu.VMEM((side, width), F32),
            pltpu.VMEM((side, 3 * side), F32),
            pltpu.VMEM((side, side), F32),
            pltpu.VMEM((side, hidden), F32),
            pltpu.VMEM((side, hidden), F32),
            pltpu.VMEM((side, 8), F32),
            pltpu.VMEM((2, side, bundle), F32),
            pltpu.VMEM((SEQ, SEQ), BF16),
            pltpu.VMEM((3 * side, side), BF16),
            pltpu.VMEM((side, hidden), BF16),
            pltpu.VMEM((side, side), BF16),
            pltpu.VMEM((hidden, side), BF16),
            pltpu.VMEM((heads, SEQ, SEQ), BF16),
            pltpu.VMEM((3 * side, SEQ), F32),
            pltpu.VMEM((heads, 16, SEQ), BF16),
            pltpu.VMEM((heads, 16, SEQ), BF16),
            pltpu.VMEM((heads, ROWS, SEQ), BF16),
            pltpu.VMEM((heads, ROWS, SEQ), F32),
            pltpu.VMEM((side, SEQ), F32),
            pltpu.VMEM((side, SEQ), F32),
            pltpu.VMEM((3 * side, SEQ), F32),
        ],
        compiler_params=pltpu.CompilerParams(vmem_limit_bytes=60 << 20),
        name="side_block",
    )(index, segment, tap, stream, up, top, table, before, middle, own, other)


def unpack_kernel(
    index_ref,
    near_ref,
    far_ref,
    tap_ref,
    gate_ref,
    before_ref,
    middle_ref,
    q_ref,
    k_ref,
    v_ref,
    output_ref,
    expand_ref,
    reduce_ref,
    bundle_ref,
):
    side, width = tap_ref.shape
    half = expand_ref.shape[1]
    local = side // 2
    fourth = side // 4
    taps = width // 256
    tiles = bundle_ref.shape[1] // 128
    block = fourth * (taps + tiles)
    place = lax.axis_index("dp")
    me = (place % 2, (place // 2) % 2, lax.axis_index("side"))
    for core in range(2):
        held = (far_ref if core else near_ref)[...].astype(F32)
        for x in range(2):
            part = 2 * (me[0] ^ core) + (me[1] ^ x)
            lines = pl.ds(pl.multiple_of(part * fourth, 8), fourth)
            for turn in range(2):
                at = 2 * block + x * taps * fourth if turn else x * block
                first = (me[2] ^ turn) * (width // 2)
                for j in range(taps):
                    cols = pl.ds(pl.multiple_of(first + j * 128, 128), 128)
                    tap_ref[lines, cols] = held[at + j * fourth : at + (j + 1) * fourth]
            for j in range(tiles):
                at = x * block + (taps + j) * fourth
                bundle_ref[lines, j * 128 : (j + 1) * 128] = held[at : at + fourth]
    expand_ref[...] = bundle_ref[:, 0:half]
    reduce_ref[...] = jnp.transpose(bundle_ref[:, half : 2 * half])
    rest = jnp.transpose(bundle_ref[:, 2 * half : 2 * half + 4 * local + 8])
    q_ref[...] = rest[0:local]
    k_ref[...] = rest[local : 2 * local]
    v_ref[...] = rest[2 * local : 3 * local]
    output_ref[...] = rest[3 * local : 4 * local]
    small = rest[4 * local : 4 * local + 8]
    picked = lax.broadcasted_iota(jnp.int32, gate_ref.shape, 0) == index_ref[0]
    gate_ref[...] = jnp.where(picked, small[0:1], 0.0)
    before_ref[...] = small[1:2]
    middle_ref[...] = small[2:3]


def exchange(values, dp, side, dp_size):
    pairs = [
        (2 * i + s, 2 * (i ^ dp) + (s ^ side)) for i in range(dp_size) for s in range(2)
    ]
    return lax.ppermute(values, ("dp", "side"), pairs)


def add(*values):
    return functools.reduce(lambda a, b: a + b, [v.astype(F32) for v in values]).astype(BF16)


def shards(
    dp_size,
    backbone_in,
    segment_ids,
    gate_index,
    norm_before,
    norm_middle,
    frozen_query,
    frozen_key,
    frozen_value,
    frozen_output,
    frozen_expand,
    frozen_reduce,
    tap_weight,
    gate_table,
    side_stream,
    ladder_before,
    ladder_middle,
    ladder_query,
    ladder_key,
    ladder_value,
    ladder_output,
    ladder_expand,
    ladder_reduce,
    cotangent,
):
    side = side_stream.shape[1]
    width = tap_weight.shape[0]
    local = side // 2
    half = ladder_expand.shape[1]
    swap = functools.partial(exchange, dp_size=dp_size)
    own = pl.pallas_call(
        pack_kernel,
        out_shape=jax.ShapeDtypeStruct((2 * half + 4 * local, side), BF16),
        name="pack_weights",
    )(ladder_expand, ladder_query.T, ladder_key.T, ladder_value.T, ladder_output, ladder_reduce)
    other = swap(own, 0, 1)
    segment = segment_ids.reshape(-1, 1, SEQ)
    top, tap = frozen_block(
        segment,
        backbone_in,
        norm_before,
        norm_middle,
        frozen_query,
        frozen_key,
        frozen_value,
        frozen_output,
        frozen_expand,
        frozen_reduce,
        tap_weight.T,
    )
    result, stream_grad, keep, send = side_block(
        gate_index,
        segment,
        tap,
        side_stream.T,
        cotangent.T,
        top,
        gate_table,
        ladder_before[None],
        ladder_middle[None],
        own,
        other,
    )
    block = keep.shape[1]
    taps = (side // 4) * (width // 256)
    quad = add(keep, swap(send, 1, 0))
    mine = add(quad[0], swap(quad[1], 0, 1), swap(quad[2], 2, 0), swap(quad[3], 2, 1))
    bit = 4
    while bit < dp_size:
        mine = add(mine, swap(mine, bit, 0))
        bit *= 2
    near = jnp.concatenate(
        [mine, swap(mine, 2, 0), swap(mine[:taps], 0, 1), swap(mine[:taps], 2, 1)], axis=0
    )
    far = swap(near, 1, 0)
    shape = functools.partial(jax.ShapeDtypeStruct, dtype=F32)
    tap_sum, gate_sum, before_sum, middle_sum, q_sum, k_sum, v_sum, out_sum, expand_sum, reduce_sum = pl.pallas_call(
        unpack_kernel,
        in_specs=[
            pl.BlockSpec(memory_space=pltpu.SMEM),
            pl.BlockSpec(memory_space=pltpu.VMEM),
            pl.BlockSpec(memory_space=pltpu.VMEM),
        ],
        out_shape=[
            shape((side, width)),
            shape(gate_table.shape),
            shape((1, side)),
            shape((1, side)),
            shape((local, side)),
            shape((local, side)),
            shape((local, side)),
            shape((local, side)),
            shape((side, half)),
            shape((half, side)),
        ],
        scratch_shapes=[pltpu.VMEM((side, (block - taps) // (side // 4) * 128), F32)],
        compiler_params=pltpu.CompilerParams(vmem_limit_bytes=8 << 20),
        name="unpack_gradients",
    )(gate_index, near, far)
    return (
        result.T,
        stream_grad.T,
        tap_sum.T,
        gate_sum,
        before_sum[0],
        middle_sum[0],
        q_sum.T,
        k_sum.T,
        v_sum.T,
        out_sum,
        expand_sum,
        reduce_sum,
    )


def solution(mesh):
    rows = P(("dp", "side"), None)
    placed = (
        rows,
        P("dp"),
        *([P()] * 11),
        rows,
        P(),
        P(),
        P(None, "side"),
        P(None, "side"),
        P(None, "side"),
        P("side", None),
        P(None, "side"),
        P("side", None),
        rows,
    )
    return jax.shard_map(
        functools.partial(shards, mesh.shape["dp"]),
        mesh=mesh,
        in_specs=placed,
        out_specs=(
            rows,
            rows,
            P(),
            P(),
            P(),
            P(),
            P(None, "side"),
            P(None, "side"),
            P(None, "side"),
            P("side", None),
            P(None, "side"),
            P("side", None),
        ),
        check_vma=False,
    )
```

```python
import functools

import jax
import jax.numpy as jnp
from jax import lax
from jax.experimental import pallas as pl
from jax.experimental.pallas import tpu as pltpu
from jax.sharding import PartitionSpec as P

HEAD = 64
SIDE_HEAD = 8
SEQ = 1024
EPS = 1e-06
MASKED = -1e30
LOG2E = 1.4426950408889634
LEAST = 2.0**-64
MOST = 2.0**64
TILE = 512
ROWS = 96
GROUP = 4
PAIRS = 2

F32 = jnp.float32
BF16 = jnp.bfloat16
NN = (((1,), (0,)), ((), ()))
NT = (((1,), (1,)), ((), ()))
TN = (((0,), (0,)), ((), ()))


def dot(left, right, dims=NN):
    return lax.dot_general(left, right, dims, preferred_element_type=F32)


def gelu_inner(values):
    return 0.7978845608028654 * values * (1.0 + 0.044715 * values * values)


def gelu(values):
    return 0.5 * values * (1.0 + jnp.tanh(gelu_inner(values)))


def gelu_both(values):
    square = values * values
    bend = jnp.tanh(0.7978845608028654 * values * (1.0 + 0.044715 * square))
    half = 0.5 * (1.0 + bend)
    slope = 0.7978845608028654 * (1.0 + 3.0 * 0.044715 * square)
    return values * half, half + 0.5 * values * (1.0 - bend * bend) * slope


def fill_mask(row, mask_ref):
    row = row.astype(F32)
    column = jnp.transpose(jnp.broadcast_to(row, (8, SEQ)))[:, 0:1]
    for step in range(SEQ // 128):
        lanes = slice(step * 128, (step + 1) * 128)
        mask_ref[:, lanes] = jnp.where(column == row[:, lanes], 1.0, 0.0).astype(BF16)


def note_totals(fine_ref, totals):
    fine = jnp.logical_and(totals >= LEAST, totals <= MOST)
    fine_ref[...] = jnp.where(fine, fine_ref[...], 0.0)


def weights_of(scores, mask, careful):
    if not careful:
        return jnp.exp2(scores).astype(BF16) * mask
    allowed = mask.astype(F32) > 0.5
    scores = jnp.where(allowed, scores, MASKED)
    highest = jnp.max(scores, axis=0, keepdims=True)
    return jnp.exp2(scores - highest).astype(BF16)


def frozen_kernel(
    segment_ref,
    x_ref,
    before_ref,
    middle_ref,
    tap_t_ref,
    wq_hbm,
    wk_hbm,
    wv_hbm,
    wo_hbm,
    we_hbm,
    wr_hbm,
    top_ref,
    tap_ref,
    wq_ref,
    wk_ref,
    wv_ref,
    wo_ref,
    we_ref,
    wr_ref,
    copied,
    mask_ref,
    normed_ref,
    q_ref,
    k_ref,
    v_ref,
    ctx_ref,
    wv_t_ref,
    fine_ref,
):
    width = x_ref.shape[1]
    heads = width // HEAD
    padded = v_ref.shape[1]

    starting = pl.program_id(0) == 0
    copies = [
        pltpu.make_async_copy(source, target, copied.at[i])
        for i, (source, target) in enumerate(
            (
                (wq_hbm, wq_ref),
                (wk_hbm, wk_ref),
                (wv_hbm, wv_ref),
                (wo_hbm, wo_ref),
                (we_hbm, we_ref),
                (wr_hbm, wr_ref),
            )
        )
    ]

    @pl.when(starting)
    def _():
        for copy in copies[0:3]:
            copy.start()
        v_ref[:, HEAD:padded] = jnp.ones((heads, padded - HEAD, SEQ), BF16)

    here = lax.axis_index("side") * pl.num_programs(0) + pl.program_id(0)
    fill_mask(segment_ref[here], mask_ref)
    base = x_ref[...].astype(F32)
    factor = lax.rsqrt(jnp.mean(base * base, axis=-1, keepdims=True) + EPS)
    normed_ref[...] = (base * factor * before_ref[...][None]).astype(BF16)
    @pl.when(starting)
    def _():
        for copy in copies[0:3]:
            copy.wait()
        for copy in copies[3:6]:
            copy.start()
        wv_t_ref[...] = jnp.transpose(wv_ref[...])

    q_ref[...] = (dot(normed_ref[...], wq_ref[...]) * (HEAD**-0.5 * LOG2E)).astype(BF16)
    k_ref[...] = dot(normed_ref[...], wk_ref[...]).astype(BF16)
    v = dot(wv_t_ref[...], normed_ref[...], NT).astype(BF16)
    for head in range(heads):
        v_ref[head, 0:HEAD] = v[head * HEAD : (head + 1) * HEAD]

    def attend(careful, tile, together):
        def one(pair, turn, start):
            lanes = pl.ds(start, tile)
            both = pl.ds(pl.multiple_of(pair * 2 * HEAD, 2 * HEAD), 2 * HEAD)
            cols = slice(turn * HEAD, (turn + 1) * HEAD)
            scores = dot(k_ref[:, both][:, cols], q_ref[lanes, both][:, cols], NT)
            probs = weights_of(scores, mask_ref[:, lanes], careful)
            mixed = dot(v_ref[2 * pair + turn], probs)
            if not careful:
                note_totals(fine_ref, mixed[HEAD : HEAD + 8])
            rows = pl.ds(pl.multiple_of((2 * pair + turn) * HEAD, HEAD), HEAD)
            ctx_ref[rows, lanes] = (mixed[0:HEAD] / mixed[HEAD : HEAD + 1]).astype(BF16)

        def step(group, carry):
            for pair in range(together):
                for turn in range(2):
                    for i in range(SEQ // tile):
                        one(group * together + pair, turn, i * tile)
            return carry

        lax.fori_loop(0, heads // 2 // together, step, 0)

    fine_ref[...] = jnp.ones_like(fine_ref)
    attend(False, TILE, PAIRS)
    pl.when(jnp.min(fine_ref[...]) < 0.5)(lambda: attend(True, TILE, 1))

    @pl.when(starting)
    def _():
        for copy in copies[3:6]:
            copy.wait()

    chunk = 1024
    hidden = we_ref.shape[1]
    piece = 768

    def feed_forward(part, carry):
        rows = pl.ds(pl.multiple_of(part * chunk, chunk), chunk)
        middle = x_ref[rows].astype(F32) + dot(ctx_ref[:, rows], wo_ref[...], TN)
        scale = lax.rsqrt(jnp.mean(middle * middle, axis=-1, keepdims=True) + EPS)
        normed = (middle * scale * middle_ref[...][None]).astype(BF16)
        total = middle
        for j in range(hidden // piece):
            cols = slice(j * piece, (j + 1) * piece)
            expanded = gelu(dot(normed, we_ref[:, cols])).astype(BF16)
            total = total + dot(expanded, wr_ref[cols])
        top = total.astype(BF16)
        top_ref[rows] = top
        tap_ref[:, rows] = dot(tap_t_ref[...], top, NT).astype(BF16)
        return carry

    lax.fori_loop(0, SEQ // chunk, feed_forward, 0)


def whole(array):
    shape = array.shape
    return pl.BlockSpec(shape, lambda i: (0,) * len(shape), pipeline_mode=pl.Buffered(1))


def frozen_block(segment, x, before, middle, wq, wk, wv, wo, we, wr, tap_t):
    tokens, width = x.shape
    heads = width // HEAD
    side = tap_t.shape[0]
    return pl.pallas_call(
        frozen_kernel,
        grid=(tokens // SEQ,),
        in_specs=[
            whole(segment),
            pl.BlockSpec((SEQ, width), lambda i: (i, 0)),
            *map(whole, (before, middle, tap_t)),
            *[pl.BlockSpec(memory_space=pl.ANY)] * 6,
        ],
        out_specs=[
            pl.BlockSpec((SEQ, width), lambda i: (i, 0)),
            pl.BlockSpec((side, SEQ), lambda i: (0, i)),
        ],
        out_shape=[
            jax.ShapeDtypeStruct((tokens, width), BF16),
            jax.ShapeDtypeStruct((side, tokens), BF16),
        ],
        scratch_shapes=[
            *[pltpu.VMEM(w.shape, BF16) for w in (wq, wk, wv, wo, we, wr)],
            pltpu.SemaphoreType.DMA((6,)),
            pltpu.VMEM((SEQ, SEQ), BF16),
            pltpu.VMEM((SEQ, width), BF16),
            pltpu.VMEM((SEQ, width), BF16),
            pltpu.VMEM((SEQ, width), BF16),
            pltpu.VMEM((heads, HEAD + 16, SEQ), BF16),
            pltpu.VMEM((width, SEQ), BF16),
            pltpu.VMEM((width, width), BF16),
            pltpu.VMEM((8, TILE), F32),
        ],
        compiler_params=pltpu.CompilerParams(vmem_limit_bytes=60 << 20),
        name="frozen_block",
    )(segment, x, before, middle, tap_t, wq, wk, wv, wo, we, wr)


def outer_rows(left, right):
    return [left[e : e + 1] * right for e in range(SIDE_HEAD)]


def pack_kernel(expand_ref, q_ref, k_ref, v_ref, output_ref, reduce_ref, packed_ref):
    side, half = expand_ref.shape
    packed_ref[0:side] = expand_ref[:, 0:side]
    packed_ref[side : 2 * side] = expand_ref[:, side:half]
    at = half
    for ref in (q_ref, k_ref, v_ref, output_ref, reduce_ref):
        packed_ref[at : at + ref.shape[0]] = ref[...]
        at += ref.shape[0]


def side_kernel(
    index_ref,
    segment_ref,
    tap_ref,
    stream_ref,
    up_ref,
    top_ref,
    table_ref,
    before_ref,
    middle_ref,
    own_ref,
    other_ref,
    out_ref,
    stream_grad_ref,
    keep_ref,
    send_ref,
    tap_grad_ref,
    qkv_grad_ref,
    out_grad_ref,
    expand_grad_ref,
    reduce_grad_ref,
    small_ref,
    bundle_ref,
    mask_ref,
    w_ref,
    we_ref,
    wo_ref,
    wr_ref,
    e_ref,
    qkv_ref,
    q16_ref,
    k16_ref,
    rows_ref,
    moment_ref,
    ctx_ref,
    dctx_ref,
    dqkv_ref,
    fine_ref,
):
    side = tap_ref.shape[0]
    heads = side // SIDE_HEAD
    local = side // 2
    hidden = we_ref.shape[1]
    half = hidden // 2

    @pl.when(pl.program_id(0) == 0)
    def _():
        for turn, ref in ((0, own_ref), (1, other_ref)):
            we_ref[:, turn * half : turn * half + side] = ref[0:side]
            we_ref[:, turn * half + side : (turn + 1) * half] = ref[side:half]
            at = half
            w_ref[turn * 3 * local : (turn + 1) * 3 * local] = ref[at : at + 3 * local]
            at += 3 * local
            wo_ref[turn * local : (turn + 1) * local] = ref[at : at + local]
            at += local
            wr_ref[turn * half : (turn + 1) * half] = ref[at : at + half]
        tap_grad_ref[...] = jnp.zeros_like(tap_grad_ref)
        qkv_grad_ref[...] = jnp.zeros_like(qkv_grad_ref)
        out_grad_ref[...] = jnp.zeros_like(out_grad_ref)
        expand_grad_ref[...] = jnp.zeros_like(expand_grad_ref)
        reduce_grad_ref[...] = jnp.zeros_like(reduce_grad_ref)
        small_ref[...] = jnp.zeros_like(small_ref)

    here = lax.axis_index("side") * pl.num_programs(0) + pl.program_id(0)
    fill_mask(segment_ref[here], mask_ref)
    logits = table_ref[pl.ds(index_ref[0], 1), :]
    stacked = jnp.concatenate(
        [
            jnp.broadcast_to(jax.nn.sigmoid(logits), (8, side)),
            jnp.broadcast_to(before_ref[...], (8, side)),
            jnp.broadcast_to(middle_ref[...], (8, side)),
        ],
        axis=0,
    )
    columns = jnp.transpose(stacked)
    gate, before, middle = columns[:, 0:1], columns[:, 8:9], columns[:, 16:17]

    def head_rows(kind, head):
        start = (head // (heads // 2)) * 3 * local + kind * local + (head % (heads // 2)) * SIDE_HEAD
        return pl.ds(pl.multiple_of(start, SIDE_HEAD), SIDE_HEAD)

    tap = tap_ref[...].astype(F32)
    stream = stream_ref[...].astype(F32)
    mixed = gate * tap + (1.0 - gate) * stream
    factor1 = lax.rsqrt(jnp.mean(mixed * mixed, axis=0, keepdims=True) + EPS)
    n1 = (mixed * factor1 * before).astype(BF16)
    qkv_ref[...] = dot(w_ref[...], n1)

    zeros8 = jnp.zeros((SIDE_HEAD, SEQ), F32)
    ones8 = jnp.ones((SIDE_HEAD, SEQ), F32)

    def prepare(head, carry):
        q = qkv_ref[head_rows(0, head)] * (SIDE_HEAD**-0.5 * LOG2E)
        q = q.astype(BF16).astype(F32)
        k = qkv_ref[head_rows(1, head)].astype(BF16).astype(F32)
        v = qkv_ref[head_rows(2, head)].astype(BF16).astype(F32)
        qkv_ref[head_rows(0, head)] = q
        qkv_ref[head_rows(1, head)] = k
        qkv_ref[head_rows(2, head)] = v
        q16_ref[head] = jnp.concatenate([q, zeros8], axis=0).astype(BF16)
        k16_ref[head] = jnp.concatenate([k, zeros8], axis=0).astype(BF16)
        rows = [v, ones8, k, zeros8] + outer_rows(v, k)
        rows_ref[head] = jnp.concatenate(rows, axis=0).astype(BF16)
        return carry

    lax.fori_loop(0, heads, prepare, 0)

    def attend(careful, tile):
        def one(head, start):
            at = pl.multiple_of(head * SIDE_HEAD, SIDE_HEAD)
            lanes = pl.ds(start, tile)
            scores = dot(k16_ref[head], q16_ref[head, :, lanes], TN)
            probs = weights_of(scores, mask_ref[:, lanes], careful)
            e_ref[head, lanes, :] = jnp.transpose(probs)
            found = dot(rows_ref[head], probs)
            if not careful:
                note_totals(fine_ref, found[8:16])
            inverse = 1.0 / found[8:16]
            ctx_ref[pl.ds(at, SIDE_HEAD), lanes] = found[0:8] * inverse
            moment_ref[head, 8:16, lanes] = inverse
            moment_ref[head, 16:24, lanes] = found[16:24] * inverse
            for e in range(SIDE_HEAD):
                low = 32 + e * SIDE_HEAD
                moment_ref[head, low : low + 8, lanes] = found[low : low + 8] * inverse

        together = 1 if careful else GROUP

        def step(group, carry):
            for turn in range(together):
                for i in range(SEQ // tile):
                    one(group * together + turn, i * tile)
            return carry

        lax.fori_loop(0, heads // together, step, 0)

    fine_ref[...] = jnp.ones_like(fine_ref)
    attend(False, TILE)
    pl.when(jnp.min(fine_ref[...]) < 0.5)(lambda: attend(True, TILE))

    ctx = ctx_ref[...].astype(BF16)
    res1 = mixed + dot(wo_ref[...], ctx, TN)
    factor2 = lax.rsqrt(jnp.mean(res1 * res1, axis=0, keepdims=True) + EPS)
    z = res1 * factor2
    n2 = (z * middle).astype(BF16)
    pre = dot(we_ref[...], n2, TN)
    act, slope = gelu_both(pre)
    act = act.astype(BF16)
    result = res1 + dot(wr_ref[...], act, TN)
    out_ref[...] = result.astype(BF16)

    low_up = up_ref[...]
    up = low_up.astype(F32)
    reduce_grad_ref[...] += dot(low_up, act, NT)
    dpre = (dot(wr_ref[...], low_up) * slope).astype(BF16)
    expand_grad_ref[...] += dot(n2, dpre, NT)
    dn2 = dot(we_ref[...], dpre)
    middle_grad = jnp.sum(dn2 * z, axis=1, keepdims=True)
    u = dn2 * middle
    spread = jnp.mean(u * res1, axis=0, keepdims=True)
    dres1 = up + factor2 * u - z * (factor2 * factor2 * spread)
    low_dres = dres1.astype(BF16)
    out_grad_ref[...] += dot(low_dres, ctx, NT)
    dctx_ref[...] = dot(wo_ref[...], low_dres).astype(BF16).astype(F32)

    def prepare_back(head, carry):
        at = pl.multiple_of(head * SIDE_HEAD, SIDE_HEAD)
        q = qkv_ref[head_rows(0, head)]
        dctx = dctx_ref[pl.ds(at, SIDE_HEAD)]
        inverse = moment_ref[head, 8:16]
        inner = jnp.sum(dctx * ctx_ref[pl.ds(at, SIDE_HEAD)], axis=0, keepdims=True)
        dq = -inner * moment_ref[head, 16:24]
        for e in range(SIDE_HEAD):
            low = 32 + e * SIDE_HEAD
            dq = dq + dctx[e : e + 1] * moment_ref[head, low : low + 8]
        dqkv_ref[head_rows(0, head)] = dq * SIDE_HEAD**-0.5
        scaled = dctx * inverse
        rows = [scaled, zeros8, (inner * inverse) * q, zeros8] + outer_rows(scaled, q)
        rows_ref[head] = jnp.concatenate(rows, axis=0).astype(BF16)
        return carry

    lax.fori_loop(0, heads, prepare_back, 0)

    def back(head):
        found = dot(rows_ref[head], e_ref[head])
        v = qkv_ref[head_rows(2, head)]
        dk = -found[16:24]
        for e in range(SIDE_HEAD):
            low = 32 + e * SIDE_HEAD
            dk = dk + v[e : e + 1] * found[low : low + 8]
        dqkv_ref[head_rows(1, head)] = dk * (1.0 / LOG2E)
        dqkv_ref[head_rows(2, head)] = found[0:8]

    def back_group(group, carry):
        for turn in range(GROUP):
            back(group * GROUP + turn)
        return carry

    lax.fori_loop(0, heads // GROUP, back_group, 0)

    dqkv = dqkv_ref[...].astype(BF16)
    qkv_grad_ref[...] += dot(n1, dqkv, NT)
    dn1 = dot(w_ref[...], dqkv, TN)
    unit = mixed * factor1
    before_grad = jnp.sum(dn1 * unit, axis=1, keepdims=True)
    u = dn1 * before
    spread = jnp.mean(u * mixed, axis=0, keepdims=True)
    dmixed = dres1 + factor1 * u - unit * (factor1 * factor1 * spread)
    logit = jnp.sum(dmixed * (tap - stream), axis=1, keepdims=True) * gate * (1.0 - gate)
    small_ref[...] += jnp.concatenate(
        [logit, before_grad, middle_grad, jnp.zeros((side, 5), F32)], axis=1
    )
    tap_grad_ref[...] += dot((gate * dmixed).astype(BF16), top_ref[...])
    stream_grad_ref[...] = ((1.0 - gate) * dmixed).astype(BF16)

    @pl.when(pl.program_id(0) == pl.num_programs(0) - 1)
    def _():
        for turn in range(2):
            bundle_ref[turn] = jnp.concatenate(
                [
                    expand_grad_ref[:, turn * half : (turn + 1) * half],
                    reduce_grad_ref[:, turn * half : (turn + 1) * half],
                    qkv_grad_ref[:, turn * 3 * local : (turn + 1) * 3 * local],
                    out_grad_ref[:, turn * local : (turn + 1) * local],
                    small_ref[...],
                    jnp.zeros((side, bundle_ref.shape[2] - 2 * half - 4 * local - 8), F32),
                ],
                axis=1,
            )
        place = lax.axis_index("dp")
        me = (place % 2, (place // 2) % 2, lax.axis_index("side"))
        fourth = side // 4
        width = tap_grad_ref.shape[1]
        for core in range(2):
            for x in range(2):
                part = 2 * (me[0] ^ core) + (me[1] ^ x)
                lines = pl.ds(pl.multiple_of(part * fourth, 8), fourth)
                for turn in range(2):
                    first = (me[2] ^ turn) * (width // 2)
                    pieces = [
                        tap_grad_ref[lines, pl.ds(pl.multiple_of(first + j * 128, 128), 128)]
                        for j in range(width // 256)
                    ] + [
                        bundle_ref[turn, lines, j * 128 : (j + 1) * 128]
                        for j in range(bundle_ref.shape[2] // 128)
                    ]
                    block = jnp.concatenate(pieces, axis=0).astype(BF16)
                    (send_ref if core else keep_ref)[2 * x + turn] = block


def side_block(index, segment, tap, stream, up, top, table, before, middle, own, other):
    side, tokens = stream.shape
    width = top.shape[1]
    heads = side // SIDE_HEAD
    hidden = own.shape[0] - 2 * side
    bundle = -(-(hidden + 2 * side + 8) // 128) * 128
    block = (side // 4) * (width // 256 + bundle // 128)

    def lanes(height):
        return pl.BlockSpec((height, SEQ), lambda i: (0, i))

    packed = pl.BlockSpec((4, block, 128), lambda i: (0, 0, 0))
    return pl.pallas_call(
        side_kernel,
        grid=(tokens // SEQ,),
        in_specs=[
            pl.BlockSpec(memory_space=pltpu.SMEM),
            whole(segment),
            lanes(side),
            lanes(side),
            lanes(side),
            pl.BlockSpec((SEQ, width), lambda i: (i, 0)),
            *map(whole, (table, before, middle, own, other)),
        ],
        out_specs=[lanes(side), lanes(side), packed, packed],
        out_shape=[
            jax.ShapeDtypeStruct((side, tokens), BF16),
            jax.ShapeDtypeStruct((side, tokens), BF16),
            jax.ShapeDtypeStruct((4, block, 128), BF16),
            jax.ShapeDtypeStruct((4, block, 128), BF16),
        ],
        scratch_shapes=[
            pltpu.VMEM((side, width), F32),
            pltpu.VMEM((side, 3 * side), F32),
            pltpu.VMEM((side, side), F32),
            pltpu.VMEM((side, hidden), F32),
            pltpu.VMEM((side, hidden), F32),
            pltpu.VMEM((side, 8), F32),
            pltpu.VMEM((2, side, bundle), F32),
            pltpu.VMEM((SEQ, SEQ), BF16),
            pltpu.VMEM((3 * side, side), BF16),
            pltpu.VMEM((side, hidden), BF16),
            pltpu.VMEM((side, side), BF16),
            pltpu.VMEM((hidden, side), BF16),
            pltpu.VMEM((heads, SEQ, SEQ), BF16),
            pltpu.VMEM((3 * side, SEQ), F32),
            pltpu.VMEM((heads, 16, SEQ), BF16),
            pltpu.VMEM((heads, 16, SEQ), BF16),
            pltpu.VMEM((heads, ROWS, SEQ), BF16),
            pltpu.VMEM((heads, ROWS, SEQ), F32),
            pltpu.VMEM((side, SEQ), F32),
            pltpu.VMEM((side, SEQ), F32),
            pltpu.VMEM((3 * side, SEQ), F32),
            pltpu.VMEM((8, TILE), F32),
        ],
        compiler_params=pltpu.CompilerParams(vmem_limit_bytes=60 << 20),
        name="side_block",
    )(index, segment, tap, stream, up, top, table, before, middle, own, other)


def unpack_kernel(
    index_ref,
    near_ref,
    far_ref,
    tap_ref,
    gate_ref,
    before_ref,
    middle_ref,
    q_ref,
    k_ref,
    v_ref,
    output_ref,
    expand_ref,
    reduce_ref,
    bundle_ref,
):
    side, width = tap_ref.shape
    half = expand_ref.shape[1]
    local = side // 2
    fourth = side // 4
    taps = width // 256
    tiles = bundle_ref.shape[1] // 128
    block = fourth * (taps + tiles)
    place = lax.axis_index("dp")
    me = (place % 2, (place // 2) % 2, lax.axis_index("side"))
    for core in range(2):
        held = (far_ref if core else near_ref)[...].astype(F32)
        for x in range(2):
            part = 2 * (me[0] ^ core) + (me[1] ^ x)
            lines = pl.ds(pl.multiple_of(part * fourth, 8), fourth)
            for turn in range(2):
                at = 2 * block + x * taps * fourth if turn else x * block
                first = (me[2] ^ turn) * (width // 2)
                for j in range(taps):
                    cols = pl.ds(pl.multiple_of(first + j * 128, 128), 128)
                    tap_ref[lines, cols] = held[at + j * fourth : at + (j + 1) * fourth]
            for j in range(tiles):
                at = x * block + (taps + j) * fourth
                bundle_ref[lines, j * 128 : (j + 1) * 128] = held[at : at + fourth]
    expand_ref[...] = bundle_ref[:, 0:half]
    reduce_ref[...] = jnp.transpose(bundle_ref[:, half : 2 * half])
    rest = jnp.transpose(bundle_ref[:, 2 * half : 2 * half + 4 * local + 8])
    q_ref[...] = rest[0:local]
    k_ref[...] = rest[local : 2 * local]
    v_ref[...] = rest[2 * local : 3 * local]
    output_ref[...] = rest[3 * local : 4 * local]
    small = rest[4 * local : 4 * local + 8]
    picked = lax.broadcasted_iota(jnp.int32, gate_ref.shape, 0) == index_ref[0]
    gate_ref[...] = jnp.where(picked, small[0:1], 0.0)
    before_ref[...] = small[1:2]
    middle_ref[...] = small[2:3]


def exchange(values, dp, side, dp_size):
    pairs = [
        (2 * i + s, 2 * (i ^ dp) + (s ^ side)) for i in range(dp_size) for s in range(2)
    ]
    return lax.ppermute(values, ("dp", "side"), pairs)


def add(*values):
    return functools.reduce(lambda a, b: a + b, [v.astype(F32) for v in values]).astype(BF16)


def shards(
    dp_size,
    backbone_in,
    segment_ids,
    gate_index,
    norm_before,
    norm_middle,
    frozen_query,
    frozen_key,
    frozen_value,
    frozen_output,
    frozen_expand,
    frozen_reduce,
    tap_weight,
    gate_table,
    side_stream,
    ladder_before,
    ladder_middle,
    ladder_query,
    ladder_key,
    ladder_value,
    ladder_output,
    ladder_expand,
    ladder_reduce,
    cotangent,
):
    side = side_stream.shape[1]
    width = tap_weight.shape[0]
    local = side // 2
    half = ladder_expand.shape[1]
    swap = functools.partial(exchange, dp_size=dp_size)
    own = pl.pallas_call(
        pack_kernel,
        out_shape=jax.ShapeDtypeStruct((2 * half + 4 * local, side), BF16),
        name="pack_weights",
    )(ladder_expand, ladder_query.T, ladder_key.T, ladder_value.T, ladder_output, ladder_reduce)
    other = swap(own, 0, 1)
    segment = segment_ids.reshape(-1, 1, SEQ)
    top, tap = frozen_block(
        segment,
        backbone_in,
        norm_before,
        norm_middle,
        frozen_query,
        frozen_key,
        frozen_value,
        frozen_output,
        frozen_expand,
        frozen_reduce,
        tap_weight.T,
    )
    result, stream_grad, keep, send = side_block(
        gate_index,
        segment,
        tap,
        side_stream.T,
        cotangent.T,
        top,
        gate_table,
        ladder_before[None],
        ladder_middle[None],
        own,
        other,
    )
    block = keep.shape[1]
    taps = (side // 4) * (width // 256)
    quad = add(keep, swap(send, 1, 0))
    mine = add(quad[0], swap(quad[1], 0, 1), swap(quad[2], 2, 0), swap(quad[3], 2, 1))
    bit = 4
    while bit < dp_size:
        mine = add(mine, swap(mine, bit, 0))
        bit *= 2
    near = jnp.concatenate(
        [mine, swap(mine, 2, 0), swap(mine[:taps], 0, 1), swap(mine[:taps], 2, 1)], axis=0
    )
    far = swap(near, 1, 0)
    shape = functools.partial(jax.ShapeDtypeStruct, dtype=F32)
    tap_sum, gate_sum, before_sum, middle_sum, q_sum, k_sum, v_sum, out_sum, expand_sum, reduce_sum = pl.pallas_call(
        unpack_kernel,
        in_specs=[
            pl.BlockSpec(memory_space=pltpu.SMEM),
            pl.BlockSpec(memory_space=pltpu.VMEM),
            pl.BlockSpec(memory_space=pltpu.VMEM),
        ],
        out_shape=[
            shape((side, width)),
            shape(gate_table.shape),
            shape((1, side)),
            shape((1, side)),
            shape((local, side)),
            shape((local, side)),
            shape((local, side)),
            shape((local, side)),
            shape((side, half)),
            shape((half, side)),
        ],
        scratch_shapes=[pltpu.VMEM((side, (block - taps) // (side // 4) * 128), F32)],
        compiler_params=pltpu.CompilerParams(vmem_limit_bytes=8 << 20),
        name="unpack_gradients",
    )(gate_index, near, far)
    return (
        result.T,
        stream_grad.T,
        tap_sum.T,
        gate_sum,
        before_sum[0],
        middle_sum[0],
        q_sum.T,
        k_sum.T,
        v_sum.T,
        out_sum,
        expand_sum,
        reduce_sum,
    )


def solution(mesh):
    rows = P(("dp", "side"), None)
    placed = (
        rows,
        P("dp"),
        *([P()] * 11),
        rows,
        P(),
        P(),
        P(None, "side"),
        P(None, "side"),
        P(None, "side"),
        P("side", None),
        P(None, "side"),
        P("side", None),
        rows,
    )
    return jax.shard_map(
        functools.partial(shards, mesh.shape["dp"]),
        mesh=mesh,
        in_specs=placed,
        out_specs=(
            rows,
            rows,
            P(),
            P(),
            P(),
            P(),
            P(None, "side"),
            P(None, "side"),
            P(None, "side"),
            P("side", None),
            P(None, "side"),
            P("side", None),
        ),
        check_vma=False,
    )
```

```python
import functools

import jax
import jax.numpy as jnp
from jax import lax
from jax.experimental import pallas as pl
from jax.experimental.pallas import tpu as pltpu
from jax.sharding import PartitionSpec as P

HEAD = 64
SIDE_HEAD = 8
SEQ = 1024
EPS = 1e-06
MASKED = -1e30
LOG2E = 1.4426950408889634
LEAST = 2.0**-64
MOST = 2.0**64
TILE = 1024
ROWS = 96
GROUP = 4
PAIRS = 2

F32 = jnp.float32
BF16 = jnp.bfloat16
NN = (((1,), (0,)), ((), ()))
NT = (((1,), (1,)), ((), ()))
TN = (((0,), (0,)), ((), ()))


def dot(left, right, dims=NN):
    return lax.dot_general(left, right, dims, preferred_element_type=F32)


def gelu_inner(values):
    return 0.7978845608028654 * values * (1.0 + 0.044715 * values * values)


def gelu(values):
    return 0.5 * values * (1.0 + jnp.tanh(gelu_inner(values)))


def gelu_both(values):
    square = values * values
    bend = jnp.tanh(0.7978845608028654 * values * (1.0 + 0.044715 * square))
    half = 0.5 * (1.0 + bend)
    slope = 0.7978845608028654 * (1.0 + 3.0 * 0.044715 * square)
    return values * half, half + 0.5 * values * (1.0 - bend * bend) * slope


def fill_mask(row, mask_ref):
    row = row.astype(F32)
    column = jnp.transpose(jnp.broadcast_to(row, (8, SEQ)))[:, 0:1]
    for step in range(SEQ // 128):
        lanes = slice(step * 128, (step + 1) * 128)
        mask_ref[:, lanes] = jnp.where(column == row[:, lanes], 1.0, 0.0).astype(BF16)


def note_totals(fine_ref, totals):
    fine = jnp.logical_and(totals >= LEAST, totals <= MOST)
    fine_ref[...] = jnp.where(fine, fine_ref[...], 0.0)


def weights_of(scores, mask, careful):
    if not careful:
        return jnp.exp2(scores).astype(BF16) * mask
    allowed = mask.astype(F32) > 0.5
    scores = jnp.where(allowed, scores, MASKED)
    highest = jnp.max(scores, axis=0, keepdims=True)
    return jnp.exp2(scores - highest).astype(BF16)


def frozen_kernel(
    segment_ref,
    x_ref,
    before_ref,
    middle_ref,
    tap_t_ref,
    wq_hbm,
    wk_hbm,
    wv_hbm,
    wo_hbm,
    we_hbm,
    wr_hbm,
    top_ref,
    tap_ref,
    wq_ref,
    wk_ref,
    wv_ref,
    wo_ref,
    we_ref,
    wr_ref,
    copied,
    mask_ref,
    normed_ref,
    q_ref,
    k_ref,
    v_ref,
    ctx_ref,
    wv_t_ref,
    fine_ref,
):
    width = x_ref.shape[1]
    heads = width // HEAD
    padded = v_ref.shape[1]

    starting = pl.program_id(0) == 0
    copies = [
        pltpu.make_async_copy(source, target, copied.at[i])
        for i, (source, target) in enumerate(
            (
                (wq_hbm, wq_ref),
                (wk_hbm, wk_ref),
                (wv_hbm, wv_ref),
                (wo_hbm, wo_ref),
                (we_hbm, we_ref),
                (wr_hbm, wr_ref),
            )
        )
    ]

    @pl.when(starting)
    def _():
        for copy in copies[0:3]:
            copy.start()
        v_ref[:, HEAD:padded] = jnp.ones((heads, padded - HEAD, SEQ), BF16)

    here = lax.axis_index("side") * pl.num_programs(0) + pl.program_id(0)
    fill_mask(segment_ref[here], mask_ref)
    base = x_ref[...].astype(F32)
    factor = lax.rsqrt(jnp.mean(base * base, axis=-1, keepdims=True) + EPS)
    normed_ref[...] = (base * factor * before_ref[...][None]).astype(BF16)
    @pl.when(starting)
    def _():
        for copy in copies[0:3]:
            copy.wait()
        for copy in copies[3:6]:
            copy.start()
        wv_t_ref[...] = jnp.transpose(wv_ref[...])

    q_ref[...] = (dot(normed_ref[...], wq_ref[...]) * (HEAD**-0.5 * LOG2E)).astype(BF16)
    k_ref[...] = dot(normed_ref[...], wk_ref[...]).astype(BF16)
    v = dot(wv_t_ref[...], normed_ref[...], NT).astype(BF16)
    for head in range(heads):
        v_ref[head, 0:HEAD] = v[head * HEAD : (head + 1) * HEAD]

    def attend(careful, tile, together):
        def one(pair, turn, start):
            lanes = pl.ds(start, tile)
            both = pl.ds(pl.multiple_of(pair * 2 * HEAD, 2 * HEAD), 2 * HEAD)
            cols = slice(turn * HEAD, (turn + 1) * HEAD)
            scores = dot(k_ref[:, both][:, cols], q_ref[lanes, both][:, cols], NT)
            probs = weights_of(scores, mask_ref[:, lanes], careful)
            mixed = dot(v_ref[2 * pair + turn], probs)
            if not careful:
                note_totals(fine_ref, mixed[HEAD : HEAD + 8])
            rows = pl.ds(pl.multiple_of((2 * pair + turn) * HEAD, HEAD), HEAD)
            ctx_ref[rows, lanes] = (mixed[0:HEAD] / mixed[HEAD : HEAD + 1]).astype(BF16)

        def step(group, carry):
            for pair in range(together):
                for turn in range(2):
                    for i in range(SEQ // tile):
                        one(group * together + pair, turn, i * tile)
            return carry

        lax.fori_loop(0, heads // 2 // together, step, 0)

    fine_ref[...] = jnp.ones_like(fine_ref)
    attend(False, TILE, PAIRS)
    pl.when(jnp.min(fine_ref[...]) < 0.5)(lambda: attend(True, TILE, 1))

    @pl.when(starting)
    def _():
        for copy in copies[3:6]:
            copy.wait()

    chunk = 1024
    hidden = we_ref.shape[1]
    piece = 768

    def feed_forward(part, carry):
        rows = pl.ds(pl.multiple_of(part * chunk, chunk), chunk)
        middle = x_ref[rows].astype(F32) + dot(ctx_ref[:, rows], wo_ref[...], TN)
        scale = lax.rsqrt(jnp.mean(middle * middle, axis=-1, keepdims=True) + EPS)
        normed = (middle * scale * middle_ref[...][None]).astype(BF16)
        total = middle
        for j in range(hidden // piece):
            cols = slice(j * piece, (j + 1) * piece)
            expanded = gelu(dot(normed, we_ref[:, cols])).astype(BF16)
            total = total + dot(expanded, wr_ref[cols])
        top = total.astype(BF16)
        top_ref[rows] = top
        tap_ref[:, rows] = dot(tap_t_ref[...], top, NT).astype(BF16)
        return carry

    lax.fori_loop(0, SEQ // chunk, feed_forward, 0)


def whole(array):
    shape = array.shape
    return pl.BlockSpec(shape, lambda i: (0,) * len(shape), pipeline_mode=pl.Buffered(1))


def frozen_block(segment, x, before, middle, wq, wk, wv, wo, we, wr, tap_t):
    tokens, width = x.shape
    heads = width // HEAD
    side = tap_t.shape[0]
    return pl.pallas_call(
        frozen_kernel,
        grid=(tokens // SEQ,),
        in_specs=[
            whole(segment),
            pl.BlockSpec((SEQ, width), lambda i: (i, 0)),
            *map(whole, (before, middle, tap_t)),
            *[pl.BlockSpec(memory_space=pl.ANY)] * 6,
        ],
        out_specs=[
            pl.BlockSpec((SEQ, width), lambda i: (i, 0)),
            pl.BlockSpec((side, SEQ), lambda i: (0, i)),
        ],
        out_shape=[
            jax.ShapeDtypeStruct((tokens, width), BF16),
            jax.ShapeDtypeStruct((side, tokens), BF16),
        ],
        scratch_shapes=[
            *[pltpu.VMEM(w.shape, BF16) for w in (wq, wk, wv, wo, we, wr)],
            pltpu.SemaphoreType.DMA((6,)),
            pltpu.VMEM((SEQ, SEQ), BF16),
            pltpu.VMEM((SEQ, width), BF16),
            pltpu.VMEM((SEQ, width), BF16),
            pltpu.VMEM((SEQ, width), BF16),
            pltpu.VMEM((heads, HEAD + 16, SEQ), BF16),
            pltpu.VMEM((width, SEQ), BF16),
            pltpu.VMEM((width, width), BF16),
            pltpu.VMEM((8, TILE), F32),
        ],
        compiler_params=pltpu.CompilerParams(vmem_limit_bytes=60 << 20),
        name="frozen_block",
    )(segment, x, before, middle, tap_t, wq, wk, wv, wo, we, wr)


def outer_rows(left, right):
    return [left[e : e + 1] * right for e in range(SIDE_HEAD)]


def pack_kernel(expand_ref, q_ref, k_ref, v_ref, output_ref, reduce_ref, packed_ref):
    side, half = expand_ref.shape
    packed_ref[0:side] = expand_ref[:, 0:side]
    packed_ref[side : 2 * side] = expand_ref[:, side:half]
    at = half
    for ref in (q_ref, k_ref, v_ref, output_ref, reduce_ref):
        packed_ref[at : at + ref.shape[0]] = ref[...]
        at += ref.shape[0]


def side_kernel(
    index_ref,
    segment_ref,
    tap_ref,
    stream_ref,
    up_ref,
    top_ref,
    table_ref,
    before_ref,
    middle_ref,
    own_ref,
    other_ref,
    out_ref,
    stream_grad_ref,
    keep_ref,
    send_ref,
    tap_grad_ref,
    qkv_grad_ref,
    out_grad_ref,
    expand_grad_ref,
    reduce_grad_ref,
    small_ref,
    bundle_ref,
    mask_ref,
    w_ref,
    we_ref,
    wo_ref,
    wr_ref,
    e_ref,
    qkv_ref,
    q16_ref,
    k16_ref,
    rows_ref,
    moment_ref,
    ctx_ref,
    dctx_ref,
    dqkv_ref,
    fine_ref,
):
    side = tap_ref.shape[0]
    heads = side // SIDE_HEAD
    local = side // 2
    hidden = we_ref.shape[1]
    half = hidden // 2

    @pl.when(pl.program_id(0) == 0)
    def _():
        for turn, ref in ((0, own_ref), (1, other_ref)):
            we_ref[:, turn * half : turn * half + side] = ref[0:side]
            we_ref[:, turn * half + side : (turn + 1) * half] = ref[side:half]
            at = half
            w_ref[turn * 3 * local : (turn + 1) * 3 * local] = ref[at : at + 3 * local]
            at += 3 * local
            wo_ref[turn * local : (turn + 1) * local] = ref[at : at + local]
            at += local
            wr_ref[turn * half : (turn + 1) * half] = ref[at : at + half]
        tap_grad_ref[...] = jnp.zeros_like(tap_grad_ref)
        qkv_grad_ref[...] = jnp.zeros_like(qkv_grad_ref)
        out_grad_ref[...] = jnp.zeros_like(out_grad_ref)
        expand_grad_ref[...] = jnp.zeros_like(expand_grad_ref)
        reduce_grad_ref[...] = jnp.zeros_like(reduce_grad_ref)
        small_ref[...] = jnp.zeros_like(small_ref)

    here = lax.axis_index("side") * pl.num_programs(0) + pl.program_id(0)
    fill_mask(segment_ref[here], mask_ref)
    logits = table_ref[pl.ds(index_ref[0], 1), :]
    stacked = jnp.concatenate(
        [
            jnp.broadcast_to(jax.nn.sigmoid(logits), (8, side)),
            jnp.broadcast_to(before_ref[...], (8, side)),
            jnp.broadcast_to(middle_ref[...], (8, side)),
        ],
        axis=0,
    )
    columns = jnp.transpose(stacked)
    gate, before, middle = columns[:, 0:1], columns[:, 8:9], columns[:, 16:17]

    def head_rows(kind, head):
        start = (head // (heads // 2)) * 3 * local + kind * local + (head % (heads // 2)) * SIDE_HEAD
        return pl.ds(pl.multiple_of(start, SIDE_HEAD), SIDE_HEAD)

    tap = tap_ref[...].astype(F32)
    stream = stream_ref[...].astype(F32)
    mixed = gate * tap + (1.0 - gate) * stream
    factor1 = lax.rsqrt(jnp.mean(mixed * mixed, axis=0, keepdims=True) + EPS)
    n1 = (mixed * factor1 * before).astype(BF16)
    qkv_ref[...] = dot(w_ref[...], n1)

    zeros8 = jnp.zeros((SIDE_HEAD, SEQ), F32)
    ones8 = jnp.ones((SIDE_HEAD, SEQ), F32)

    def prepare(head):
        q = qkv_ref[head_rows(0, head)] * (SIDE_HEAD**-0.5 * LOG2E)
        q = q.astype(BF16).astype(F32)
        k = qkv_ref[head_rows(1, head)].astype(BF16).astype(F32)
        v = qkv_ref[head_rows(2, head)].astype(BF16).astype(F32)
        qkv_ref[head_rows(0, head)] = q
        qkv_ref[head_rows(1, head)] = k
        qkv_ref[head_rows(2, head)] = v
        q16_ref[head] = jnp.concatenate([q, zeros8], axis=0).astype(BF16)
        k16_ref[head] = jnp.concatenate([k, zeros8], axis=0).astype(BF16)
        rows = [v, ones8, k, zeros8] + outer_rows(v, k)
        rows_ref[head] = jnp.concatenate(rows, axis=0).astype(BF16)

    def prepare_group(group, carry):
        for turn in range(GROUP):
            prepare(group * GROUP + turn)
        return carry

    lax.fori_loop(0, heads // GROUP, prepare_group, 0)

    def attend(careful, tile):
        def one(head, start):
            at = pl.multiple_of(head * SIDE_HEAD, SIDE_HEAD)
            lanes = pl.ds(start, tile)
            scores = dot(k16_ref[head], q16_ref[head, :, lanes], TN)
            probs = weights_of(scores, mask_ref[:, lanes], careful)
            e_ref[head, lanes, :] = jnp.transpose(probs)
            found = dot(rows_ref[head], probs)
            if not careful:
                note_totals(fine_ref, found[8:16])
            inverse = 1.0 / found[8:16]
            ctx_ref[pl.ds(at, SIDE_HEAD), lanes] = found[0:8] * inverse
            moment_ref[head, 8:16, lanes] = inverse
            moment_ref[head, 16:24, lanes] = found[16:24] * inverse
            for e in range(SIDE_HEAD):
                low = 32 + e * SIDE_HEAD
                moment_ref[head, low : low + 8, lanes] = found[low : low + 8] * inverse

        together = 1 if careful else GROUP

        def step(group, carry):
            for turn in range(together):
                for i in range(SEQ // tile):
                    one(group * together + turn, i * tile)
            return carry

        lax.fori_loop(0, heads // together, step, 0)

    fine_ref[...] = jnp.ones_like(fine_ref)
    attend(False, TILE)
    pl.when(jnp.min(fine_ref[...]) < 0.5)(lambda: attend(True, TILE))

    ctx = ctx_ref[...].astype(BF16)
    res1 = mixed + dot(wo_ref[...], ctx, TN)
    factor2 = lax.rsqrt(jnp.mean(res1 * res1, axis=0, keepdims=True) + EPS)
    z = res1 * factor2
    n2 = (z * middle).astype(BF16)
    pre = dot(we_ref[...], n2, TN)
    act, slope = gelu_both(pre)
    act = act.astype(BF16)
    result = res1 + dot(wr_ref[...], act, TN)
    out_ref[...] = result.astype(BF16)

    low_up = up_ref[...]
    up = low_up.astype(F32)
    reduce_grad_ref[...] += dot(low_up, act, NT)
    dpre = (dot(wr_ref[...], low_up) * slope).astype(BF16)
    expand_grad_ref[...] += dot(n2, dpre, NT)
    dn2 = dot(we_ref[...], dpre)
    middle_grad = jnp.sum(dn2 * z, axis=1, keepdims=True)
    u = dn2 * middle
    spread = jnp.mean(u * res1, axis=0, keepdims=True)
    dres1 = up + factor2 * u - z * (factor2 * factor2 * spread)
    low_dres = dres1.astype(BF16)
    out_grad_ref[...] += dot(low_dres, ctx, NT)
    dctx_ref[...] = dot(wo_ref[...], low_dres).astype(BF16).astype(F32)

    def prepare_back(head):
        at = pl.multiple_of(head * SIDE_HEAD, SIDE_HEAD)
        q = qkv_ref[head_rows(0, head)]
        dctx = dctx_ref[pl.ds(at, SIDE_HEAD)]
        inverse = moment_ref[head, 8:16]
        inner = jnp.sum(dctx * ctx_ref[pl.ds(at, SIDE_HEAD)], axis=0, keepdims=True)
        dq = -inner * moment_ref[head, 16:24]
        for e in range(SIDE_HEAD):
            low = 32 + e * SIDE_HEAD
            dq = dq + dctx[e : e + 1] * moment_ref[head, low : low + 8]
        dqkv_ref[head_rows(0, head)] = dq * SIDE_HEAD**-0.5
        scaled = dctx * inverse
        rows = [scaled, zeros8, (inner * inverse) * q, zeros8] + outer_rows(scaled, q)
        rows_ref[head] = jnp.concatenate(rows, axis=0).astype(BF16)

    def prepare_back_group(group, carry):
        for turn in range(GROUP):
            prepare_back(group * GROUP + turn)
        return carry

    lax.fori_loop(0, heads // GROUP, prepare_back_group, 0)

    def back(head):
        found = dot(rows_ref[head], e_ref[head])
        v = qkv_ref[head_rows(2, head)]
        dk = -found[16:24]
        for e in range(SIDE_HEAD):
            low = 32 + e * SIDE_HEAD
            dk = dk + v[e : e + 1] * found[low : low + 8]
        dqkv_ref[head_rows(1, head)] = dk * (1.0 / LOG2E)
        dqkv_ref[head_rows(2, head)] = found[0:8]

    def back_group(group, carry):
        for turn in range(GROUP):
            back(group * GROUP + turn)
        return carry

    lax.fori_loop(0, heads // GROUP, back_group, 0)

    dqkv = dqkv_ref[...].astype(BF16)
    qkv_grad_ref[...] += dot(n1, dqkv, NT)
    dn1 = dot(w_ref[...], dqkv, TN)
    unit = mixed * factor1
    before_grad = jnp.sum(dn1 * unit, axis=1, keepdims=True)
    u = dn1 * before
    spread = jnp.mean(u * mixed, axis=0, keepdims=True)
    dmixed = dres1 + factor1 * u - unit * (factor1 * factor1 * spread)
    logit = jnp.sum(dmixed * (tap - stream), axis=1, keepdims=True) * gate * (1.0 - gate)
    small_ref[...] += jnp.concatenate(
        [logit, before_grad, middle_grad, jnp.zeros((side, 5), F32)], axis=1
    )
    tap_grad_ref[...] += dot((gate * dmixed).astype(BF16), top_ref[...])
    stream_grad_ref[...] = ((1.0 - gate) * dmixed).astype(BF16)

    @pl.when(pl.program_id(0) == pl.num_programs(0) - 1)
    def _():
        for turn in range(2):
            bundle_ref[turn] = jnp.concatenate(
                [
                    expand_grad_ref[:, turn * half : (turn + 1) * half],
                    reduce_grad_ref[:, turn * half : (turn + 1) * half],
                    qkv_grad_ref[:, turn * 3 * local : (turn + 1) * 3 * local],
                    out_grad_ref[:, turn * local : (turn + 1) * local],
                    small_ref[...],
                    jnp.zeros((side, bundle_ref.shape[2] - 2 * half - 4 * local - 8), F32),
                ],
                axis=1,
            )
        place = lax.axis_index("dp")
        me = (place % 2, (place // 2) % 2, lax.axis_index("side"))
        fourth = side // 4
        width = tap_grad_ref.shape[1]
        for core in range(2):
            for x in range(2):
                part = 2 * (me[0] ^ core) + (me[1] ^ x)
                lines = pl.ds(pl.multiple_of(part * fourth, 8), fourth)
                for turn in range(2):
                    first = (me[2] ^ turn) * (width // 2)
                    pieces = [
                        tap_grad_ref[lines, pl.ds(pl.multiple_of(first + j * 128, 128), 128)]
                        for j in range(width // 256)
                    ] + [
                        bundle_ref[turn, lines, j * 128 : (j + 1) * 128]
                        for j in range(bundle_ref.shape[2] // 128)
                    ]
                    block = jnp.concatenate(pieces, axis=0).astype(BF16)
                    (send_ref if core else keep_ref)[2 * x + turn] = block


def side_block(index, segment, tap, stream, up, top, table, before, middle, own, other):
    side, tokens = stream.shape
    width = top.shape[1]
    heads = side // SIDE_HEAD
    hidden = own.shape[0] - 2 * side
    bundle = -(-(hidden + 2 * side + 8) // 128) * 128
    block = (side // 4) * (width // 256 + bundle // 128)

    def lanes(height):
        return pl.BlockSpec((height, SEQ), lambda i: (0, i))

    packed = pl.BlockSpec((4, block, 128), lambda i: (0, 0, 0))
    return pl.pallas_call(
        side_kernel,
        grid=(tokens // SEQ,),
        in_specs=[
            pl.BlockSpec(memory_space=pltpu.SMEM),
            whole(segment),
            lanes(side),
            lanes(side),
            lanes(side),
            pl.BlockSpec((SEQ, width), lambda i: (i, 0)),
            *map(whole, (table, before, middle, own, other)),
        ],
        out_specs=[lanes(side), lanes(side), packed, packed],
        out_shape=[
            jax.ShapeDtypeStruct((side, tokens), BF16),
            jax.ShapeDtypeStruct((side, tokens), BF16),
            jax.ShapeDtypeStruct((4, block, 128), BF16),
            jax.ShapeDtypeStruct((4, block, 128), BF16),
        ],
        scratch_shapes=[
            pltpu.VMEM((side, width), F32),
            pltpu.VMEM((side, 3 * side), F32),
            pltpu.VMEM((side, side), F32),
            pltpu.VMEM((side, hidden), F32),
            pltpu.VMEM((side, hidden), F32),
            pltpu.VMEM((side, 8), F32),
            pltpu.VMEM((2, side, bundle), F32),
            pltpu.VMEM((SEQ, SEQ), BF16),
            pltpu.VMEM((3 * side, side), BF16),
            pltpu.VMEM((side, hidden), BF16),
            pltpu.VMEM((side, side), BF16),
            pltpu.VMEM((hidden, side), BF16),
            pltpu.VMEM((heads, SEQ, SEQ), BF16),
            pltpu.VMEM((3 * side, SEQ), F32),
            pltpu.VMEM((heads, 16, SEQ), BF16),
            pltpu.VMEM((heads, 16, SEQ), BF16),
            pltpu.VMEM((heads, ROWS, SEQ), BF16),
            pltpu.VMEM((heads, ROWS, SEQ), F32),
            pltpu.VMEM((side, SEQ), F32),
            pltpu.VMEM((side, SEQ), F32),
            pltpu.VMEM((3 * side, SEQ), F32),
            pltpu.VMEM((8, TILE), F32),
        ],
        compiler_params=pltpu.CompilerParams(vmem_limit_bytes=60 << 20),
        name="side_block",
    )(index, segment, tap, stream, up, top, table, before, middle, own, other)


def unpack_kernel(
    index_ref,
    near_ref,
    far_ref,
    tap_ref,
    gate_ref,
    before_ref,
    middle_ref,
    q_ref,
    k_ref,
    v_ref,
    output_ref,
    expand_ref,
    reduce_ref,
    bundle_ref,
):
    side, width = tap_ref.shape
    half = expand_ref.shape[1]
    local = side // 2
    fourth = side // 4
    taps = width // 256
    tiles = bundle_ref.shape[1] // 128
    block = fourth * (taps + tiles)
    place = lax.axis_index("dp")
    me = (place % 2, (place // 2) % 2, lax.axis_index("side"))
    for core in range(2):
        held = (far_ref if core else near_ref)[...].astype(F32)
        for x in range(2):
            part = 2 * (me[0] ^ core) + (me[1] ^ x)
            lines = pl.ds(pl.multiple_of(part * fourth, 8), fourth)
            for turn in range(2):
                at = 2 * block + x * taps * fourth if turn else x * block
                first = (me[2] ^ turn) * (width // 2)
                for j in range(taps):
                    cols = pl.ds(pl.multiple_of(first + j * 128, 128), 128)
                    tap_ref[lines, cols] = held[at + j * fourth : at + (j + 1) * fourth]
            for j in range(tiles):
                at = x * block + (taps + j) * fourth
                bundle_ref[lines, j * 128 : (j + 1) * 128] = held[at : at + fourth]
    expand_ref[...] = bundle_ref[:, 0:half]
    reduce_ref[...] = jnp.transpose(bundle_ref[:, half : 2 * half])
    rest = jnp.transpose(bundle_ref[:, 2 * half : 2 * half + 4 * local + 8])
    q_ref[...] = rest[0:local]
    k_ref[...] = rest[local : 2 * local]
    v_ref[...] = rest[2 * local : 3 * local]
    output_ref[...] = rest[3 * local : 4 * local]
    small = rest[4 * local : 4 * local + 8]
    picked = lax.broadcasted_iota(jnp.int32, gate_ref.shape, 0) == index_ref[0]
    gate_ref[...] = jnp.where(picked, small[0:1], 0.0)
    before_ref[...] = small[1:2]
    middle_ref[...] = small[2:3]


def exchange(values, dp, side, dp_size):
    pairs = [
        (2 * i + s, 2 * (i ^ dp) + (s ^ side)) for i in range(dp_size) for s in range(2)
    ]
    return lax.ppermute(values, ("dp", "side"), pairs)


def add(*values):
    return functools.reduce(lambda a, b: a + b, [v.astype(F32) for v in values]).astype(BF16)


def shards(
    dp_size,
    backbone_in,
    segment_ids,
    gate_index,
    norm_before,
    norm_middle,
    frozen_query,
    frozen_key,
    frozen_value,
    frozen_output,
    frozen_expand,
    frozen_reduce,
    tap_weight,
    gate_table,
    side_stream,
    ladder_before,
    ladder_middle,
    ladder_query,
    ladder_key,
    ladder_value,
    ladder_output,
    ladder_expand,
    ladder_reduce,
    cotangent,
):
    side = side_stream.shape[1]
    width = tap_weight.shape[0]
    local = side // 2
    half = ladder_expand.shape[1]
    swap = functools.partial(exchange, dp_size=dp_size)
    own = pl.pallas_call(
        pack_kernel,
        out_shape=jax.ShapeDtypeStruct((2 * half + 4 * local, side), BF16),
        name="pack_weights",
    )(ladder_expand, ladder_query.T, ladder_key.T, ladder_value.T, ladder_output, ladder_reduce)
    other = swap(own, 0, 1)
    segment = segment_ids.reshape(-1, 1, SEQ)
    top, tap = frozen_block(
        segment,
        backbone_in,
        norm_before,
        norm_middle,
        frozen_query,
        frozen_key,
        frozen_value,
        frozen_output,
        frozen_expand,
        frozen_reduce,
        tap_weight.T,
    )
    result, stream_grad, keep, send = side_block(
        gate_index,
        segment,
        tap,
        side_stream.T,
        cotangent.T,
        top,
        gate_table,
        ladder_before[None],
        ladder_middle[None],
        own,
        other,
    )
    block = keep.shape[1]
    taps = (side // 4) * (width // 256)
    quad = add(keep, swap(send, 1, 0))
    mine = add(quad[0], swap(quad[1], 0, 1), swap(quad[2], 2, 0), swap(quad[3], 2, 1))
    bit = 4
    while bit < dp_size:
        steps = [bit, 2 * bit, 3 * bit] if 2 * bit < dp_size else [bit]
        mine = add(mine, *[swap(mine, step, 0) for step in steps])
        bit *= len(steps) + 1
    near = jnp.concatenate(
        [mine, swap(mine, 2, 0), swap(mine[:taps], 0, 1), swap(mine[:taps], 2, 1)], axis=0
    )
    far = swap(near, 1, 0)
    shape = functools.partial(jax.ShapeDtypeStruct, dtype=F32)
    tap_sum, gate_sum, before_sum, middle_sum, q_sum, k_sum, v_sum, out_sum, expand_sum, reduce_sum = pl.pallas_call(
        unpack_kernel,
        in_specs=[
            pl.BlockSpec(memory_space=pltpu.SMEM),
            pl.BlockSpec(memory_space=pltpu.VMEM),
            pl.BlockSpec(memory_space=pltpu.VMEM),
        ],
        out_shape=[
            shape((side, width)),
            shape(gate_table.shape),
            shape((1, side)),
            shape((1, side)),
            shape((local, side)),
            shape((local, side)),
            shape((local, side)),
            shape((local, side)),
            shape((side, half)),
            shape((half, side)),
        ],
        scratch_shapes=[pltpu.VMEM((side, (block - taps) // (side // 4) * 128), F32)],
        compiler_params=pltpu.CompilerParams(vmem_limit_bytes=8 << 20),
        name="unpack_gradients",
    )(gate_index, near, far)
    return (
        result.T,
        stream_grad.T,
        tap_sum.T,
        gate_sum,
        before_sum[0],
        middle_sum[0],
        q_sum.T,
        k_sum.T,
        v_sum.T,
        out_sum,
        expand_sum,
        reduce_sum,
    )


def solution(mesh):
    rows = P(("dp", "side"), None)
    placed = (
        rows,
        P("dp"),
        *([P()] * 11),
        rows,
        P(),
        P(),
        P(None, "side"),
        P(None, "side"),
        P(None, "side"),
        P("side", None),
        P(None, "side"),
        P("side", None),
        rows,
    )
    return jax.shard_map(
        functools.partial(shards, mesh.shape["dp"]),
        mesh=mesh,
        in_specs=placed,
        out_specs=(
            rows,
            rows,
            P(),
            P(),
            P(),
            P(),
            P(None, "side"),
            P(None, "side"),
            P(None, "side"),
            P("side", None),
            P(None, "side"),
            P("side", None),
        ),
        check_vma=False,
    )
```

```python
import functools

import jax
import jax.numpy as jnp
from jax import lax
from jax.experimental import pallas as pl
from jax.experimental.pallas import tpu as pltpu
from jax.sharding import PartitionSpec as P

HEAD = 64
SIDE_HEAD = 8
SEQ = 1024
EPS = 1e-06
MASKED = -1e30
LOG2E = 1.4426950408889634
LEAST = 2.0**-64
MOST = 2.0**64
TILE = 1024
ROWS = 96
GROUP = 4
PAIRS = 3

F32 = jnp.float32
BF16 = jnp.bfloat16
NN = (((1,), (0,)), ((), ()))
NT = (((1,), (1,)), ((), ()))
TN = (((0,), (0,)), ((), ()))


def dot(left, right, dims=NN):
    return lax.dot_general(left, right, dims, preferred_element_type=F32)


def gelu_inner(values):
    return 0.7978845608028654 * values * (1.0 + 0.044715 * values * values)


def gelu(values):
    return 0.5 * values * (1.0 + jnp.tanh(gelu_inner(values)))


def gelu_both(values):
    square = values * values
    bend = jnp.tanh(0.7978845608028654 * values * (1.0 + 0.044715 * square))
    half = 0.5 * (1.0 + bend)
    slope = 0.7978845608028654 * (1.0 + 3.0 * 0.044715 * square)
    return values * half, half + 0.5 * values * (1.0 - bend * bend) * slope


def fill_mask(row, mask_ref):
    row = row.astype(F32)
    column = jnp.transpose(jnp.broadcast_to(row, (8, SEQ)))[:, 0:1]
    for step in range(SEQ // 128):
        lanes = slice(step * 128, (step + 1) * 128)
        mask_ref[:, lanes] = jnp.where(column == row[:, lanes], 1.0, 0.0).astype(BF16)


def note_totals(fine_ref, totals):
    fine = jnp.logical_and(totals >= LEAST, totals <= MOST)
    fine_ref[...] = jnp.where(fine, fine_ref[...], 0.0)


def weights_of(scores, mask, careful):
    if not careful:
        return jnp.exp2(scores).astype(BF16) * mask
    allowed = mask.astype(F32) > 0.5
    scores = jnp.where(allowed, scores, MASKED)
    highest = jnp.max(scores, axis=0, keepdims=True)
    return jnp.exp2(scores - highest).astype(BF16)


def frozen_kernel(
    segment_ref,
    x_ref,
    before_ref,
    middle_ref,
    tap_t_ref,
    wq_hbm,
    wk_hbm,
    wv_hbm,
    wo_hbm,
    we_hbm,
    wr_hbm,
    top_ref,
    tap_ref,
    wq_ref,
    wk_ref,
    wv_ref,
    wo_ref,
    we_ref,
    wr_ref,
    copied,
    mask_ref,
    normed_ref,
    q_ref,
    k_ref,
    v_ref,
    ctx_ref,
    wv_t_ref,
    fine_ref,
):
    width = x_ref.shape[1]
    heads = width // HEAD
    padded = v_ref.shape[1]

    starting = pl.program_id(0) == 0
    copies = [
        pltpu.make_async_copy(source, target, copied.at[i])
        for i, (source, target) in enumerate(
            (
                (wq_hbm, wq_ref),
                (wk_hbm, wk_ref),
                (wv_hbm, wv_ref),
                (wo_hbm, wo_ref),
                (we_hbm, we_ref),
                (wr_hbm, wr_ref),
            )
        )
    ]

    @pl.when(starting)
    def _():
        for copy in copies[0:3]:
            copy.start()
        v_ref[:, HEAD:padded] = jnp.ones((heads, padded - HEAD, SEQ), BF16)

    @pl.when(starting)
    def _():
        for copy in copies[0:3]:
            copy.wait()
        for copy in copies[3:6]:
            copy.start()
        wv_t_ref[...] = jnp.transpose(wv_ref[...])

    for part in range(2):
        rows = slice(part * SEQ // 2, (part + 1) * SEQ // 2)
        base = x_ref[rows].astype(F32)
        factor = lax.rsqrt(jnp.mean(base * base, axis=-1, keepdims=True) + EPS)
        normed = (base * factor * before_ref[...][None]).astype(BF16)
        normed_ref[rows] = normed
        q_ref[rows] = (dot(normed, wq_ref[...]) * (HEAD**-0.5 * LOG2E)).astype(BF16)
        k_ref[rows] = dot(normed, wk_ref[...]).astype(BF16)
    here = lax.axis_index("side") * pl.num_programs(0) + pl.program_id(0)
    fill_mask(segment_ref[here], mask_ref)
    v = dot(wv_t_ref[...], normed_ref[...], NT).astype(BF16)
    for head in range(heads):
        v_ref[head, 0:HEAD] = v[head * HEAD : (head + 1) * HEAD]

    def attend(careful, tile, together):
        def one(pair, turn, start):
            lanes = pl.ds(start, tile)
            both = pl.ds(pl.multiple_of(pair * 2 * HEAD, 2 * HEAD), 2 * HEAD)
            cols = slice(turn * HEAD, (turn + 1) * HEAD)
            scores = dot(k_ref[:, both][:, cols], q_ref[lanes, both][:, cols], NT)
            probs = weights_of(scores, mask_ref[:, lanes], careful)
            mixed = dot(v_ref[2 * pair + turn], probs)
            if not careful:
                note_totals(fine_ref, mixed[HEAD : HEAD + 8])
            rows = pl.ds(pl.multiple_of((2 * pair + turn) * HEAD, HEAD), HEAD)
            ctx_ref[rows, lanes] = (mixed[0:HEAD] / mixed[HEAD : HEAD + 1]).astype(BF16)

        def step(group, carry):
            for pair in range(together):
                for turn in range(2):
                    for i in range(SEQ // tile):
                        one(group * together + pair, turn, i * tile)
            return carry

        lax.fori_loop(0, heads // 2 // together, step, 0)

    fine_ref[...] = jnp.ones_like(fine_ref)
    attend(False, TILE, PAIRS)
    pl.when(jnp.min(fine_ref[...]) < 0.5)(lambda: attend(True, TILE, 1))

    @pl.when(starting)
    def _():
        for copy in copies[3:6]:
            copy.wait()

    chunk = 1024
    hidden = we_ref.shape[1]
    piece = 768

    def feed_forward(part, carry):
        rows = pl.ds(pl.multiple_of(part * chunk, chunk), chunk)
        middle = x_ref[rows].astype(F32) + dot(ctx_ref[:, rows], wo_ref[...], TN)
        scale = lax.rsqrt(jnp.mean(middle * middle, axis=-1, keepdims=True) + EPS)
        normed = (middle * scale * middle_ref[...][None]).astype(BF16)
        total = middle
        for j in range(hidden // piece):
            cols = slice(j * piece, (j + 1) * piece)
            expanded = gelu(dot(normed, we_ref[:, cols])).astype(BF16)
            total = total + dot(expanded, wr_ref[cols])
        top = total.astype(BF16)
        top_ref[rows] = top
        tap_ref[:, rows] = dot(tap_t_ref[...], top, NT).astype(BF16)
        return carry

    lax.fori_loop(0, SEQ // chunk, feed_forward, 0)


def whole(array):
    shape = array.shape
    return pl.BlockSpec(shape, lambda i: (0,) * len(shape), pipeline_mode=pl.Buffered(1))


def frozen_block(segment, x, before, middle, wq, wk, wv, wo, we, wr, tap_t):
    tokens, width = x.shape
    heads = width // HEAD
    side = tap_t.shape[0]
    return pl.pallas_call(
        frozen_kernel,
        grid=(tokens // SEQ,),
        in_specs=[
            whole(segment),
            pl.BlockSpec((SEQ, width), lambda i: (i, 0)),
            *map(whole, (before, middle, tap_t)),
            *[pl.BlockSpec(memory_space=pl.ANY)] * 6,
        ],
        out_specs=[
            pl.BlockSpec((SEQ, width), lambda i: (i, 0)),
            pl.BlockSpec((side, SEQ), lambda i: (0, i)),
        ],
        out_shape=[
            jax.ShapeDtypeStruct((tokens, width), BF16),
            jax.ShapeDtypeStruct((side, tokens), BF16),
        ],
        scratch_shapes=[
            *[pltpu.VMEM(w.shape, BF16) for w in (wq, wk, wv, wo, we, wr)],
            pltpu.SemaphoreType.DMA((6,)),
            pltpu.VMEM((SEQ, SEQ), BF16),
            pltpu.VMEM((SEQ, width), BF16),
            pltpu.VMEM((SEQ, width), BF16),
            pltpu.VMEM((SEQ, width), BF16),
            pltpu.VMEM((heads, HEAD + 16, SEQ), BF16),
            pltpu.VMEM((width, SEQ), BF16),
            pltpu.VMEM((width, width), BF16),
            pltpu.VMEM((8, TILE), F32),
        ],
        compiler_params=pltpu.CompilerParams(vmem_limit_bytes=60 << 20),
        name="frozen_block",
    )(segment, x, before, middle, tap_t, wq, wk, wv, wo, we, wr)


def outer_rows(left, right):
    return [left[e : e + 1] * right for e in range(SIDE_HEAD)]


def pack_kernel(expand_ref, q_ref, k_ref, v_ref, output_ref, reduce_ref, packed_ref):
    side, half = expand_ref.shape
    packed_ref[0:side] = expand_ref[:, 0:side]
    packed_ref[side : 2 * side] = expand_ref[:, side:half]
    at = half
    for ref in (q_ref, k_ref, v_ref, output_ref, reduce_ref):
        packed_ref[at : at + ref.shape[0]] = ref[...]
        at += ref.shape[0]


def side_kernel(
    index_ref,
    segment_ref,
    tap_ref,
    stream_ref,
    up_ref,
    top_ref,
    table_ref,
    before_ref,
    middle_ref,
    own_ref,
    other_ref,
    out_ref,
    stream_grad_ref,
    keep_ref,
    send_ref,
    tap_grad_ref,
    qkv_grad_ref,
    out_grad_ref,
    expand_grad_ref,
    reduce_grad_ref,
    small_ref,
    bundle_ref,
    mask_ref,
    w_ref,
    we_ref,
    wo_ref,
    wr_ref,
    e_ref,
    qkv_ref,
    q16_ref,
    k16_ref,
    rows_ref,
    moment_ref,
    ctx_ref,
    dctx_ref,
    dqkv_ref,
    fine_ref,
):
    side = tap_ref.shape[0]
    heads = side // SIDE_HEAD
    local = side // 2
    hidden = we_ref.shape[1]
    half = hidden // 2

    @pl.when(pl.program_id(0) == 0)
    def _():
        for turn, ref in ((0, own_ref), (1, other_ref)):
            we_ref[:, turn * half : turn * half + side] = ref[0:side]
            we_ref[:, turn * half + side : (turn + 1) * half] = ref[side:half]
            at = half
            w_ref[turn * 3 * local : (turn + 1) * 3 * local] = ref[at : at + 3 * local]
            at += 3 * local
            wo_ref[turn * local : (turn + 1) * local] = ref[at : at + local]
            at += local
            wr_ref[turn * half : (turn + 1) * half] = ref[at : at + half]
        tap_grad_ref[...] = jnp.zeros_like(tap_grad_ref)
        qkv_grad_ref[...] = jnp.zeros_like(qkv_grad_ref)
        out_grad_ref[...] = jnp.zeros_like(out_grad_ref)
        expand_grad_ref[...] = jnp.zeros_like(expand_grad_ref)
        reduce_grad_ref[...] = jnp.zeros_like(reduce_grad_ref)
        small_ref[...] = jnp.zeros_like(small_ref)

    logits = table_ref[pl.ds(index_ref[0], 1), :]
    stacked = jnp.concatenate(
        [
            jnp.broadcast_to(jax.nn.sigmoid(logits), (8, side)),
            jnp.broadcast_to(before_ref[...], (8, side)),
            jnp.broadcast_to(middle_ref[...], (8, side)),
        ],
        axis=0,
    )
    columns = jnp.transpose(stacked)
    gate, before, middle = columns[:, 0:1], columns[:, 8:9], columns[:, 16:17]

    def head_rows(kind, head):
        start = (head // (heads // 2)) * 3 * local + kind * local + (head % (heads // 2)) * SIDE_HEAD
        return pl.ds(pl.multiple_of(start, SIDE_HEAD), SIDE_HEAD)

    tap = tap_ref[...].astype(F32)
    stream = stream_ref[...].astype(F32)
    mixed = gate * tap + (1.0 - gate) * stream
    factor1 = lax.rsqrt(jnp.mean(mixed * mixed, axis=0, keepdims=True) + EPS)
    n1 = (mixed * factor1 * before).astype(BF16)
    qkv_ref[...] = dot(w_ref[...], n1)

    here = lax.axis_index("side") * pl.num_programs(0) + pl.program_id(0)
    fill_mask(segment_ref[here], mask_ref)

    zeros8 = jnp.zeros((SIDE_HEAD, SEQ), F32)
    ones8 = jnp.ones((SIDE_HEAD, SEQ), F32)

    def prepare(head):
        q = qkv_ref[head_rows(0, head)] * (SIDE_HEAD**-0.5 * LOG2E)
        q = q.astype(BF16).astype(F32)
        k = qkv_ref[head_rows(1, head)].astype(BF16).astype(F32)
        v = qkv_ref[head_rows(2, head)].astype(BF16).astype(F32)
        qkv_ref[head_rows(0, head)] = q
        qkv_ref[head_rows(1, head)] = k
        qkv_ref[head_rows(2, head)] = v
        q16_ref[head] = jnp.concatenate([q, zeros8], axis=0).astype(BF16)
        k16_ref[head] = jnp.concatenate([k, zeros8], axis=0).astype(BF16)
        rows = [v, ones8, k, zeros8] + outer_rows(v, k)
        rows_ref[head] = jnp.concatenate(rows, axis=0).astype(BF16)

    def prepare_group(group, carry):
        for turn in range(GROUP):
            prepare(group * GROUP + turn)
        return carry

    lax.fori_loop(0, heads // GROUP, prepare_group, 0)

    def attend(careful, tile):
        def one(head, start):
            at = pl.multiple_of(head * SIDE_HEAD, SIDE_HEAD)
            lanes = pl.ds(start, tile)
            scores = dot(k16_ref[head], q16_ref[head, :, lanes], TN)
            probs = weights_of(scores, mask_ref[:, lanes], careful)
            e_ref[head, lanes, :] = jnp.transpose(probs)
            found = dot(rows_ref[head], probs)
            if not careful:
                note_totals(fine_ref, found[8:16])
            inverse = 1.0 / found[8:16]
            ctx_ref[pl.ds(at, SIDE_HEAD), lanes] = found[0:8] * inverse
            moment_ref[head, 8:16, lanes] = inverse
            moment_ref[head, 16:24, lanes] = found[16:24] * inverse
            for e in range(SIDE_HEAD):
                low = 32 + e * SIDE_HEAD
                moment_ref[head, low : low + 8, lanes] = found[low : low + 8] * inverse

        together = 1 if careful else GROUP

        def step(group, carry):
            for turn in range(together):
                for i in range(SEQ // tile):
                    one(group * together + turn, i * tile)
            return carry

        lax.fori_loop(0, heads // together, step, 0)

    fine_ref[...] = jnp.ones_like(fine_ref)
    attend(False, TILE)
    pl.when(jnp.min(fine_ref[...]) < 0.5)(lambda: attend(True, TILE))

    ctx = ctx_ref[...].astype(BF16)
    res1 = mixed + dot(wo_ref[...], ctx, TN)
    factor2 = lax.rsqrt(jnp.mean(res1 * res1, axis=0, keepdims=True) + EPS)
    z = res1 * factor2
    n2 = (z * middle).astype(BF16)
    pre = dot(we_ref[...], n2, TN)
    act, slope = gelu_both(pre)
    act = act.astype(BF16)
    result = res1 + dot(wr_ref[...], act, TN)
    out_ref[...] = result.astype(BF16)

    low_up = up_ref[...]
    up = low_up.astype(F32)
    reduce_grad_ref[...] += dot(low_up, act, NT)
    dpre = (dot(wr_ref[...], low_up) * slope).astype(BF16)
    expand_grad_ref[...] += dot(n2, dpre, NT)
    dn2 = dot(we_ref[...], dpre)
    middle_grad = jnp.sum(dn2 * z, axis=1, keepdims=True)
    u = dn2 * middle
    spread = jnp.mean(u * res1, axis=0, keepdims=True)
    dres1 = up + factor2 * u - z * (factor2 * factor2 * spread)
    low_dres = dres1.astype(BF16)
    out_grad_ref[...] += dot(low_dres, ctx, NT)
    dctx_ref[...] = dot(wo_ref[...], low_dres).astype(BF16).astype(F32)

    def prepare_back(head):
        at = pl.multiple_of(head * SIDE_HEAD, SIDE_HEAD)
        q = qkv_ref[head_rows(0, head)]
        dctx = dctx_ref[pl.ds(at, SIDE_HEAD)]
        inverse = moment_ref[head, 8:16]
        inner = jnp.sum(dctx * ctx_ref[pl.ds(at, SIDE_HEAD)], axis=0, keepdims=True)
        dq = -inner * moment_ref[head, 16:24]
        for e in range(SIDE_HEAD):
            low = 32 + e * SIDE_HEAD
            dq = dq + dctx[e : e + 1] * moment_ref[head, low : low + 8]
        dqkv_ref[head_rows(0, head)] = dq * SIDE_HEAD**-0.5
        scaled = dctx * inverse
        rows = [scaled, zeros8, (inner * inverse) * q, zeros8] + outer_rows(scaled, q)
        rows_ref[head] = jnp.concatenate(rows, axis=0).astype(BF16)

    def prepare_back_group(group, carry):
        for turn in range(GROUP):
            prepare_back(group * GROUP + turn)
        return carry

    lax.fori_loop(0, heads // GROUP, prepare_back_group, 0)

    def back(head):
        found = dot(rows_ref[head], e_ref[head])
        v = qkv_ref[head_rows(2, head)]
        dk = -found[16:24]
        for e in range(SIDE_HEAD):
            low = 32 + e * SIDE_HEAD
            dk = dk + v[e : e + 1] * found[low : low + 8]
        dqkv_ref[head_rows(1, head)] = dk * (1.0 / LOG2E)
        dqkv_ref[head_rows(2, head)] = found[0:8]

    def back_group(group, carry):
        for turn in range(GROUP):
            back(group * GROUP + turn)
        return carry

    lax.fori_loop(0, heads // GROUP, back_group, 0)

    dqkv = dqkv_ref[...].astype(BF16)
    qkv_grad_ref[...] += dot(n1, dqkv, NT)
    dn1 = dot(w_ref[...], dqkv, TN)
    unit = mixed * factor1
    before_grad = jnp.sum(dn1 * unit, axis=1, keepdims=True)
    u = dn1 * before
    spread = jnp.mean(u * mixed, axis=0, keepdims=True)
    dmixed = dres1 + factor1 * u - unit * (factor1 * factor1 * spread)
    logit = jnp.sum(dmixed * (tap - stream), axis=1, keepdims=True) * gate * (1.0 - gate)
    small_ref[...] += jnp.concatenate(
        [logit, before_grad, middle_grad, jnp.zeros((side, 5), F32)], axis=1
    )
    tap_grad_ref[...] += dot((gate * dmixed).astype(BF16), top_ref[...])
    stream_grad_ref[...] = ((1.0 - gate) * dmixed).astype(BF16)

    @pl.when(pl.program_id(0) == pl.num_programs(0) - 1)
    def _():
        for turn in range(2):
            bundle_ref[turn] = jnp.concatenate(
                [
                    expand_grad_ref[:, turn * half : (turn + 1) * half],
                    reduce_grad_ref[:, turn * half : (turn + 1) * half],
                    qkv_grad_ref[:, turn * 3 * local : (turn + 1) * 3 * local],
                    out_grad_ref[:, turn * local : (turn + 1) * local],
                    small_ref[...],
                    jnp.zeros((side, bundle_ref.shape[2] - 2 * half - 4 * local - 8), F32),
                ],
                axis=1,
            )
        place = lax.axis_index("dp")
        me = (place % 2, (place // 2) % 2, lax.axis_index("side"))
        fourth = side // 4
        width = tap_grad_ref.shape[1]
        for core in range(2):
            for x in range(2):
                part = 2 * (me[0] ^ core) + (me[1] ^ x)
                lines = pl.ds(pl.multiple_of(part * fourth, 8), fourth)
                for turn in range(2):
                    first = (me[2] ^ turn) * (width // 2)
                    pieces = [
                        tap_grad_ref[lines, pl.ds(pl.multiple_of(first + j * 128, 128), 128)]
                        for j in range(width // 256)
                    ] + [
                        bundle_ref[turn, lines, j * 128 : (j + 1) * 128]
                        for j in range(bundle_ref.shape[2] // 128)
                    ]
                    block = jnp.concatenate(pieces, axis=0).astype(BF16)
                    (send_ref if core else keep_ref)[2 * x + turn] = block


def side_block(index, segment, tap, stream, up, top, table, before, middle, own, other):
    side, tokens = stream.shape
    width = top.shape[1]
    heads = side // SIDE_HEAD
    hidden = own.shape[0] - 2 * side
    bundle = -(-(hidden + 2 * side + 8) // 128) * 128
    block = (side // 4) * (width // 256 + bundle // 128)

    def lanes(height):
        return pl.BlockSpec((height, SEQ), lambda i: (0, i))

    packed = pl.BlockSpec((4, block, 128), lambda i: (0, 0, 0))
    return pl.pallas_call(
        side_kernel,
        grid=(tokens // SEQ,),
        in_specs=[
            pl.BlockSpec(memory_space=pltpu.SMEM),
            whole(segment),
            lanes(side),
            lanes(side),
            lanes(side),
            pl.BlockSpec((SEQ, width), lambda i: (i, 0)),
            *map(whole, (table, before, middle, own, other)),
        ],
        out_specs=[lanes(side), lanes(side), packed, packed],
        out_shape=[
            jax.ShapeDtypeStruct((side, tokens), BF16),
            jax.ShapeDtypeStruct((side, tokens), BF16),
            jax.ShapeDtypeStruct((4, block, 128), BF16),
            jax.ShapeDtypeStruct((4, block, 128), BF16),
        ],
        scratch_shapes=[
            pltpu.VMEM((side, width), F32),
            pltpu.VMEM((side, 3 * side), F32),
            pltpu.VMEM((side, side), F32),
            pltpu.VMEM((side, hidden), F32),
            pltpu.VMEM((side, hidden), F32),
            pltpu.VMEM((side, 8), F32),
            pltpu.VMEM((2, side, bundle), F32),
            pltpu.VMEM((SEQ, SEQ), BF16),
            pltpu.VMEM((3 * side, side), BF16),
            pltpu.VMEM((side, hidden), BF16),
            pltpu.VMEM((side, side), BF16),
            pltpu.VMEM((hidden, side), BF16),
            pltpu.VMEM((heads, SEQ, SEQ), BF16),
            pltpu.VMEM((3 * side, SEQ), F32),
            pltpu.VMEM((heads, 16, SEQ), BF16),
            pltpu.VMEM((heads, 16, SEQ), BF16),
            pltpu.VMEM((heads, ROWS, SEQ), BF16),
            pltpu.VMEM((heads, ROWS, SEQ), F32),
            pltpu.VMEM((side, SEQ), F32),
            pltpu.VMEM((side, SEQ), F32),
            pltpu.VMEM((3 * side, SEQ), F32),
            pltpu.VMEM((8, TILE), F32),
        ],
        compiler_params=pltpu.CompilerParams(vmem_limit_bytes=60 << 20),
        name="side_block",
    )(index, segment, tap, stream, up, top, table, before, middle, own, other)


def unpack_kernel(
    index_ref,
    near_ref,
    far_ref,
    tap_ref,
    gate_ref,
    before_ref,
    middle_ref,
    q_ref,
    k_ref,
    v_ref,
    output_ref,
    expand_ref,
    reduce_ref,
    bundle_ref,
):
    side, width = tap_ref.shape
    half = expand_ref.shape[1]
    local = side // 2
    fourth = side // 4
    taps = width // 256
    tiles = bundle_ref.shape[1] // 128
    block = fourth * (taps + tiles)
    place = lax.axis_index("dp")
    me = (place % 2, (place // 2) % 2, lax.axis_index("side"))
    for core in range(2):
        held = (far_ref if core else near_ref)[...].astype(F32)
        for x in range(2):
            part = 2 * (me[0] ^ core) + (me[1] ^ x)
            lines = pl.ds(pl.multiple_of(part * fourth, 8), fourth)
            for turn in range(2):
                at = 2 * block + x * taps * fourth if turn else x * block
                first = (me[2] ^ turn) * (width // 2)
                for j in range(taps):
                    cols = pl.ds(pl.multiple_of(first + j * 128, 128), 128)
                    tap_ref[lines, cols] = held[at + j * fourth : at + (j + 1) * fourth]
            for j in range(tiles):
                at = x * block + (taps + j) * fourth
                bundle_ref[lines, j * 128 : (j + 1) * 128] = held[at : at + fourth]
    expand_ref[...] = bundle_ref[:, 0:half]
    reduce_ref[...] = jnp.transpose(bundle_ref[:, half : 2 * half])
    rest = jnp.transpose(bundle_ref[:, 2 * half : 2 * half + 4 * local + 8])
    q_ref[...] = rest[0:local]
    k_ref[...] = rest[local : 2 * local]
    v_ref[...] = rest[2 * local : 3 * local]
    output_ref[...] = rest[3 * local : 4 * local]
    small = rest[4 * local : 4 * local + 8]
    picked = lax.broadcasted_iota(jnp.int32, gate_ref.shape, 0) == index_ref[0]
    gate_ref[...] = jnp.where(picked, small[0:1], 0.0)
    before_ref[...] = small[1:2]
    middle_ref[...] = small[2:3]


def exchange(values, dp, side, dp_size):
    pairs = [
        (2 * i + s, 2 * (i ^ dp) + (s ^ side)) for i in range(dp_size) for s in range(2)
    ]
    return lax.ppermute(values, ("dp", "side"), pairs)


def add(*values):
    return functools.reduce(lambda a, b: a + b, [v.astype(F32) for v in values]).astype(BF16)


def shards(
    dp_size,
    backbone_in,
    segment_ids,
    gate_index,
    norm_before,
    norm_middle,
    frozen_query,
    frozen_key,
    frozen_value,
    frozen_output,
    frozen_expand,
    frozen_reduce,
    tap_weight,
    gate_table,
    side_stream,
    ladder_before,
    ladder_middle,
    ladder_query,
    ladder_key,
    ladder_value,
    ladder_output,
    ladder_expand,
    ladder_reduce,
    cotangent,
):
    side = side_stream.shape[1]
    width = tap_weight.shape[0]
    local = side // 2
    half = ladder_expand.shape[1]
    swap = functools.partial(exchange, dp_size=dp_size)
    own = pl.pallas_call(
        pack_kernel,
        out_shape=jax.ShapeDtypeStruct((2 * half + 4 * local, side), BF16),
        name="pack_weights",
    )(ladder_expand, ladder_query.T, ladder_key.T, ladder_value.T, ladder_output, ladder_reduce)
    other = swap(own, 0, 1)
    segment = segment_ids.reshape(-1, 1, SEQ)
    top, tap = frozen_block(
        segment,
        backbone_in,
        norm_before,
        norm_middle,
        frozen_query,
        frozen_key,
        frozen_value,
        frozen_output,
        frozen_expand,
        frozen_reduce,
        tap_weight.T,
    )
    result, stream_grad, keep, send = side_block(
        gate_index,
        segment,
        tap,
        side_stream.T,
        cotangent.T,
        top,
        gate_table,
        ladder_before[None],
        ladder_middle[None],
        own,
        other,
    )
    block = keep.shape[1]
    taps = (side // 4) * (width // 256)
    quad = add(keep, swap(send, 1, 0))
    mine = add(quad[0], swap(quad[1], 0, 1), swap(quad[2], 2, 0), swap(quad[3], 2, 1))
    bit = 4
    while bit < dp_size:
        steps = [bit, 2 * bit, 3 * bit] if 2 * bit < dp_size else [bit]
        mine = add(mine, *[swap(mine, step, 0) for step in steps])
        bit *= len(steps) + 1
    near = jnp.concatenate(
        [mine, swap(mine, 2, 0), swap(mine[:taps], 0, 1), swap(mine[:taps], 2, 1)], axis=0
    )
    far = swap(near, 1, 0)
    shape = functools.partial(jax.ShapeDtypeStruct, dtype=F32)
    tap_sum, gate_sum, before_sum, middle_sum, q_sum, k_sum, v_sum, out_sum, expand_sum, reduce_sum = pl.pallas_call(
        unpack_kernel,
        in_specs=[
            pl.BlockSpec(memory_space=pltpu.SMEM),
            pl.BlockSpec(memory_space=pltpu.VMEM),
            pl.BlockSpec(memory_space=pltpu.VMEM),
        ],
        out_shape=[
            shape((side, width)),
            shape(gate_table.shape),
            shape((1, side)),
            shape((1, side)),
            shape((local, side)),
            shape((local, side)),
            shape((local, side)),
            shape((local, side)),
            shape((side, half)),
            shape((half, side)),
        ],
        scratch_shapes=[pltpu.VMEM((side, (block - taps) // (side // 4) * 128), F32)],
        compiler_params=pltpu.CompilerParams(vmem_limit_bytes=8 << 20),
        name="unpack_gradients",
    )(gate_index, near, far)
    return (
        result.T,
        stream_grad.T,
        tap_sum.T,
        gate_sum,
        before_sum[0],
        middle_sum[0],
        q_sum.T,
        k_sum.T,
        v_sum.T,
        out_sum,
        expand_sum,
        reduce_sum,
    )


def solution(mesh):
    rows = P(("dp", "side"), None)
    placed = (
        rows,
        P("dp"),
        *([P()] * 11),
        rows,
        P(),
        P(),
        P(None, "side"),
        P(None, "side"),
        P(None, "side"),
        P("side", None),
        P(None, "side"),
        P("side", None),
        rows,
    )
    return jax.shard_map(
        functools.partial(shards, mesh.shape["dp"]),
        mesh=mesh,
        in_specs=placed,
        out_specs=(
            rows,
            rows,
            P(),
            P(),
            P(),
            P(),
            P(None, "side"),
            P(None, "side"),
            P(None, "side"),
            P("side", None),
            P(None, "side"),
            P("side", None),
        ),
        check_vma=False,
    )
```

```python
import functools

import jax
import jax.numpy as jnp
from jax import lax
from jax.experimental import pallas as pl
from jax.experimental.pallas import tpu as pltpu
from jax.sharding import PartitionSpec as P

HEAD = 64
SIDE_HEAD = 8
SEQ = 1024
EPS = 1e-06
MASKED = -1e30
LOG2E = 1.4426950408889634
LEAST = 2.0**-64
MOST = 2.0**64
TILE = 1024
ROWS = 96
GROUP = 4
PAIRS = 3

F32 = jnp.float32
BF16 = jnp.bfloat16
NN = (((1,), (0,)), ((), ()))
NT = (((1,), (1,)), ((), ()))
TN = (((0,), (0,)), ((), ()))


def dot(left, right, dims=NN):
    return lax.dot_general(left, right, dims, preferred_element_type=F32)


def gelu_inner(values):
    return 0.7978845608028654 * values * (1.0 + 0.044715 * values * values)


def gelu(values):
    return 0.5 * values * (1.0 + jnp.tanh(gelu_inner(values)))


def gelu_both(values):
    square = values * values
    bend = jnp.tanh(0.7978845608028654 * values * (1.0 + 0.044715 * square))
    half = 0.5 * (1.0 + bend)
    slope = 0.7978845608028654 * (1.0 + 3.0 * 0.044715 * square)
    return values * half, half + 0.5 * values * (1.0 - bend * bend) * slope


def fill_mask(row, mask_ref):
    row = row.astype(F32)
    column = jnp.transpose(jnp.broadcast_to(row, (8, SEQ)))[:, 0:1]
    for step in range(SEQ // 128):
        lanes = slice(step * 128, (step + 1) * 128)
        mask_ref[:, lanes] = jnp.where(column == row[:, lanes], 1.0, 0.0).astype(BF16)


def note_totals(fine_ref, totals):
    fine = jnp.logical_and(totals >= LEAST, totals <= MOST)
    fine_ref[...] = jnp.where(fine, fine_ref[...], 0.0)


def weights_of(scores, mask, careful):
    if not careful:
        return jnp.exp2(scores).astype(BF16) * mask
    allowed = mask.astype(F32) > 0.5
    scores = jnp.where(allowed, scores, MASKED)
    highest = jnp.max(scores, axis=0, keepdims=True)
    return jnp.exp2(scores - highest).astype(BF16)


def frozen_kernel(
    segment_ref,
    x_ref,
    before_ref,
    middle_ref,
    tap_t_ref,
    wq_ref,
    wk_ref,
    wv_ref,
    wo_hbm,
    we_hbm,
    wr_hbm,
    top_ref,
    tap_ref,
    wo_ref,
    we_ref,
    wr_ref,
    copied,
    mask_ref,
    normed_ref,
    q_ref,
    k_ref,
    v_ref,
    ctx_ref,
    fine_ref,
):
    width = x_ref.shape[1]
    heads = width // HEAD
    padded = v_ref.shape[1]

    starting = pl.program_id(0) == 0
    copies = [
        pltpu.make_async_copy(source, target, copied.at[i])
        for i, (source, target) in enumerate(
            (
                (wo_hbm, wo_ref),
                (we_hbm, we_ref),
                (wr_hbm, wr_ref),
            )
        )
    ]

    @pl.when(starting)
    def _():
        for copy in copies:
            copy.start()
        v_ref[:, HEAD:padded] = jnp.ones((heads, padded - HEAD, SEQ), BF16)

    for part in range(2):
        rows = slice(part * SEQ // 2, (part + 1) * SEQ // 2)
        base = x_ref[rows].astype(F32)
        factor = lax.rsqrt(jnp.mean(base * base, axis=-1, keepdims=True) + EPS)
        normed = (base * factor * before_ref[...][None]).astype(BF16)
        normed_ref[rows] = normed
        q_ref[rows] = (dot(normed, wq_ref[...]) * (HEAD**-0.5 * LOG2E)).astype(BF16)
        k_ref[rows] = dot(normed, wk_ref[...]).astype(BF16)
    here = lax.axis_index("side") * pl.num_programs(0) + pl.program_id(0)
    fill_mask(segment_ref[here], mask_ref)
    v = dot(wv_ref[...], normed_ref[...], (((0,), (1,)), ((), ()))).astype(BF16)
    for head in range(heads):
        v_ref[head, 0:HEAD] = v[head * HEAD : (head + 1) * HEAD]

    def attend(careful, tile, together):
        def one(pair, turn, start):
            lanes = pl.ds(start, tile)
            both = pl.ds(pl.multiple_of(pair * 2 * HEAD, 2 * HEAD), 2 * HEAD)
            cols = slice(turn * HEAD, (turn + 1) * HEAD)
            scores = dot(k_ref[:, both][:, cols], q_ref[lanes, both][:, cols], NT)
            probs = weights_of(scores, mask_ref[:, lanes], careful)
            mixed = dot(v_ref[2 * pair + turn], probs)
            if not careful:
                note_totals(fine_ref, mixed[HEAD : HEAD + 8])
            rows = pl.ds(pl.multiple_of((2 * pair + turn) * HEAD, HEAD), HEAD)
            ctx_ref[rows, lanes] = (mixed[0:HEAD] / mixed[HEAD : HEAD + 1]).astype(BF16)

        def step(group, carry):
            for pair in range(together):
                for turn in range(2):
                    for i in range(SEQ // tile):
                        one(group * together + pair, turn, i * tile)
            return carry

        lax.fori_loop(0, heads // 2 // together, step, 0)

    fine_ref[...] = jnp.ones_like(fine_ref)
    attend(False, TILE, PAIRS)
    pl.when(jnp.min(fine_ref[...]) < 0.5)(lambda: attend(True, TILE, 1))

    @pl.when(starting)
    def _():
        for copy in copies:
            copy.wait()

    chunk = 1024
    hidden = we_ref.shape[1]
    piece = 768

    def feed_forward(part, carry):
        rows = pl.ds(pl.multiple_of(part * chunk, chunk), chunk)
        middle = x_ref[rows].astype(F32) + dot(ctx_ref[:, rows], wo_ref[...], TN)
        scale = lax.rsqrt(jnp.mean(middle * middle, axis=-1, keepdims=True) + EPS)
        normed = (middle * scale * middle_ref[...][None]).astype(BF16)
        total = middle
        for j in range(hidden // piece):
            cols = slice(j * piece, (j + 1) * piece)
            expanded = gelu(dot(normed, we_ref[:, cols])).astype(BF16)
            total = total + dot(expanded, wr_ref[cols])
        top = total.astype(BF16)
        top_ref[rows] = top
        tap_ref[:, rows] = dot(tap_t_ref[...], top, NT).astype(BF16)
        return carry

    lax.fori_loop(0, SEQ // chunk, feed_forward, 0)


def whole(array):
    shape = array.shape
    return pl.BlockSpec(shape, lambda i: (0,) * len(shape), pipeline_mode=pl.Buffered(1))


def frozen_block(segment, x, before, middle, wq, wk, wv, wo, we, wr, tap_t):
    tokens, width = x.shape
    heads = width // HEAD
    side = tap_t.shape[0]
    return pl.pallas_call(
        frozen_kernel,
        grid=(tokens // SEQ,),
        in_specs=[
            whole(segment),
            pl.BlockSpec((SEQ, width), lambda i: (i, 0)),
            *map(whole, (before, middle, tap_t, wq, wk, wv)),
            *[pl.BlockSpec(memory_space=pl.ANY)] * 3,
        ],
        out_specs=[
            pl.BlockSpec((SEQ, width), lambda i: (i, 0)),
            pl.BlockSpec((side, SEQ), lambda i: (0, i)),
        ],
        out_shape=[
            jax.ShapeDtypeStruct((tokens, width), BF16),
            jax.ShapeDtypeStruct((side, tokens), BF16),
        ],
        scratch_shapes=[
            *[pltpu.VMEM(w.shape, BF16) for w in (wo, we, wr)],
            pltpu.SemaphoreType.DMA((3,)),
            pltpu.VMEM((SEQ, SEQ), BF16),
            pltpu.VMEM((SEQ, width), BF16),
            pltpu.VMEM((SEQ, width), BF16),
            pltpu.VMEM((SEQ, width), BF16),
            pltpu.VMEM((heads, HEAD + 16, SEQ), BF16),
            pltpu.VMEM((width, SEQ), BF16),
            pltpu.VMEM((8, TILE), F32),
        ],
        compiler_params=pltpu.CompilerParams(vmem_limit_bytes=60 << 20),
        name="frozen_block",
    )(segment, x, before, middle, tap_t, wq, wk, wv, wo, we, wr)


def outer_rows(left, right):
    return [left[e : e + 1] * right for e in range(SIDE_HEAD)]


def pack_kernel(expand_ref, q_ref, k_ref, v_ref, output_ref, reduce_ref, packed_ref):
    side, half = expand_ref.shape
    packed_ref[0:side] = expand_ref[:, 0:side]
    packed_ref[side : 2 * side] = expand_ref[:, side:half]
    at = half
    for ref in (q_ref, k_ref, v_ref, output_ref, reduce_ref):
        packed_ref[at : at + ref.shape[0]] = ref[...]
        at += ref.shape[0]


def side_kernel(
    index_ref,
    segment_ref,
    tap_ref,
    stream_ref,
    up_ref,
    top_ref,
    table_ref,
    before_ref,
    middle_ref,
    own_ref,
    other_ref,
    out_ref,
    stream_grad_ref,
    keep_ref,
    send_ref,
    tap_grad_ref,
    qkv_grad_ref,
    out_grad_ref,
    expand_grad_ref,
    reduce_grad_ref,
    small_ref,
    bundle_ref,
    mask_ref,
    w_ref,
    we_ref,
    wo_ref,
    wr_ref,
    e_ref,
    qkv_ref,
    q16_ref,
    k16_ref,
    rows_ref,
    moment_ref,
    ctx_ref,
    dctx_ref,
    dqkv_ref,
    fine_ref,
):
    side = tap_ref.shape[0]
    heads = side // SIDE_HEAD
    local = side // 2
    hidden = we_ref.shape[1]
    half = hidden // 2

    @pl.when(pl.program_id(0) == 0)
    def _():
        for turn, ref in ((0, own_ref), (1, other_ref)):
            we_ref[:, turn * half : turn * half + side] = ref[0:side]
            we_ref[:, turn * half + side : (turn + 1) * half] = ref[side:half]
            at = half
            w_ref[turn * 3 * local : (turn + 1) * 3 * local] = ref[at : at + 3 * local]
            at += 3 * local
            wo_ref[turn * local : (turn + 1) * local] = ref[at : at + local]
            at += local
            wr_ref[turn * half : (turn + 1) * half] = ref[at : at + half]
        tap_grad_ref[...] = jnp.zeros_like(tap_grad_ref)
        qkv_grad_ref[...] = jnp.zeros_like(qkv_grad_ref)
        out_grad_ref[...] = jnp.zeros_like(out_grad_ref)
        expand_grad_ref[...] = jnp.zeros_like(expand_grad_ref)
        reduce_grad_ref[...] = jnp.zeros_like(reduce_grad_ref)
        small_ref[...] = jnp.zeros_like(small_ref)

    logits = table_ref[pl.ds(index_ref[0], 1), :]
    stacked = jnp.concatenate(
        [
            jnp.broadcast_to(jax.nn.sigmoid(logits), (8, side)),
            jnp.broadcast_to(before_ref[...], (8, side)),
            jnp.broadcast_to(middle_ref[...], (8, side)),
        ],
        axis=0,
    )
    columns = jnp.transpose(stacked)
    gate, before, middle = columns[:, 0:1], columns[:, 8:9], columns[:, 16:17]

    def head_rows(kind, head):
        start = (head // (heads // 2)) * 3 * local + kind * local + (head % (heads // 2)) * SIDE_HEAD
        return pl.ds(pl.multiple_of(start, SIDE_HEAD), SIDE_HEAD)

    tap = tap_ref[...].astype(F32)
    stream = stream_ref[...].astype(F32)
    mixed = gate * tap + (1.0 - gate) * stream
    factor1 = lax.rsqrt(jnp.mean(mixed * mixed, axis=0, keepdims=True) + EPS)
    n1 = (mixed * factor1 * before).astype(BF16)
    qkv_ref[...] = dot(w_ref[...], n1)

    here = lax.axis_index("side") * pl.num_programs(0) + pl.program_id(0)
    fill_mask(segment_ref[here], mask_ref)

    zeros8 = jnp.zeros((SIDE_HEAD, SEQ), F32)
    ones8 = jnp.ones((SIDE_HEAD, SEQ), F32)

    def prepare(head):
        q = qkv_ref[head_rows(0, head)] * (SIDE_HEAD**-0.5 * LOG2E)
        q = q.astype(BF16).astype(F32)
        k = qkv_ref[head_rows(1, head)].astype(BF16).astype(F32)
        v = qkv_ref[head_rows(2, head)].astype(BF16).astype(F32)
        qkv_ref[head_rows(0, head)] = q
        qkv_ref[head_rows(1, head)] = k
        qkv_ref[head_rows(2, head)] = v
        q16_ref[head] = jnp.concatenate([q, zeros8], axis=0).astype(BF16)
        k16_ref[head] = jnp.concatenate([k, zeros8], axis=0).astype(BF16)
        rows = [v, ones8, k, zeros8] + outer_rows(v, k)
        rows_ref[head] = jnp.concatenate(rows, axis=0).astype(BF16)

    def prepare_group(group, carry):
        for turn in range(GROUP):
            prepare(group * GROUP + turn)
        return carry

    lax.fori_loop(0, heads // GROUP, prepare_group, 0)

    def attend(careful, tile):
        def one(head, start):
            at = pl.multiple_of(head * SIDE_HEAD, SIDE_HEAD)
            lanes = pl.ds(start, tile)
            scores = dot(k16_ref[head], q16_ref[head, :, lanes], TN)
            probs = weights_of(scores, mask_ref[:, lanes], careful)
            e_ref[head, lanes, :] = jnp.transpose(probs)
            found = dot(rows_ref[head], probs)
            if not careful:
                note_totals(fine_ref, found[8:16])
            inverse = 1.0 / found[8:16]
            ctx_ref[pl.ds(at, SIDE_HEAD), lanes] = found[0:8] * inverse
            moment_ref[head, 8:16, lanes] = inverse
            moment_ref[head, 16:24, lanes] = found[16:24] * inverse
            for e in range(SIDE_HEAD):
                low = 32 + e * SIDE_HEAD
                moment_ref[head, low : low + 8, lanes] = found[low : low + 8] * inverse

        together = 1 if careful else GROUP

        def step(group, carry):
            for turn in range(together):
                for i in range(SEQ // tile):
                    one(group * together + turn, i * tile)
            return carry

        lax.fori_loop(0, heads // together, step, 0)

    fine_ref[...] = jnp.ones_like(fine_ref)
    attend(False, TILE)
    pl.when(jnp.min(fine_ref[...]) < 0.5)(lambda: attend(True, TILE))

    ctx = ctx_ref[...].astype(BF16)
    res1 = mixed + dot(wo_ref[...], ctx, TN)
    factor2 = lax.rsqrt(jnp.mean(res1 * res1, axis=0, keepdims=True) + EPS)
    z = res1 * factor2
    n2 = (z * middle).astype(BF16)
    pre = dot(we_ref[...], n2, TN)
    act, slope = gelu_both(pre)
    act = act.astype(BF16)
    result = res1 + dot(wr_ref[...], act, TN)
    out_ref[...] = result.astype(BF16)

    low_up = up_ref[...]
    up = low_up.astype(F32)
    reduce_grad_ref[...] += dot(low_up, act, NT)
    dpre = (dot(wr_ref[...], low_up) * slope).astype(BF16)
    expand_grad_ref[...] += dot(n2, dpre, NT)
    dn2 = dot(we_ref[...], dpre)
    middle_grad = jnp.sum(dn2 * z, axis=1, keepdims=True)
    u = dn2 * middle
    spread = jnp.mean(u * res1, axis=0, keepdims=True)
    dres1 = up + factor2 * u - z * (factor2 * factor2 * spread)
    low_dres = dres1.astype(BF16)
    out_grad_ref[...] += dot(low_dres, ctx, NT)
    dctx_ref[...] = dot(wo_ref[...], low_dres).astype(BF16).astype(F32)

    def prepare_back(head):
        at = pl.multiple_of(head * SIDE_HEAD, SIDE_HEAD)
        q = qkv_ref[head_rows(0, head)]
        dctx = dctx_ref[pl.ds(at, SIDE_HEAD)]
        inverse = moment_ref[head, 8:16]
        inner = jnp.sum(dctx * ctx_ref[pl.ds(at, SIDE_HEAD)], axis=0, keepdims=True)
        dq = -inner * moment_ref[head, 16:24]
        for e in range(SIDE_HEAD):
            low = 32 + e * SIDE_HEAD
            dq = dq + dctx[e : e + 1] * moment_ref[head, low : low + 8]
        dqkv_ref[head_rows(0, head)] = dq * SIDE_HEAD**-0.5
        scaled = dctx * inverse
        rows = [scaled, zeros8, (inner * inverse) * q, zeros8] + outer_rows(scaled, q)
        rows_ref[head] = jnp.concatenate(rows, axis=0).astype(BF16)

    def prepare_back_group(group, carry):
        for turn in range(GROUP):
            prepare_back(group * GROUP + turn)
        return carry

    lax.fori_loop(0, heads // GROUP, prepare_back_group, 0)

    def back(head):
        found = dot(rows_ref[head], e_ref[head])
        v = qkv_ref[head_rows(2, head)]
        dk = -found[16:24]
        for e in range(SIDE_HEAD):
            low = 32 + e * SIDE_HEAD
            dk = dk + v[e : e + 1] * found[low : low + 8]
        dqkv_ref[head_rows(1, head)] = dk * (1.0 / LOG2E)
        dqkv_ref[head_rows(2, head)] = found[0:8]

    def back_group(group, carry):
        for turn in range(GROUP):
            back(group * GROUP + turn)
        return carry

    lax.fori_loop(0, heads // GROUP, back_group, 0)

    dqkv = dqkv_ref[...].astype(BF16)
    qkv_grad_ref[...] += dot(n1, dqkv, NT)
    dn1 = dot(w_ref[...], dqkv, TN)
    unit = mixed * factor1
    before_grad = jnp.sum(dn1 * unit, axis=1, keepdims=True)
    u = dn1 * before
    spread = jnp.mean(u * mixed, axis=0, keepdims=True)
    dmixed = dres1 + factor1 * u - unit * (factor1 * factor1 * spread)
    logit = jnp.sum(dmixed * (tap - stream), axis=1, keepdims=True) * gate * (1.0 - gate)
    small_ref[...] += jnp.concatenate(
        [logit, before_grad, middle_grad, jnp.zeros((side, 5), F32)], axis=1
    )
    tap_grad_ref[...] += dot((gate * dmixed).astype(BF16), top_ref[...])
    stream_grad_ref[...] = ((1.0 - gate) * dmixed).astype(BF16)

    @pl.when(pl.program_id(0) == pl.num_programs(0) - 1)
    def _():
        for turn in range(2):
            bundle_ref[turn] = jnp.concatenate(
                [
                    expand_grad_ref[:, turn * half : (turn + 1) * half],
                    reduce_grad_ref[:, turn * half : (turn + 1) * half],
                    qkv_grad_ref[:, turn * 3 * local : (turn + 1) * 3 * local],
                    out_grad_ref[:, turn * local : (turn + 1) * local],
                    small_ref[...],
                    jnp.zeros((side, bundle_ref.shape[2] - 2 * half - 4 * local - 8), F32),
                ],
                axis=1,
            )
        place = lax.axis_index("dp")
        me = (place % 2, (place // 2) % 2, lax.axis_index("side"))
        fourth = side // 4
        width = tap_grad_ref.shape[1]
        for core in range(2):
            for x in range(2):
                part = 2 * (me[0] ^ core) + (me[1] ^ x)
                lines = pl.ds(pl.multiple_of(part * fourth, 8), fourth)
                for turn in range(2):
                    first = (me[2] ^ turn) * (width // 2)
                    pieces = [
                        tap_grad_ref[lines, pl.ds(pl.multiple_of(first + j * 128, 128), 128)]
                        for j in range(width // 256)
                    ] + [
                        bundle_ref[turn, lines, j * 128 : (j + 1) * 128]
                        for j in range(bundle_ref.shape[2] // 128)
                    ]
                    block = jnp.concatenate(pieces, axis=0).astype(BF16)
                    (send_ref if core else keep_ref)[2 * x + turn] = block


def side_block(index, segment, tap, stream, up, top, table, before, middle, own, other):
    side, tokens = stream.shape
    width = top.shape[1]
    heads = side // SIDE_HEAD
    hidden = own.shape[0] - 2 * side
    bundle = -(-(hidden + 2 * side + 8) // 128) * 128
    block = (side // 4) * (width // 256 + bundle // 128)

    def lanes(height):
        return pl.BlockSpec((height, SEQ), lambda i: (0, i))

    packed = pl.BlockSpec((4, block, 128), lambda i: (0, 0, 0))
    return pl.pallas_call(
        side_kernel,
        grid=(tokens // SEQ,),
        in_specs=[
            pl.BlockSpec(memory_space=pltpu.SMEM),
            whole(segment),
            lanes(side),
            lanes(side),
            lanes(side),
            pl.BlockSpec((SEQ, width), lambda i: (i, 0)),
            *map(whole, (table, before, middle, own, other)),
        ],
        out_specs=[lanes(side), lanes(side), packed, packed],
        out_shape=[
            jax.ShapeDtypeStruct((side, tokens), BF16),
            jax.ShapeDtypeStruct((side, tokens), BF16),
            jax.ShapeDtypeStruct((4, block, 128), BF16),
            jax.ShapeDtypeStruct((4, block, 128), BF16),
        ],
        scratch_shapes=[
            pltpu.VMEM((side, width), F32),
            pltpu.VMEM((side, 3 * side), F32),
            pltpu.VMEM((side, side), F32),
            pltpu.VMEM((side, hidden), F32),
            pltpu.VMEM((side, hidden), F32),
            pltpu.VMEM((side, 8), F32),
            pltpu.VMEM((2, side, bundle), F32),
            pltpu.VMEM((SEQ, SEQ), BF16),
            pltpu.VMEM((3 * side, side), BF16),
            pltpu.VMEM((side, hidden), BF16),
            pltpu.VMEM((side, side), BF16),
            pltpu.VMEM((hidden, side), BF16),
            pltpu.VMEM((heads, SEQ, SEQ), BF16),
            pltpu.VMEM((3 * side, SEQ), F32),
            pltpu.VMEM((heads, 16, SEQ), BF16),
            pltpu.VMEM((heads, 16, SEQ), BF16),
            pltpu.VMEM((heads, ROWS, SEQ), BF16),
            pltpu.VMEM((heads, ROWS, SEQ), F32),
            pltpu.VMEM((side, SEQ), F32),
            pltpu.VMEM((side, SEQ), F32),
            pltpu.VMEM((3 * side, SEQ), F32),
            pltpu.VMEM((8, TILE), F32),
        ],
        compiler_params=pltpu.CompilerParams(vmem_limit_bytes=60 << 20),
        name="side_block",
    )(index, segment, tap, stream, up, top, table, before, middle, own, other)


def unpack_kernel(
    index_ref,
    near_ref,
    far_ref,
    tap_ref,
    gate_ref,
    before_ref,
    middle_ref,
    q_ref,
    k_ref,
    v_ref,
    output_ref,
    expand_ref,
    reduce_ref,
    bundle_ref,
):
    side, width = tap_ref.shape
    half = expand_ref.shape[1]
    local = side // 2
    fourth = side // 4
    taps = width // 256
    tiles = bundle_ref.shape[1] // 128
    block = fourth * (taps + tiles)
    place = lax.axis_index("dp")
    me = (place % 2, (place // 2) % 2, lax.axis_index("side"))
    for core in range(2):
        held = (far_ref if core else near_ref)[...].astype(F32)
        for x in range(2):
            part = 2 * (me[0] ^ core) + (me[1] ^ x)
            lines = pl.ds(pl.multiple_of(part * fourth, 8), fourth)
            for turn in range(2):
                at = 2 * block + x * taps * fourth if turn else x * block
                first = (me[2] ^ turn) * (width // 2)
                for j in range(taps):
                    cols = pl.ds(pl.multiple_of(first + j * 128, 128), 128)
                    tap_ref[lines, cols] = held[at + j * fourth : at + (j + 1) * fourth]
            for j in range(tiles):
                at = x * block + (taps + j) * fourth
                bundle_ref[lines, j * 128 : (j + 1) * 128] = held[at : at + fourth]
    expand_ref[...] = bundle_ref[:, 0:half]
    reduce_ref[...] = jnp.transpose(bundle_ref[:, half : 2 * half])
    rest = jnp.transpose(bundle_ref[:, 2 * half : 2 * half + 4 * local + 8])
    q_ref[...] = rest[0:local]
    k_ref[...] = rest[local : 2 * local]
    v_ref[...] = rest[2 * local : 3 * local]
    output_ref[...] = rest[3 * local : 4 * local]
    small = rest[4 * local : 4 * local + 8]
    picked = lax.broadcasted_iota(jnp.int32, gate_ref.shape, 0) == index_ref[0]
    gate_ref[...] = jnp.where(picked, small[0:1], 0.0)
    before_ref[...] = small[1:2]
    middle_ref[...] = small[2:3]


def exchange(values, dp, side, dp_size):
    pairs = [
        (2 * i + s, 2 * (i ^ dp) + (s ^ side)) for i in range(dp_size) for s in range(2)
    ]
    return lax.ppermute(values, ("dp", "side"), pairs)


def add(*values):
    return functools.reduce(lambda a, b: a + b, [v.astype(F32) for v in values]).astype(BF16)


def shards(
    dp_size,
    backbone_in,
    segment_ids,
    gate_index,
    norm_before,
    norm_middle,
    frozen_query,
    frozen_key,
    frozen_value,
    frozen_output,
    frozen_expand,
    frozen_reduce,
    tap_weight,
    gate_table,
    side_stream,
    ladder_before,
    ladder_middle,
    ladder_query,
    ladder_key,
    ladder_value,
    ladder_output,
    ladder_expand,
    ladder_reduce,
    cotangent,
):
    side = side_stream.shape[1]
    width = tap_weight.shape[0]
    local = side // 2
    half = ladder_expand.shape[1]
    swap = functools.partial(exchange, dp_size=dp_size)
    own = pl.pallas_call(
        pack_kernel,
        out_shape=jax.ShapeDtypeStruct((2 * half + 4 * local, side), BF16),
        name="pack_weights",
    )(ladder_expand, ladder_query.T, ladder_key.T, ladder_value.T, ladder_output, ladder_reduce)
    other = swap(own, 0, 1)
    segment = segment_ids.reshape(-1, 1, SEQ)
    top, tap = frozen_block(
        segment,
        backbone_in,
        norm_before,
        norm_middle,
        frozen_query,
        frozen_key,
        frozen_value,
        frozen_output,
        frozen_expand,
        frozen_reduce,
        tap_weight.T,
    )
    result, stream_grad, keep, send = side_block(
        gate_index,
        segment,
        tap,
        side_stream.T,
        cotangent.T,
        top,
        gate_table,
        ladder_before[None],
        ladder_middle[None],
        own,
        other,
    )
    block = keep.shape[1]
    taps = (side // 4) * (width // 256)
    quad = add(keep, swap(send, 1, 0))
    mine = add(quad[0], swap(quad[1], 0, 1), swap(quad[2], 2, 0), swap(quad[3], 2, 1))
    bit = 4
    while bit < dp_size:
        steps = [bit, 2 * bit, 3 * bit] if 2 * bit < dp_size else [bit]
        mine = add(mine, *[swap(mine, step, 0) for step in steps])
        bit *= len(steps) + 1
    near = jnp.concatenate(
        [mine, swap(mine, 2, 0), swap(mine[:taps], 0, 1), swap(mine[:taps], 2, 1)], axis=0
    )
    far = swap(near, 1, 0)
    shape = functools.partial(jax.ShapeDtypeStruct, dtype=F32)
    tap_sum, gate_sum, before_sum, middle_sum, q_sum, k_sum, v_sum, out_sum, expand_sum, reduce_sum = pl.pallas_call(
        unpack_kernel,
        in_specs=[
            pl.BlockSpec(memory_space=pltpu.SMEM),
            pl.BlockSpec(memory_space=pltpu.VMEM),
            pl.BlockSpec(memory_space=pltpu.VMEM),
        ],
        out_shape=[
            shape((side, width)),
            shape(gate_table.shape),
            shape((1, side)),
            shape((1, side)),
            shape((local, side)),
            shape((local, side)),
            shape((local, side)),
            shape((local, side)),
            shape((side, half)),
            shape((half, side)),
        ],
        scratch_shapes=[pltpu.VMEM((side, (block - taps) // (side // 4) * 128), F32)],
        compiler_params=pltpu.CompilerParams(vmem_limit_bytes=8 << 20),
        name="unpack_gradients",
    )(gate_index, near, far)
    return (
        result.T,
        stream_grad.T,
        tap_sum.T,
        gate_sum,
        before_sum[0],
        middle_sum[0],
        q_sum.T,
        k_sum.T,
        v_sum.T,
        out_sum,
        expand_sum,
        reduce_sum,
    )


def solution(mesh):
    rows = P(("dp", "side"), None)
    placed = (
        rows,
        P("dp"),
        *([P()] * 11),
        rows,
        P(),
        P(),
        P(None, "side"),
        P(None, "side"),
        P(None, "side"),
        P("side", None),
        P(None, "side"),
        P("side", None),
        rows,
    )
    return jax.shard_map(
        functools.partial(shards, mesh.shape["dp"]),
        mesh=mesh,
        in_specs=placed,
        out_specs=(
            rows,
            rows,
            P(),
            P(),
            P(),
            P(),
            P(None, "side"),
            P(None, "side"),
            P(None, "side"),
            P("side", None),
            P(None, "side"),
            P("side", None),
        ),
        check_vma=False,
    )
```

```python
import functools

import jax
import jax.numpy as jnp
from jax import lax
from jax.experimental import pallas as pl
from jax.experimental.pallas import tpu as pltpu
from jax.sharding import PartitionSpec as P

HEAD = 64
SIDE_HEAD = 8
SEQ = 1024
EPS = 1e-06
MASKED = -1e30
LOG2E = 1.4426950408889634
LEAST = 2.0**-64
MOST = 2.0**64
TILE = 1024
ROWS = 96
GROUP = 4
PAIRS = 3

F32 = jnp.float32
BF16 = jnp.bfloat16
NN = (((1,), (0,)), ((), ()))
NT = (((1,), (1,)), ((), ()))
TN = (((0,), (0,)), ((), ()))


def dot(left, right, dims=NN):
    return lax.dot_general(left, right, dims, preferred_element_type=F32)


def gelu_inner(values):
    return 0.7978845608028654 * values * (1.0 + 0.044715 * values * values)


def gelu(values):
    return 0.5 * values * (1.0 + jnp.tanh(gelu_inner(values)))


def gelu_both(values):
    square = values * values
    bend = jnp.tanh(0.7978845608028654 * values * (1.0 + 0.044715 * square))
    half = 0.5 * (1.0 + bend)
    slope = 0.7978845608028654 * (1.0 + 3.0 * 0.044715 * square)
    return values * half, half + 0.5 * values * (1.0 - bend * bend) * slope


def fill_mask(row, mask_ref):
    row = row.astype(F32)
    column = jnp.transpose(jnp.broadcast_to(row, (8, SEQ)))[:, 0:1]
    for step in range(SEQ // 128):
        lanes = slice(step * 128, (step + 1) * 128)
        mask_ref[:, lanes] = jnp.where(column == row[:, lanes], 1.0, 0.0).astype(BF16)


def note_totals(fine_ref, totals):
    fine = jnp.logical_and(totals >= LEAST, totals <= MOST)
    fine_ref[...] = jnp.where(fine, fine_ref[...], 0.0)


def weights_of(scores, mask, careful):
    if not careful:
        return jnp.exp2(scores).astype(BF16) * mask
    allowed = mask.astype(F32) > 0.5
    scores = jnp.where(allowed, scores, MASKED)
    highest = jnp.max(scores, axis=0, keepdims=True)
    return jnp.exp2(scores - highest).astype(BF16)


def frozen_kernel(
    segment_ref,
    x_ref,
    before_ref,
    middle_ref,
    tap_t_ref,
    wq_ref,
    wk_ref,
    wv_ref,
    wo_hbm,
    we_hbm,
    wr_hbm,
    top_ref,
    tap_ref,
    wo_ref,
    we_ref,
    wr_ref,
    copied,
    mask_ref,
    normed_ref,
    q_ref,
    k_ref,
    v_ref,
    ctx_ref,
    fine_ref,
):
    width = x_ref.shape[1]
    heads = width // HEAD
    padded = v_ref.shape[1]

    starting = pl.program_id(0) == 0
    copies = [
        pltpu.make_async_copy(source, target, copied.at[i])
        for i, (source, target) in enumerate(
            (
                (wo_hbm, wo_ref),
                (we_hbm, we_ref),
                (wr_hbm, wr_ref),
            )
        )
    ]

    @pl.when(starting)
    def _():
        for copy in copies:
            copy.start()
        v_ref[:, HEAD:padded] = jnp.ones((heads, padded - HEAD, SEQ), BF16)

    for part in range(2):
        rows = slice(part * SEQ // 2, (part + 1) * SEQ // 2)
        base = x_ref[rows].astype(F32)
        factor = lax.rsqrt(jnp.mean(base * base, axis=-1, keepdims=True) + EPS)
        normed = (base * factor * before_ref[...][None]).astype(BF16)
        normed_ref[rows] = normed
        q_ref[rows] = (dot(normed, wq_ref[...]) * (HEAD**-0.5 * LOG2E)).astype(BF16)
        k_ref[rows] = dot(normed, wk_ref[...]).astype(BF16)
    here = lax.axis_index("side") * pl.num_programs(0) + pl.program_id(0)
    fill_mask(segment_ref[here], mask_ref)
    v = dot(wv_ref[...], normed_ref[...], (((0,), (1,)), ((), ()))).astype(BF16)
    for head in range(heads):
        v_ref[head, 0:HEAD] = v[head * HEAD : (head + 1) * HEAD]

    def attend(careful, tile, together):
        def one(pair, turn, start):
            lanes = pl.ds(start, tile)
            both = pl.ds(pl.multiple_of(pair * 2 * HEAD, 2 * HEAD), 2 * HEAD)
            cols = slice(turn * HEAD, (turn + 1) * HEAD)
            scores = dot(k_ref[:, both][:, cols], q_ref[lanes, both][:, cols], NT)
            probs = weights_of(scores, mask_ref[:, lanes], careful)
            mixed = dot(v_ref[2 * pair + turn], probs)
            if not careful:
                note_totals(fine_ref, mixed[HEAD : HEAD + 8])
            rows = pl.ds(pl.multiple_of((2 * pair + turn) * HEAD, HEAD), HEAD)
            ctx_ref[rows, lanes] = (mixed[0:HEAD] / mixed[HEAD : HEAD + 1]).astype(BF16)

        def step(group, carry):
            for pair in range(together):
                for turn in range(2):
                    for i in range(SEQ // tile):
                        one(group * together + pair, turn, i * tile)
            return carry

        lax.fori_loop(0, heads // 2 // together, step, 0)

    fine_ref[...] = jnp.ones_like(fine_ref)
    attend(False, TILE, PAIRS)
    pl.when(jnp.min(fine_ref[...]) < 0.5)(lambda: attend(True, TILE, 1))

    @pl.when(starting)
    def _():
        for copy in copies:
            copy.wait()

    chunk = 1024
    hidden = we_ref.shape[1]
    piece = 768

    def feed_forward(part, carry):
        rows = pl.ds(pl.multiple_of(part * chunk, chunk), chunk)
        middle = x_ref[rows].astype(F32) + dot(ctx_ref[:, rows], wo_ref[...], TN)
        scale = lax.rsqrt(jnp.mean(middle * middle, axis=-1, keepdims=True) + EPS)
        normed = (middle * scale * middle_ref[...][None]).astype(BF16)
        total = middle
        for j in range(hidden // piece):
            cols = slice(j * piece, (j + 1) * piece)
            expanded = gelu(dot(normed, we_ref[:, cols])).astype(BF16)
            total = total + dot(expanded, wr_ref[cols])
        top = total.astype(BF16)
        top_ref[rows] = top
        tap_ref[:, rows] = dot(tap_t_ref[...], top, NT).astype(BF16)
        return carry

    lax.fori_loop(0, SEQ // chunk, feed_forward, 0)


def whole(array):
    shape = array.shape
    return pl.BlockSpec(shape, lambda i: (0,) * len(shape), pipeline_mode=pl.Buffered(1))


def frozen_block(segment, x, before, middle, wq, wk, wv, wo, we, wr, tap_t):
    tokens, width = x.shape
    heads = width // HEAD
    side = tap_t.shape[0]
    return pl.pallas_call(
        frozen_kernel,
        grid=(tokens // SEQ,),
        in_specs=[
            whole(segment),
            pl.BlockSpec((SEQ, width), lambda i: (i, 0)),
            *map(whole, (before, middle, tap_t, wq, wk, wv)),
            *[pl.BlockSpec(memory_space=pl.ANY)] * 3,
        ],
        out_specs=[
            pl.BlockSpec((SEQ, width), lambda i: (i, 0)),
            pl.BlockSpec((side, SEQ), lambda i: (0, i)),
        ],
        out_shape=[
            jax.ShapeDtypeStruct((tokens, width), BF16),
            jax.ShapeDtypeStruct((side, tokens), BF16),
        ],
        scratch_shapes=[
            *[pltpu.VMEM(w.shape, BF16) for w in (wo, we, wr)],
            pltpu.SemaphoreType.DMA((3,)),
            pltpu.VMEM((SEQ, SEQ), BF16),
            pltpu.VMEM((SEQ, width), BF16),
            pltpu.VMEM((SEQ, width), BF16),
            pltpu.VMEM((SEQ, width), BF16),
            pltpu.VMEM((heads, HEAD + 16, SEQ), BF16),
            pltpu.VMEM((width, SEQ), BF16),
            pltpu.VMEM((8, TILE), F32),
        ],
        compiler_params=pltpu.CompilerParams(vmem_limit_bytes=60 << 20),
        name="frozen_block",
    )(segment, x, before, middle, tap_t, wq, wk, wv, wo, we, wr)


def outer_rows(left, right):
    return [left[e : e + 1] * right for e in range(SIDE_HEAD)]


def pack_kernel(expand_ref, q_ref, k_ref, v_ref, output_ref, reduce_ref, packed_ref):
    side, half = expand_ref.shape
    packed_ref[0:side] = expand_ref[:, 0:side]
    packed_ref[side : 2 * side] = expand_ref[:, side:half]
    at = half
    for ref in (q_ref, k_ref, v_ref, output_ref, reduce_ref):
        packed_ref[at : at + ref.shape[0]] = ref[...]
        at += ref.shape[0]


def side_kernel(
    index_ref,
    segment_ref,
    tap_ref,
    stream_ref,
    up_ref,
    top_hbm,
    table_ref,
    before_ref,
    middle_ref,
    own_ref,
    other_ref,
    out_ref,
    stream_grad_ref,
    keep_ref,
    send_ref,
    tap_grad_ref,
    qkv_grad_ref,
    out_grad_ref,
    expand_grad_ref,
    reduce_grad_ref,
    small_ref,
    bundle_ref,
    mask_ref,
    w_ref,
    we_ref,
    wo_ref,
    wr_ref,
    e_ref,
    qkv_ref,
    q16_ref,
    k16_ref,
    rows_ref,
    moment_ref,
    ctx_ref,
    dctx_ref,
    dqkv_ref,
    fine_ref,
    top_ref,
    copied,
):
    side = tap_ref.shape[0]
    heads = side // SIDE_HEAD
    local = side // 2
    hidden = we_ref.shape[1]
    half = hidden // 2

    @pl.when(pl.program_id(0) == 0)
    def _():
        for turn, ref in ((0, own_ref), (1, other_ref)):
            we_ref[:, turn * half : turn * half + side] = ref[0:side]
            we_ref[:, turn * half + side : (turn + 1) * half] = ref[side:half]
            at = half
            w_ref[turn * 3 * local : (turn + 1) * 3 * local] = ref[at : at + 3 * local]
            at += 3 * local
            wo_ref[turn * local : (turn + 1) * local] = ref[at : at + local]
            at += local
            wr_ref[turn * half : (turn + 1) * half] = ref[at : at + half]
        tap_grad_ref[...] = jnp.zeros_like(tap_grad_ref)
        qkv_grad_ref[...] = jnp.zeros_like(qkv_grad_ref)
        out_grad_ref[...] = jnp.zeros_like(out_grad_ref)
        expand_grad_ref[...] = jnp.zeros_like(expand_grad_ref)
        reduce_grad_ref[...] = jnp.zeros_like(reduce_grad_ref)
        small_ref[...] = jnp.zeros_like(small_ref)

    logits = table_ref[pl.ds(index_ref[0], 1), :]
    stacked = jnp.concatenate(
        [
            jnp.broadcast_to(jax.nn.sigmoid(logits), (8, side)),
            jnp.broadcast_to(before_ref[...], (8, side)),
            jnp.broadcast_to(middle_ref[...], (8, side)),
        ],
        axis=0,
    )
    columns = jnp.transpose(stacked)
    gate, before, middle = columns[:, 0:1], columns[:, 8:9], columns[:, 16:17]

    def head_rows(kind, head):
        start = (head // (heads // 2)) * 3 * local + kind * local + (head % (heads // 2)) * SIDE_HEAD
        return pl.ds(pl.multiple_of(start, SIDE_HEAD), SIDE_HEAD)

    tap = tap_ref[...].astype(F32)
    stream = stream_ref[...].astype(F32)
    mixed = gate * tap + (1.0 - gate) * stream
    factor1 = lax.rsqrt(jnp.mean(mixed * mixed, axis=0, keepdims=True) + EPS)
    n1 = (mixed * factor1 * before).astype(BF16)
    qkv_ref[...] = dot(w_ref[...], n1)

    here = lax.axis_index("side") * pl.num_programs(0) + pl.program_id(0)
    fill_mask(segment_ref[here], mask_ref)

    zeros8 = jnp.zeros((SIDE_HEAD, SEQ), F32)
    ones8 = jnp.ones((SIDE_HEAD, SEQ), F32)

    def prepare(head):
        q = qkv_ref[head_rows(0, head)] * (SIDE_HEAD**-0.5 * LOG2E)
        q = q.astype(BF16).astype(F32)
        k = qkv_ref[head_rows(1, head)].astype(BF16).astype(F32)
        v = qkv_ref[head_rows(2, head)].astype(BF16).astype(F32)
        qkv_ref[head_rows(0, head)] = q
        qkv_ref[head_rows(1, head)] = k
        qkv_ref[head_rows(2, head)] = v
        q16_ref[head] = jnp.concatenate([q, zeros8], axis=0).astype(BF16)
        k16_ref[head] = jnp.concatenate([k, zeros8], axis=0).astype(BF16)
        rows = [v, ones8, k, zeros8] + outer_rows(v, k)
        rows_ref[head] = jnp.concatenate(rows, axis=0).astype(BF16)

    def prepare_group(group, carry):
        for turn in range(GROUP):
            prepare(group * GROUP + turn)
        return carry

    lax.fori_loop(0, heads // GROUP, prepare_group, 0)

    def attend(careful, tile):
        def one(head, start):
            at = pl.multiple_of(head * SIDE_HEAD, SIDE_HEAD)
            lanes = pl.ds(start, tile)
            scores = dot(k16_ref[head], q16_ref[head, :, lanes], TN)
            probs = weights_of(scores, mask_ref[:, lanes], careful)
            e_ref[head, lanes, :] = jnp.transpose(probs)
            found = dot(rows_ref[head], probs)
            if not careful:
                note_totals(fine_ref, found[8:16])
            inverse = 1.0 / found[8:16]
            ctx_ref[pl.ds(at, SIDE_HEAD), lanes] = found[0:8] * inverse
            moment_ref[head, 8:16, lanes] = inverse
            moment_ref[head, 16:24, lanes] = found[16:24] * inverse
            for e in range(SIDE_HEAD):
                low = 32 + e * SIDE_HEAD
                moment_ref[head, low : low + 8, lanes] = found[low : low + 8] * inverse

        together = 1 if careful else GROUP

        def step(group, carry):
            for turn in range(together):
                for i in range(SEQ // tile):
                    one(group * together + turn, i * tile)
            return carry

        lax.fori_loop(0, heads // together, step, 0)

    lines = pl.ds(pl.multiple_of(pl.program_id(0) * SEQ, SEQ), SEQ)
    top_copy = pltpu.make_async_copy(top_hbm.at[lines], top_ref, copied)
    top_copy.start()
    fine_ref[...] = jnp.ones_like(fine_ref)
    attend(False, TILE)
    pl.when(jnp.min(fine_ref[...]) < 0.5)(lambda: attend(True, TILE))

    ctx = ctx_ref[...].astype(BF16)
    res1 = mixed + dot(wo_ref[...], ctx, TN)
    factor2 = lax.rsqrt(jnp.mean(res1 * res1, axis=0, keepdims=True) + EPS)
    z = res1 * factor2
    n2 = (z * middle).astype(BF16)
    pre = dot(we_ref[...], n2, TN)
    act, slope = gelu_both(pre)
    act = act.astype(BF16)
    result = res1 + dot(wr_ref[...], act, TN)
    out_ref[...] = result.astype(BF16)

    low_up = up_ref[...]
    up = low_up.astype(F32)
    reduce_grad_ref[...] += dot(low_up, act, NT)
    dpre = (dot(wr_ref[...], low_up) * slope).astype(BF16)
    expand_grad_ref[...] += dot(n2, dpre, NT)
    dn2 = dot(we_ref[...], dpre)
    middle_grad = jnp.sum(dn2 * z, axis=1, keepdims=True)
    u = dn2 * middle
    spread = jnp.mean(u * res1, axis=0, keepdims=True)
    dres1 = up + factor2 * u - z * (factor2 * factor2 * spread)
    low_dres = dres1.astype(BF16)
    out_grad_ref[...] += dot(low_dres, ctx, NT)
    dctx_ref[...] = dot(wo_ref[...], low_dres).astype(BF16).astype(F32)

    def prepare_back(head):
        at = pl.multiple_of(head * SIDE_HEAD, SIDE_HEAD)
        q = qkv_ref[head_rows(0, head)]
        dctx = dctx_ref[pl.ds(at, SIDE_HEAD)]
        inverse = moment_ref[head, 8:16]
        inner = jnp.sum(dctx * ctx_ref[pl.ds(at, SIDE_HEAD)], axis=0, keepdims=True)
        dq = -inner * moment_ref[head, 16:24]
        for e in range(SIDE_HEAD):
            low = 32 + e * SIDE_HEAD
            dq = dq + dctx[e : e + 1] * moment_ref[head, low : low + 8]
        dqkv_ref[head_rows(0, head)] = dq * SIDE_HEAD**-0.5
        scaled = dctx * inverse
        rows = [scaled, zeros8, (inner * inverse) * q, zeros8] + outer_rows(scaled, q)
        rows_ref[head] = jnp.concatenate(rows, axis=0).astype(BF16)

    def prepare_back_group(group, carry):
        for turn in range(GROUP):
            prepare_back(group * GROUP + turn)
        return carry

    lax.fori_loop(0, heads // GROUP, prepare_back_group, 0)

    def back(head):
        found = dot(rows_ref[head], e_ref[head])
        v = qkv_ref[head_rows(2, head)]
        dk = -found[16:24]
        for e in range(SIDE_HEAD):
            low = 32 + e * SIDE_HEAD
            dk = dk + v[e : e + 1] * found[low : low + 8]
        dqkv_ref[head_rows(1, head)] = dk * (1.0 / LOG2E)
        dqkv_ref[head_rows(2, head)] = found[0:8]

    def back_group(group, carry):
        for turn in range(GROUP):
            back(group * GROUP + turn)
        return carry

    lax.fori_loop(0, heads // GROUP, back_group, 0)

    top_copy.wait()
    dqkv = dqkv_ref[...].astype(BF16)
    qkv_grad_ref[...] += dot(n1, dqkv, NT)
    dn1 = dot(w_ref[...], dqkv, TN)
    unit = mixed * factor1
    before_grad = jnp.sum(dn1 * unit, axis=1, keepdims=True)
    u = dn1 * before
    spread = jnp.mean(u * mixed, axis=0, keepdims=True)
    dmixed = dres1 + factor1 * u - unit * (factor1 * factor1 * spread)
    logit = jnp.sum(dmixed * (tap - stream), axis=1, keepdims=True) * gate * (1.0 - gate)
    small_ref[...] += jnp.concatenate(
        [logit, before_grad, middle_grad, jnp.zeros((side, 5), F32)], axis=1
    )
    tap_grad_ref[...] += dot((gate * dmixed).astype(BF16), top_ref[...])
    stream_grad_ref[...] = ((1.0 - gate) * dmixed).astype(BF16)

    @pl.when(pl.program_id(0) == pl.num_programs(0) - 1)
    def _():
        for turn in range(2):
            bundle_ref[turn] = jnp.concatenate(
                [
                    expand_grad_ref[:, turn * half : (turn + 1) * half],
                    reduce_grad_ref[:, turn * half : (turn + 1) * half],
                    qkv_grad_ref[:, turn * 3 * local : (turn + 1) * 3 * local],
                    out_grad_ref[:, turn * local : (turn + 1) * local],
                    small_ref[...],
                    jnp.zeros((side, bundle_ref.shape[2] - 2 * half - 4 * local - 8), F32),
                ],
                axis=1,
            )
        place = lax.axis_index("dp")
        me = (place % 2, (place // 2) % 2, lax.axis_index("side"))
        fourth = side // 4
        width = tap_grad_ref.shape[1]
        for core in range(2):
            for x in range(2):
                part = 2 * (me[0] ^ core) + (me[1] ^ x)
                lines = pl.ds(pl.multiple_of(part * fourth, 8), fourth)
                for turn in range(2):
                    first = (me[2] ^ turn) * (width // 2)
                    pieces = [
                        tap_grad_ref[lines, pl.ds(pl.multiple_of(first + j * 128, 128), 128)]
                        for j in range(width // 256)
                    ] + [
                        bundle_ref[turn, lines, j * 128 : (j + 1) * 128]
                        for j in range(bundle_ref.shape[2] // 128)
                    ]
                    block = jnp.concatenate(pieces, axis=0).astype(BF16)
                    (send_ref if core else keep_ref)[2 * x + turn] = block


def side_block(index, segment, tap, stream, up, top, table, before, middle, own, other):
    side, tokens = stream.shape
    width = top.shape[1]
    heads = side // SIDE_HEAD
    hidden = own.shape[0] - 2 * side
    bundle = -(-(hidden + 2 * side + 8) // 128) * 128
    block = (side // 4) * (width // 256 + bundle // 128)

    def lanes(height):
        return pl.BlockSpec((height, SEQ), lambda i: (0, i))

    packed = pl.BlockSpec((4, block, 128), lambda i: (0, 0, 0))
    return pl.pallas_call(
        side_kernel,
        grid=(tokens // SEQ,),
        in_specs=[
            pl.BlockSpec(memory_space=pltpu.SMEM),
            whole(segment),
            lanes(side),
            lanes(side),
            lanes(side),
            pl.BlockSpec(memory_space=pl.ANY),
            *map(whole, (table, before, middle, own, other)),
        ],
        out_specs=[lanes(side), lanes(side), packed, packed],
        out_shape=[
            jax.ShapeDtypeStruct((side, tokens), BF16),
            jax.ShapeDtypeStruct((side, tokens), BF16),
            jax.ShapeDtypeStruct((4, block, 128), BF16),
            jax.ShapeDtypeStruct((4, block, 128), BF16),
        ],
        scratch_shapes=[
            pltpu.VMEM((side, width), F32),
            pltpu.VMEM((side, 3 * side), F32),
            pltpu.VMEM((side, side), F32),
            pltpu.VMEM((side, hidden), F32),
            pltpu.VMEM((side, hidden), F32),
            pltpu.VMEM((side, 8), F32),
            pltpu.VMEM((2, side, bundle), F32),
            pltpu.VMEM((SEQ, SEQ), BF16),
            pltpu.VMEM((3 * side, side), BF16),
            pltpu.VMEM((side, hidden), BF16),
            pltpu.VMEM((side, side), BF16),
            pltpu.VMEM((hidden, side), BF16),
            pltpu.VMEM((heads, SEQ, SEQ), BF16),
            pltpu.VMEM((3 * side, SEQ), F32),
            pltpu.VMEM((heads, 16, SEQ), BF16),
            pltpu.VMEM((heads, 16, SEQ), BF16),
            pltpu.VMEM((heads, ROWS, SEQ), BF16),
            pltpu.VMEM((heads, ROWS, SEQ), F32),
            pltpu.VMEM((side, SEQ), F32),
            pltpu.VMEM((side, SEQ), F32),
            pltpu.VMEM((3 * side, SEQ), F32),
            pltpu.VMEM((8, TILE), F32),
            pltpu.VMEM((SEQ, width), BF16),
            pltpu.SemaphoreType.DMA,
        ],
        compiler_params=pltpu.CompilerParams(vmem_limit_bytes=60 << 20),
        name="side_block",
    )(index, segment, tap, stream, up, top, table, before, middle, own, other)


def unpack_kernel(
    index_ref,
    near_ref,
    far_ref,
    tap_ref,
    gate_ref,
    before_ref,
    middle_ref,
    q_ref,
    k_ref,
    v_ref,
    output_ref,
    expand_ref,
    reduce_ref,
    bundle_ref,
):
    side, width = tap_ref.shape
    half = expand_ref.shape[1]
    local = side // 2
    fourth = side // 4
    taps = width // 256
    tiles = bundle_ref.shape[1] // 128
    block = fourth * (taps + tiles)
    place = lax.axis_index("dp")
    me = (place % 2, (place // 2) % 2, lax.axis_index("side"))
    for core in range(2):
        held = (far_ref if core else near_ref)[...].astype(F32)
        for x in range(2):
            part = 2 * (me[0] ^ core) + (me[1] ^ x)
            lines = pl.ds(pl.multiple_of(part * fourth, 8), fourth)
            for turn in range(2):
                at = 2 * block + x * taps * fourth if turn else x * block
                first = (me[2] ^ turn) * (width // 2)
                for j in range(taps):
                    cols = pl.ds(pl.multiple_of(first + j * 128, 128), 128)
                    tap_ref[lines, cols] = held[at + j * fourth : at + (j + 1) * fourth]
            for j in range(tiles):
                at = x * block + (taps + j) * fourth
                bundle_ref[lines, j * 128 : (j + 1) * 128] = held[at : at + fourth]
    expand_ref[...] = bundle_ref[:, 0:half]
    reduce_ref[...] = jnp.transpose(bundle_ref[:, half : 2 * half])
    rest = jnp.transpose(bundle_ref[:, 2 * half : 2 * half + 4 * local + 8])
    q_ref[...] = rest[0:local]
    k_ref[...] = rest[local : 2 * local]
    v_ref[...] = rest[2 * local : 3 * local]
    output_ref[...] = rest[3 * local : 4 * local]
    small = rest[4 * local : 4 * local + 8]
    picked = lax.broadcasted_iota(jnp.int32, gate_ref.shape, 0) == index_ref[0]
    gate_ref[...] = jnp.where(picked, small[0:1], 0.0)
    before_ref[...] = small[1:2]
    middle_ref[...] = small[2:3]


def exchange(values, dp, side, dp_size):
    pairs = [
        (2 * i + s, 2 * (i ^ dp) + (s ^ side)) for i in range(dp_size) for s in range(2)
    ]
    return lax.ppermute(values, ("dp", "side"), pairs)


def add(*values):
    return functools.reduce(lambda a, b: a + b, [v.astype(F32) for v in values]).astype(BF16)


def shards(
    dp_size,
    backbone_in,
    segment_ids,
    gate_index,
    norm_before,
    norm_middle,
    frozen_query,
    frozen_key,
    frozen_value,
    frozen_output,
    frozen_expand,
    frozen_reduce,
    tap_weight,
    gate_table,
    side_stream,
    ladder_before,
    ladder_middle,
    ladder_query,
    ladder_key,
    ladder_value,
    ladder_output,
    ladder_expand,
    ladder_reduce,
    cotangent,
):
    side = side_stream.shape[1]
    width = tap_weight.shape[0]
    local = side // 2
    half = ladder_expand.shape[1]
    swap = functools.partial(exchange, dp_size=dp_size)
    own = pl.pallas_call(
        pack_kernel,
        out_shape=jax.ShapeDtypeStruct((2 * half + 4 * local, side), BF16),
        name="pack_weights",
    )(ladder_expand, ladder_query.T, ladder_key.T, ladder_value.T, ladder_output, ladder_reduce)
    other = swap(own, 0, 1)
    segment = segment_ids.reshape(-1, 1, SEQ)
    top, tap = frozen_block(
        segment,
        backbone_in,
        norm_before,
        norm_middle,
        frozen_query,
        frozen_key,
        frozen_value,
        frozen_output,
        frozen_expand,
        frozen_reduce,
        tap_weight.T,
    )
    result, stream_grad, keep, send = side_block(
        gate_index,
        segment,
        tap,
        side_stream.T,
        cotangent.T,
        top,
        gate_table,
        ladder_before[None],
        ladder_middle[None],
        own,
        other,
    )
    block = keep.shape[1]
    taps = (side // 4) * (width // 256)
    quad = add(keep, swap(send, 1, 0))
    mine = add(quad[0], swap(quad[1], 0, 1), swap(quad[2], 2, 0), swap(quad[3], 2, 1))
    bit = 4
    while bit < dp_size:
        steps = [bit, 2 * bit, 3 * bit] if 2 * bit < dp_size else [bit]
        mine = add(mine, *[swap(mine, step, 0) for step in steps])
        bit *= len(steps) + 1
    near = jnp.concatenate(
        [mine, swap(mine, 2, 0), swap(mine[:taps], 0, 1), swap(mine[:taps], 2, 1)], axis=0
    )
    far = swap(near, 1, 0)
    shape = functools.partial(jax.ShapeDtypeStruct, dtype=F32)
    tap_sum, gate_sum, before_sum, middle_sum, q_sum, k_sum, v_sum, out_sum, expand_sum, reduce_sum = pl.pallas_call(
        unpack_kernel,
        in_specs=[
            pl.BlockSpec(memory_space=pltpu.SMEM),
            pl.BlockSpec(memory_space=pltpu.VMEM),
            pl.BlockSpec(memory_space=pltpu.VMEM),
        ],
        out_shape=[
            shape((side, width)),
            shape(gate_table.shape),
            shape((1, side)),
            shape((1, side)),
            shape((local, side)),
            shape((local, side)),
            shape((local, side)),
            shape((local, side)),
            shape((side, half)),
            shape((half, side)),
        ],
        scratch_shapes=[pltpu.VMEM((side, (block - taps) // (side // 4) * 128), F32)],
        compiler_params=pltpu.CompilerParams(vmem_limit_bytes=8 << 20),
        name="unpack_gradients",
    )(gate_index, near, far)
    return (
        result.T,
        stream_grad.T,
        tap_sum.T,
        gate_sum,
        before_sum[0],
        middle_sum[0],
        q_sum.T,
        k_sum.T,
        v_sum.T,
        out_sum,
        expand_sum,
        reduce_sum,
    )


def solution(mesh):
    rows = P(("dp", "side"), None)
    placed = (
        rows,
        P("dp"),
        *([P()] * 11),
        rows,
        P(),
        P(),
        P(None, "side"),
        P(None, "side"),
        P(None, "side"),
        P("side", None),
        P(None, "side"),
        P("side", None),
        rows,
    )
    return jax.shard_map(
        functools.partial(shards, mesh.shape["dp"]),
        mesh=mesh,
        in_specs=placed,
        out_specs=(
            rows,
            rows,
            P(),
            P(),
            P(),
            P(),
            P(None, "side"),
            P(None, "side"),
            P(None, "side"),
            P("side", None),
            P(None, "side"),
            P("side", None),
        ),
        check_vma=False,
    )
```

```python
import functools

import jax
import jax.numpy as jnp
from jax import lax
from jax.experimental import pallas as pl
from jax.experimental.pallas import tpu as pltpu
from jax.sharding import PartitionSpec as P

HEAD = 64
SIDE_HEAD = 8
SEQ = 1024
EPS = 1e-06
MASKED = -1e30
LOG2E = 1.4426950408889634
LEAST = 2.0**-64
MOST = 2.0**64
TILE = 1024
ROWS = 96
GROUP = 4
PAIRS = 3

F32 = jnp.float32
BF16 = jnp.bfloat16
NN = (((1,), (0,)), ((), ()))
NT = (((1,), (1,)), ((), ()))
TN = (((0,), (0,)), ((), ()))


def dot(left, right, dims=NN):
    return lax.dot_general(left, right, dims, preferred_element_type=F32)


def gelu_inner(values):
    return 0.7978845608028654 * values * (1.0 + 0.044715 * values * values)


def gelu(values):
    return 0.5 * values * (1.0 + jnp.tanh(gelu_inner(values)))


def gelu_both(values):
    square = values * values
    bend = jnp.tanh(0.7978845608028654 * values * (1.0 + 0.044715 * square))
    half = 0.5 * (1.0 + bend)
    slope = 0.7978845608028654 * (1.0 + 3.0 * 0.044715 * square)
    return values * half, half + 0.5 * values * (1.0 - bend * bend) * slope


def fill_mask(row, mask_ref):
    row = row.astype(F32)
    column = jnp.transpose(jnp.broadcast_to(row, (8, SEQ)))[:, 0:1]
    for step in range(SEQ // 128):
        lanes = slice(step * 128, (step + 1) * 128)
        mask_ref[:, lanes] = jnp.where(column == row[:, lanes], 1.0, 0.0).astype(BF16)


def note_totals(fine_ref, totals):
    fine = jnp.logical_and(totals >= LEAST, totals <= MOST)
    fine_ref[...] = jnp.where(fine, fine_ref[...], 0.0)


def weights_of(scores, mask, careful):
    if not careful:
        return jnp.exp2(scores).astype(BF16) * mask
    allowed = mask.astype(F32) > 0.5
    scores = jnp.where(allowed, scores, MASKED)
    highest = jnp.max(scores, axis=0, keepdims=True)
    return jnp.exp2(scores - highest).astype(BF16)


def frozen_kernel(
    segment_ref,
    x_ref,
    before_ref,
    middle_ref,
    tap_t_ref,
    wq_ref,
    wk_ref,
    wv_ref,
    wo_hbm,
    we_hbm,
    wr_hbm,
    top_ref,
    tap_ref,
    wo_ref,
    we_ref,
    wr_ref,
    copied,
    mask_ref,
    normed_ref,
    q_ref,
    k_ref,
    v_ref,
    ctx_ref,
    fine_ref,
):
    width = x_ref.shape[1]
    heads = width // HEAD
    padded = v_ref.shape[1]

    starting = pl.program_id(0) == 0
    copies = [
        pltpu.make_async_copy(source, target, copied.at[i])
        for i, (source, target) in enumerate(
            (
                (wo_hbm, wo_ref),
                (we_hbm, we_ref),
                (wr_hbm, wr_ref),
            )
        )
    ]

    @pl.when(starting)
    def _():
        for copy in copies:
            copy.start()
        v_ref[:, HEAD:padded] = jnp.ones((heads, padded - HEAD, SEQ), BF16)

    for part in range(2):
        rows = slice(part * SEQ // 2, (part + 1) * SEQ // 2)
        base = x_ref[rows].astype(F32)
        factor = lax.rsqrt(jnp.mean(base * base, axis=-1, keepdims=True) + EPS)
        normed = (base * factor * before_ref[...][None]).astype(BF16)
        normed_ref[rows] = normed
        q_ref[rows] = (dot(normed, wq_ref[...]) * (HEAD**-0.5 * LOG2E)).astype(BF16)
        k_ref[rows] = dot(normed, wk_ref[...]).astype(BF16)
    here = lax.axis_index("side") * pl.num_programs(0) + pl.program_id(0)
    fill_mask(segment_ref[here], mask_ref)
    v = dot(wv_ref[...], normed_ref[...], (((0,), (1,)), ((), ()))).astype(BF16)
    for head in range(heads):
        v_ref[head, 0:HEAD] = v[head * HEAD : (head + 1) * HEAD]

    def attend(careful, tile, together):
        def one(pair, turn, start):
            lanes = pl.ds(start, tile)
            both = pl.ds(pl.multiple_of(pair * 2 * HEAD, 2 * HEAD), 2 * HEAD)
            cols = slice(turn * HEAD, (turn + 1) * HEAD)
            scores = dot(k_ref[:, both][:, cols], q_ref[lanes, both][:, cols], NT)
            probs = weights_of(scores, mask_ref[:, lanes], careful)
            mixed = dot(v_ref[2 * pair + turn], probs)
            if not careful:
                note_totals(fine_ref, mixed[HEAD : HEAD + 8])
            rows = pl.ds(pl.multiple_of((2 * pair + turn) * HEAD, HEAD), HEAD)
            ctx_ref[rows, lanes] = (mixed[0:HEAD] / mixed[HEAD : HEAD + 1]).astype(BF16)

        def step(group, carry):
            for pair in range(together):
                for turn in range(2):
                    for i in range(SEQ // tile):
                        one(group * together + pair, turn, i * tile)
            return carry

        lax.fori_loop(0, heads // 2 // together, step, 0)

    fine_ref[...] = jnp.ones_like(fine_ref)
    attend(False, TILE, PAIRS)
    pl.when(jnp.min(fine_ref[...]) < 0.5)(lambda: attend(True, TILE, 1))

    @pl.when(starting)
    def _():
        for copy in copies:
            copy.wait()

    chunk = 1024
    hidden = we_ref.shape[1]
    piece = 768

    def feed_forward(part, carry):
        rows = pl.ds(pl.multiple_of(part * chunk, chunk), chunk)
        middle = x_ref[rows].astype(F32) + dot(ctx_ref[:, rows], wo_ref[...], TN)
        scale = lax.rsqrt(jnp.mean(middle * middle, axis=-1, keepdims=True) + EPS)
        normed = (middle * scale * middle_ref[...][None]).astype(BF16)
        total = middle
        for j in range(hidden // piece):
            cols = slice(j * piece, (j + 1) * piece)
            expanded = gelu(dot(normed, we_ref[:, cols])).astype(BF16)
            total = total + dot(expanded, wr_ref[cols])
        top = total.astype(BF16)
        top_ref[rows] = top
        tap_ref[:, rows] = dot(tap_t_ref[...], top, NT).astype(BF16)
        return carry

    lax.fori_loop(0, SEQ // chunk, feed_forward, 0)


def whole(array):
    shape = array.shape
    return pl.BlockSpec(shape, lambda i: (0,) * len(shape), pipeline_mode=pl.Buffered(1))


def frozen_block(segment, x, before, middle, wq, wk, wv, wo, we, wr, tap_t):
    tokens, width = x.shape
    heads = width // HEAD
    side = tap_t.shape[0]
    return pl.pallas_call(
        frozen_kernel,
        grid=(tokens // SEQ,),
        in_specs=[
            whole(segment),
            pl.BlockSpec((SEQ, width), lambda i: (i, 0)),
            *map(whole, (before, middle, tap_t, wq, wk, wv)),
            *[pl.BlockSpec(memory_space=pl.ANY)] * 3,
        ],
        out_specs=[
            pl.BlockSpec((SEQ, width), lambda i: (i, 0)),
            pl.BlockSpec((side, SEQ), lambda i: (0, i)),
        ],
        out_shape=[
            jax.ShapeDtypeStruct((tokens, width), BF16),
            jax.ShapeDtypeStruct((side, tokens), BF16),
        ],
        scratch_shapes=[
            *[pltpu.VMEM(w.shape, BF16) for w in (wo, we, wr)],
            pltpu.SemaphoreType.DMA((3,)),
            pltpu.VMEM((SEQ, SEQ), BF16),
            pltpu.VMEM((SEQ, width), BF16),
            pltpu.VMEM((SEQ, width), BF16),
            pltpu.VMEM((SEQ, width), BF16),
            pltpu.VMEM((heads, HEAD + 16, SEQ), BF16),
            pltpu.VMEM((width, SEQ), BF16),
            pltpu.VMEM((8, TILE), F32),
        ],
        compiler_params=pltpu.CompilerParams(vmem_limit_bytes=60 << 20),
        name="frozen_block",
    )(segment, x, before, middle, tap_t, wq, wk, wv, wo, we, wr)


def outer_rows(left, right):
    return [left[e : e + 1] * right for e in range(SIDE_HEAD)]


def pack_kernel(expand_ref, q_ref, k_ref, v_ref, output_ref, reduce_ref, packed_ref):
    side, half = expand_ref.shape
    packed_ref[0:side] = expand_ref[:, 0:side]
    packed_ref[side : 2 * side] = expand_ref[:, side:half]
    at = half
    for ref in (q_ref, k_ref, v_ref, output_ref, reduce_ref):
        packed_ref[at : at + ref.shape[0]] = ref[...]
        at += ref.shape[0]


def side_kernel(
    index_ref,
    segment_ref,
    tap_ref,
    stream_ref,
    up_ref,
    top_hbm,
    table_ref,
    before_ref,
    middle_ref,
    own_ref,
    other_ref,
    out_ref,
    stream_grad_ref,
    keep_ref,
    send_ref,
    tap_grad_ref,
    qkv_grad_ref,
    out_grad_ref,
    expand_grad_ref,
    reduce_grad_ref,
    small_ref,
    bundle_ref,
    mask_ref,
    w_ref,
    we_ref,
    wo_ref,
    wr_ref,
    e_ref,
    qkv_ref,
    q16_ref,
    k16_ref,
    rows_ref,
    moment_ref,
    ctx_ref,
    dctx_ref,
    dqkv_ref,
    fine_ref,
    top_ref,
    copied,
):
    side = tap_ref.shape[0]
    heads = side // SIDE_HEAD
    local = side // 2
    hidden = we_ref.shape[1]
    half = hidden // 2

    @pl.when(pl.program_id(0) == 0)
    def _():
        for turn, ref in ((0, own_ref), (1, other_ref)):
            we_ref[:, turn * half : turn * half + side] = ref[0:side]
            we_ref[:, turn * half + side : (turn + 1) * half] = ref[side:half]
            at = half
            w_ref[turn * 3 * local : (turn + 1) * 3 * local] = ref[at : at + 3 * local]
            at += 3 * local
            wo_ref[turn * local : (turn + 1) * local] = ref[at : at + local]
            at += local
            wr_ref[turn * half : (turn + 1) * half] = ref[at : at + half]
        tap_grad_ref[...] = jnp.zeros_like(tap_grad_ref)
        qkv_grad_ref[...] = jnp.zeros_like(qkv_grad_ref)
        out_grad_ref[...] = jnp.zeros_like(out_grad_ref)
        expand_grad_ref[...] = jnp.zeros_like(expand_grad_ref)
        reduce_grad_ref[...] = jnp.zeros_like(reduce_grad_ref)
        small_ref[...] = jnp.zeros_like(small_ref)

    logits = table_ref[pl.ds(index_ref[0], 1), :]
    stacked = jnp.concatenate(
        [
            jnp.broadcast_to(jax.nn.sigmoid(logits), (8, side)),
            jnp.broadcast_to(before_ref[...], (8, side)),
            jnp.broadcast_to(middle_ref[...], (8, side)),
        ],
        axis=0,
    )
    columns = jnp.transpose(stacked)
    gate, before, middle = columns[:, 0:1], columns[:, 8:9], columns[:, 16:17]

    def head_rows(kind, head):
        start = (head // (heads // 2)) * 3 * local + kind * local + (head % (heads // 2)) * SIDE_HEAD
        return pl.ds(pl.multiple_of(start, SIDE_HEAD), SIDE_HEAD)

    tap = tap_ref[...].astype(F32)
    stream = stream_ref[...].astype(F32)
    mixed = gate * tap + (1.0 - gate) * stream
    factor1 = lax.rsqrt(jnp.mean(mixed * mixed, axis=0, keepdims=True) + EPS)
    n1 = (mixed * factor1 * before).astype(BF16)
    qkv_ref[...] = dot(w_ref[...], n1)

    here = lax.axis_index("side") * pl.num_programs(0) + pl.program_id(0)
    fill_mask(segment_ref[here], mask_ref)

    zeros8 = jnp.zeros((SIDE_HEAD, SEQ), F32)
    ones8 = jnp.ones((SIDE_HEAD, SEQ), F32)

    def prepare(head):
        q = qkv_ref[head_rows(0, head)] * (SIDE_HEAD**-0.5 * LOG2E)
        q = q.astype(BF16).astype(F32)
        k = qkv_ref[head_rows(1, head)].astype(BF16).astype(F32)
        v = qkv_ref[head_rows(2, head)].astype(BF16).astype(F32)
        qkv_ref[head_rows(0, head)] = q
        qkv_ref[head_rows(1, head)] = k
        qkv_ref[head_rows(2, head)] = v
        q16_ref[head] = jnp.concatenate([q, zeros8], axis=0).astype(BF16)
        k16_ref[head] = jnp.concatenate([k, zeros8], axis=0).astype(BF16)
        rows = [v, ones8, k, zeros8] + outer_rows(v, k)
        rows_ref[head] = jnp.concatenate(rows, axis=0).astype(BF16)

    def prepare_group(group, carry):
        for turn in range(GROUP):
            prepare(group * GROUP + turn)
        return carry

    lax.fori_loop(0, heads // GROUP, prepare_group, 0)

    def attend(careful, tile):
        def one(head, start):
            at = pl.multiple_of(head * SIDE_HEAD, SIDE_HEAD)
            lanes = pl.ds(start, tile)
            scores = dot(k16_ref[head], q16_ref[head, :, lanes], TN)
            probs = weights_of(scores, mask_ref[:, lanes], careful)
            e_ref[head, lanes, :] = jnp.transpose(probs)
            found = dot(rows_ref[head], probs)
            if not careful:
                note_totals(fine_ref, found[8:16])
            inverse = 1.0 / found[8:16]
            ctx_ref[pl.ds(at, SIDE_HEAD), lanes] = found[0:8] * inverse
            moment_ref[head, 8:16, lanes] = inverse
            moment_ref[head, 16:24, lanes] = found[16:24] * inverse
            for e in range(SIDE_HEAD):
                low = 32 + e * SIDE_HEAD
                moment_ref[head, low : low + 8, lanes] = found[low : low + 8] * inverse

        together = 1 if careful else GROUP

        def step(group, carry):
            for turn in range(together):
                for i in range(SEQ // tile):
                    one(group * together + turn, i * tile)
            return carry

        lax.fori_loop(0, heads // together, step, 0)

    lines = pl.ds(pl.multiple_of(pl.program_id(0) * SEQ, SEQ), SEQ)
    top_copy = pltpu.make_async_copy(top_hbm.at[lines], top_ref, copied)
    top_copy.start()
    fine_ref[...] = jnp.ones_like(fine_ref)
    attend(False, TILE)
    pl.when(jnp.min(fine_ref[...]) < 0.5)(lambda: attend(True, TILE))

    ctx = ctx_ref[...].astype(BF16)
    res1 = mixed + dot(wo_ref[...], ctx, TN)
    factor2 = lax.rsqrt(jnp.mean(res1 * res1, axis=0, keepdims=True) + EPS)
    z = res1 * factor2
    n2 = (z * middle).astype(BF16)
    pre = dot(we_ref[...], n2, TN)
    act, slope = gelu_both(pre)
    act = act.astype(BF16)
    result = res1 + dot(wr_ref[...], act, TN)
    out_ref[...] = result.astype(BF16)

    low_up = up_ref[...]
    up = low_up.astype(F32)
    reduce_grad_ref[...] += dot(low_up, act, NT)
    dpre = (dot(wr_ref[...], low_up) * slope).astype(BF16)
    expand_grad_ref[...] += dot(n2, dpre, NT)
    dn2 = dot(we_ref[...], dpre)
    middle_grad = jnp.sum(dn2 * z, axis=1, keepdims=True)
    u = dn2 * middle
    spread = jnp.mean(u * res1, axis=0, keepdims=True)
    dres1 = up + factor2 * u - z * (factor2 * factor2 * spread)
    low_dres = dres1.astype(BF16)
    out_grad_ref[...] += dot(low_dres, ctx, NT)
    dctx_ref[...] = dot(wo_ref[...], low_dres).astype(BF16).astype(F32)

    def prepare_back(head):
        at = pl.multiple_of(head * SIDE_HEAD, SIDE_HEAD)
        q = qkv_ref[head_rows(0, head)]
        dctx = dctx_ref[pl.ds(at, SIDE_HEAD)]
        inverse = moment_ref[head, 8:16]
        inner = jnp.sum(dctx * ctx_ref[pl.ds(at, SIDE_HEAD)], axis=0, keepdims=True)
        dq = -inner * moment_ref[head, 16:24]
        for e in range(SIDE_HEAD):
            low = 32 + e * SIDE_HEAD
            dq = dq + dctx[e : e + 1] * moment_ref[head, low : low + 8]
        dqkv_ref[head_rows(0, head)] = dq * SIDE_HEAD**-0.5
        scaled = dctx * inverse
        rows = [scaled, zeros8, (inner * inverse) * q, zeros8] + outer_rows(scaled, q)
        rows_ref[head] = jnp.concatenate(rows, axis=0).astype(BF16)

    def prepare_back_group(group, carry):
        for turn in range(GROUP):
            prepare_back(group * GROUP + turn)
        return carry

    lax.fori_loop(0, heads // GROUP, prepare_back_group, 0)

    def back(head):
        found = dot(rows_ref[head], e_ref[head])
        v = qkv_ref[head_rows(2, head)]
        dk = -found[16:24]
        for e in range(SIDE_HEAD):
            low = 32 + e * SIDE_HEAD
            dk = dk + v[e : e + 1] * found[low : low + 8]
        dqkv_ref[head_rows(1, head)] = dk * (1.0 / LOG2E)
        dqkv_ref[head_rows(2, head)] = found[0:8]

    def back_group(group, carry):
        for turn in range(heads // 2):
            back(group * (heads // 2) + turn)
        return carry

    lax.fori_loop(0, 2, back_group, 0)

    top_copy.wait()
    dqkv = dqkv_ref[...].astype(BF16)
    qkv_grad_ref[...] += dot(n1, dqkv, NT)
    dn1 = dot(w_ref[...], dqkv, TN)
    unit = mixed * factor1
    before_grad = jnp.sum(dn1 * unit, axis=1, keepdims=True)
    u = dn1 * before
    spread = jnp.mean(u * mixed, axis=0, keepdims=True)
    dmixed = dres1 + factor1 * u - unit * (factor1 * factor1 * spread)
    logit = jnp.sum(dmixed * (tap - stream), axis=1, keepdims=True) * gate * (1.0 - gate)
    small_ref[...] += jnp.concatenate(
        [logit, before_grad, middle_grad, jnp.zeros((side, 5), F32)], axis=1
    )
    tap_grad_ref[...] += dot((gate * dmixed).astype(BF16), top_ref[...])
    stream_grad_ref[...] = ((1.0 - gate) * dmixed).astype(BF16)

    @pl.when(pl.program_id(0) == pl.num_programs(0) - 1)
    def _():
        for turn in range(2):
            bundle_ref[turn] = jnp.concatenate(
                [
                    expand_grad_ref[:, turn * half : (turn + 1) * half],
                    reduce_grad_ref[:, turn * half : (turn + 1) * half],
                    qkv_grad_ref[:, turn * 3 * local : (turn + 1) * 3 * local],
                    out_grad_ref[:, turn * local : (turn + 1) * local],
                    small_ref[...],
                    jnp.zeros((side, bundle_ref.shape[2] - 2 * half - 4 * local - 8), F32),
                ],
                axis=1,
            )
        place = lax.axis_index("dp")
        me = (place % 2, (place // 2) % 2, lax.axis_index("side"))
        fourth = side // 4
        width = tap_grad_ref.shape[1]
        for core in range(2):
            for x in range(2):
                part = 2 * (me[0] ^ core) + (me[1] ^ x)
                lines = pl.ds(pl.multiple_of(part * fourth, 8), fourth)
                for turn in range(2):
                    first = (me[2] ^ turn) * (width // 2)
                    pieces = [
                        tap_grad_ref[lines, pl.ds(pl.multiple_of(first + j * 128, 128), 128)]
                        for j in range(width // 256)
                    ] + [
                        bundle_ref[turn, lines, j * 128 : (j + 1) * 128]
                        for j in range(bundle_ref.shape[2] // 128)
                    ]
                    block = jnp.concatenate(pieces, axis=0).astype(BF16)
                    (send_ref if core else keep_ref)[2 * x + turn] = block


def side_block(index, segment, tap, stream, up, top, table, before, middle, own, other):
    side, tokens = stream.shape
    width = top.shape[1]
    heads = side // SIDE_HEAD
    hidden = own.shape[0] - 2 * side
    bundle = -(-(hidden + 2 * side + 8) // 128) * 128
    block = (side // 4) * (width // 256 + bundle // 128)

    def lanes(height):
        return pl.BlockSpec((height, SEQ), lambda i: (0, i))

    packed = pl.BlockSpec((4, block, 128), lambda i: (0, 0, 0))
    return pl.pallas_call(
        side_kernel,
        grid=(tokens // SEQ,),
        in_specs=[
            pl.BlockSpec(memory_space=pltpu.SMEM),
            whole(segment),
            lanes(side),
            lanes(side),
            lanes(side),
            pl.BlockSpec(memory_space=pl.ANY),
            *map(whole, (table, before, middle, own, other)),
        ],
        out_specs=[lanes(side), lanes(side), packed, packed],
        out_shape=[
            jax.ShapeDtypeStruct((side, tokens), BF16),
            jax.ShapeDtypeStruct((side, tokens), BF16),
            jax.ShapeDtypeStruct((4, block, 128), BF16),
            jax.ShapeDtypeStruct((4, block, 128), BF16),
        ],
        scratch_shapes=[
            pltpu.VMEM((side, width), F32),
            pltpu.VMEM((side, 3 * side), F32),
            pltpu.VMEM((side, side), F32),
            pltpu.VMEM((side, hidden), F32),
            pltpu.VMEM((side, hidden), F32),
            pltpu.VMEM((side, 8), F32),
            pltpu.VMEM((2, side, bundle), F32),
            pltpu.VMEM((SEQ, SEQ), BF16),
            pltpu.VMEM((3 * side, side), BF16),
            pltpu.VMEM((side, hidden), BF16),
            pltpu.VMEM((side, side), BF16),
            pltpu.VMEM((hidden, side), BF16),
            pltpu.VMEM((heads, SEQ, SEQ), BF16),
            pltpu.VMEM((3 * side, SEQ), F32),
            pltpu.VMEM((heads, 16, SEQ), BF16),
            pltpu.VMEM((heads, 16, SEQ), BF16),
            pltpu.VMEM((heads, ROWS, SEQ), BF16),
            pltpu.VMEM((heads, ROWS, SEQ), F32),
            pltpu.VMEM((side, SEQ), F32),
            pltpu.VMEM((side, SEQ), F32),
            pltpu.VMEM((3 * side, SEQ), F32),
            pltpu.VMEM((8, TILE), F32),
            pltpu.VMEM((SEQ, width), BF16),
            pltpu.SemaphoreType.DMA,
        ],
        compiler_params=pltpu.CompilerParams(vmem_limit_bytes=60 << 20),
        name="side_block",
    )(index, segment, tap, stream, up, top, table, before, middle, own, other)


def unpack_kernel(
    index_ref,
    near_ref,
    far_ref,
    tap_ref,
    gate_ref,
    before_ref,
    middle_ref,
    q_ref,
    k_ref,
    v_ref,
    output_ref,
    expand_ref,
    reduce_ref,
    bundle_ref,
):
    side, width = tap_ref.shape
    half = expand_ref.shape[1]
    local = side // 2
    fourth = side // 4
    taps = width // 256
    tiles = bundle_ref.shape[1] // 128
    block = fourth * (taps + tiles)
    place = lax.axis_index("dp")
    me = (place % 2, (place // 2) % 2, lax.axis_index("side"))
    for core in range(2):
        held = (far_ref if core else near_ref)[...].astype(F32)
        for x in range(2):
            part = 2 * (me[0] ^ core) + (me[1] ^ x)
            lines = pl.ds(pl.multiple_of(part * fourth, 8), fourth)
            for turn in range(2):
                at = 2 * block + x * taps * fourth if turn else x * block
                first = (me[2] ^ turn) * (width // 2)
                for j in range(taps):
                    cols = pl.ds(pl.multiple_of(first + j * 128, 128), 128)
                    tap_ref[lines, cols] = held[at + j * fourth : at + (j + 1) * fourth]
            for j in range(tiles):
                at = x * block + (taps + j) * fourth
                bundle_ref[lines, j * 128 : (j + 1) * 128] = held[at : at + fourth]
    expand_ref[...] = bundle_ref[:, 0:half]
    reduce_ref[...] = jnp.transpose(bundle_ref[:, half : 2 * half])
    rest = jnp.transpose(bundle_ref[:, 2 * half : 2 * half + 4 * local + 8])
    q_ref[...] = rest[0:local]
    k_ref[...] = rest[local : 2 * local]
    v_ref[...] = rest[2 * local : 3 * local]
    output_ref[...] = rest[3 * local : 4 * local]
    small = rest[4 * local : 4 * local + 8]
    picked = lax.broadcasted_iota(jnp.int32, gate_ref.shape, 0) == index_ref[0]
    gate_ref[...] = jnp.where(picked, small[0:1], 0.0)
    before_ref[...] = small[1:2]
    middle_ref[...] = small[2:3]


def exchange(values, dp, side, dp_size):
    pairs = [
        (2 * i + s, 2 * (i ^ dp) + (s ^ side)) for i in range(dp_size) for s in range(2)
    ]
    return lax.ppermute(values, ("dp", "side"), pairs)


def add(*values):
    return functools.reduce(lambda a, b: a + b, [v.astype(F32) for v in values]).astype(BF16)


def shards(
    dp_size,
    backbone_in,
    segment_ids,
    gate_index,
    norm_before,
    norm_middle,
    frozen_query,
    frozen_key,
    frozen_value,
    frozen_output,
    frozen_expand,
    frozen_reduce,
    tap_weight,
    gate_table,
    side_stream,
    ladder_before,
    ladder_middle,
    ladder_query,
    ladder_key,
    ladder_value,
    ladder_output,
    ladder_expand,
    ladder_reduce,
    cotangent,
):
    side = side_stream.shape[1]
    width = tap_weight.shape[0]
    local = side // 2
    half = ladder_expand.shape[1]
    swap = functools.partial(exchange, dp_size=dp_size)
    own = pl.pallas_call(
        pack_kernel,
        out_shape=jax.ShapeDtypeStruct((2 * half + 4 * local, side), BF16),
        name="pack_weights",
    )(ladder_expand, ladder_query.T, ladder_key.T, ladder_value.T, ladder_output, ladder_reduce)
    other = swap(own, 0, 1)
    segment = segment_ids.reshape(-1, 1, SEQ)
    top, tap = frozen_block(
        segment,
        backbone_in,
        norm_before,
        norm_middle,
        frozen_query,
        frozen_key,
        frozen_value,
        frozen_output,
        frozen_expand,
        frozen_reduce,
        tap_weight.T,
    )
    result, stream_grad, keep, send = side_block(
        gate_index,
        segment,
        tap,
        side_stream.T,
        cotangent.T,
        top,
        gate_table,
        ladder_before[None],
        ladder_middle[None],
        own,
        other,
    )
    block = keep.shape[1]
    taps = (side // 4) * (width // 256)
    quad = add(keep, swap(send, 1, 0))
    mine = add(quad[0], swap(quad[1], 0, 1), swap(quad[2], 2, 0), swap(quad[3], 2, 1))
    bit = 4
    while bit < dp_size:
        steps = [bit, 2 * bit, 3 * bit] if 2 * bit < dp_size else [bit]
        mine = add(mine, *[swap(mine, step, 0) for step in steps])
        bit *= len(steps) + 1
    near = jnp.concatenate(
        [mine, swap(mine, 2, 0), swap(mine[:taps], 0, 1), swap(mine[:taps], 2, 1)], axis=0
    )
    far = swap(near, 1, 0)
    shape = functools.partial(jax.ShapeDtypeStruct, dtype=F32)
    tap_sum, gate_sum, before_sum, middle_sum, q_sum, k_sum, v_sum, out_sum, expand_sum, reduce_sum = pl.pallas_call(
        unpack_kernel,
        in_specs=[
            pl.BlockSpec(memory_space=pltpu.SMEM),
            pl.BlockSpec(memory_space=pltpu.VMEM),
            pl.BlockSpec(memory_space=pltpu.VMEM),
        ],
        out_shape=[
            shape((side, width)),
            shape(gate_table.shape),
            shape((1, side)),
            shape((1, side)),
            shape((local, side)),
            shape((local, side)),
            shape((local, side)),
            shape((local, side)),
            shape((side, half)),
            shape((half, side)),
        ],
        scratch_shapes=[pltpu.VMEM((side, (block - taps) // (side // 4) * 128), F32)],
        compiler_params=pltpu.CompilerParams(vmem_limit_bytes=8 << 20),
        name="unpack_gradients",
    )(gate_index, near, far)
    return (
        result.T,
        stream_grad.T,
        tap_sum.T,
        gate_sum,
        before_sum[0],
        middle_sum[0],
        q_sum.T,
        k_sum.T,
        v_sum.T,
        out_sum,
        expand_sum,
        reduce_sum,
    )


def solution(mesh):
    rows = P(("dp", "side"), None)
    placed = (
        rows,
        P("dp"),
        *([P()] * 11),
        rows,
        P(),
        P(),
        P(None, "side"),
        P(None, "side"),
        P(None, "side"),
        P("side", None),
        P(None, "side"),
        P("side", None),
        rows,
    )
    return jax.shard_map(
        functools.partial(shards, mesh.shape["dp"]),
        mesh=mesh,
        in_specs=placed,
        out_specs=(
            rows,
            rows,
            P(),
            P(),
            P(),
            P(),
            P(None, "side"),
            P(None, "side"),
            P(None, "side"),
            P("side", None),
            P(None, "side"),
            P("side", None),
        ),
        check_vma=False,
    )
```
